32 devices in a mesh: dp: 4 (over y, x), seq: 8 (over z, core).
Axes of the slice: x: 2, y: 2, z: 4, core: 2. Of those that a mesh axis runs over, the one named last changes fastest.
Arguments:
- frames_in: bfloat16 [4, 1024, 1536], P('dp', 'seq'), may hold values from -12 to 12
- lengths: int32 [4], P('dp'), may hold values from 512 to 1024
- first_gain: float32 [1536], replicated, may hold values from 0.5 to 1.5
- second_gain: float32 [1536], replicated, may hold values from 0.5 to 1.5
- qkv_weight: bfloat16 [1536, 2304], replicated, may hold values from -0.296875 to 0.296875
- out_weight: bfloat16 [1536, 768], replicated, may hold values from -0.21875 to 0.21875
- conv_kernel: float32 [31, 1536], replicated, may hold values from -1 to 1
- layer_cotangent: bfloat16 [4, 1024, 1536], P('dp', 'seq'), may hold values from -1.5 to 1.5
Outputs:
- layer_out: bfloat16 [4, 1024, 1536], P('dp', 'seq')
- input_grad: bfloat16 [4, 1024, 1536], P('dp', 'seq')
- weight_grads: float32 [1536, 3072], P(('dp', 'seq'))
- gain_grads: float32 [2, 1536], replicated
- conv_grad: float32 [31, 1536], replicated
The draws below stay inside these ranges and needn't reach their ends.
All inputs are finite; a program needn't handle non-finite values.
Results may differ from the reference program's by a relative error of at most 0.02.
Values may be sent and summed in bfloat16 or wider, within the bound.
No kernel may reach another device: no remote copies, remote signals or barrier semaphores. Data moves between devices by JAX's collectives and lax.ppermute only.
A program may use at most 128 MiB of HBM per device.

```python
import math
import jax
import jax.numpy as jnp
from jax import lax

D = 1536
TAPS = 31
HEADS = 8
HD = 768
FRAMES = 1024
NREC = 4


def draw_frames_in(key, part):
    noise_key = jax.random.fold_in(jax.random.fold_in(key, 11), 0)
    result = jax.random.normal(noise_key, (NREC, FRAMES, D), jnp.float32)
    return jnp.clip(result, -12.0, 12.0).astype(jnp.bfloat16)


def draw_qkv_weight(key, part):
    drawn_key = jax.random.fold_in(key, 23)
    columns = jnp.arange(3 * HD)
    spread = jnp.where(columns < 2 * HD, 1.5, 1.0) / math.sqrt(D)
    result = jax.random.normal(drawn_key, (D, 3 * HD), jnp.float32) * spread[None, :]
    return jnp.clip(result, -0.296875, 0.296875).astype(jnp.bfloat16)


def place_ends(values, key, low, high):
    longest = values.shape.index(max(values.shape))
    spots = []
    for shift in (0, 1):
        where = [jax.random.randint(jax.random.fold_in(key, axis), (), 0, length) for axis, length in enumerate(values.shape)]
        where[longest] = (where[longest] + shift) % values.shape[longest]
        spots.append(tuple(where))
    return values.at[spots[0]].set(low).at[spots[1]].set(high)


def shard_levels(rng, extent, cuts, least, top_value):
    loudness = 1.0
    for position, blocks in cuts:
        draws = jax.random.uniform(jax.random.fold_in(jax.random.fold_in(rng, 6), position), (blocks,), jnp.float32, least / len(cuts), top_value / len(cuts))
        loudness = loudness * jnp.repeat(jnp.exp(draws), extent[position] // blocks).reshape((-1,) + (1,) * (len(extent) - 1 - position))
    return loudness


def bell_draw(stream_key, dims, scale, bound, cuts=(), kind=jnp.bfloat16):
    level = shard_levels(stream_key, dims, cuts, -0.22, 0.18) if cuts else 1.0
    entries = jax.random.normal(stream_key, dims, jnp.float32) * scale * level
    return jnp.minimum(jnp.maximum(entries, -bound), bound).astype(kind)


def setup_inputs(seed: int = 0) -> dict:
    keys = jax.random.split(jax.random.key(seed), 9)
    return {
        "frames_in": draw_frames_in(jax.random.fold_in(keys[8], 71), 0),
        "lengths": place_ends(jax.random.randint(keys[1], (NREC,), FRAMES // 2, FRAMES + 1), jax.random.fold_in(keys[1], 1), FRAMES // 2, FRAMES).astype(jnp.int32),
        "first_gain": jnp.clip(1.0 + 0.1 * jax.random.normal(keys[2], (D,), jnp.float32), 0.5, 1.5),
        "second_gain": jnp.clip(1.0 + 0.1 * jax.random.normal(keys[3], (D,), jnp.float32), 0.5, 1.5),
        "qkv_weight": draw_qkv_weight(jax.random.fold_in(keys[8], 71), 0),
        "out_weight": bell_draw(keys[5], (D, HD), HD ** -0.5, 0.21875),
        "conv_kernel": bell_draw(keys[6], (TAPS, D), TAPS ** -0.5, 1.0, (), jnp.float32),
        "layer_cotangent": bell_draw(keys[7], (NREC, FRAMES, D), 0.25, 1.5, ((0, 4), (1, 8))),
    }


epsilon = 1e-05

def layer_norm(rows, gain_vec):
    row_mean = lax.optimization_barrier(jnp.mean(rows, axis=-1, keepdims=True))
    centered = rows - row_mean
    inv_std = lax.rsqrt(lax.optimization_barrier(jnp.mean(centered * centered, axis=-1, keepdims=True)) + epsilon)
    unit_rows = centered * inv_std
    return (unit_rows * gain_vec, unit_rows, inv_std)

def norm_backward(incoming, unit_rows, inv_std, gain_vec):
    scaled = incoming * gain_vec
    return inv_std * (scaled - lax.optimization_barrier(jnp.mean(scaled, axis=-1, keepdims=True)) - unit_rows * lax.optimization_barrier(jnp.mean(scaled * unit_rows, axis=-1, keepdims=True)))

def contract_rows(left, right):
    return lax.dot_general(left, right, (((1,), (1,)), ((), ())), preferred_element_type=jnp.float32)

def contract_cols(left, right):
    return lax.dot_general(left, right, (((0,), (0,)), ((), ())), preferred_element_type=jnp.float32)

def soft_weights(queries, key_rows, key_valid):
    score_scale = queries.shape[1] ** (-0.5)
    scores = contract_rows(queries, key_rows) * score_scale
    scores = jnp.where(key_valid[None, :], scores, -jnp.inf)
    row_max = lax.optimization_barrier(jnp.max(scores, axis=1, keepdims=True))
    exp_scores = jnp.exp(scores - row_max)
    return exp_scores / lax.optimization_barrier(jnp.sum(exp_scores, axis=1, keepdims=True))

def attend_forward(queries, key_rows, value_rows, key_valid):
    block_rows = min(512, queries.shape[0])
    blocks = queries.reshape(queries.shape[0] // block_rows, block_rows, queries.shape[1])

    def one_block(query_block):
        attn_probs = soft_weights(query_block, key_rows, key_valid).astype(jnp.bfloat16)
        return jnp.dot(attn_probs, value_rows, preferred_element_type=jnp.float32).astype(jnp.bfloat16)
    return lax.map(one_block, blocks).reshape(queries.shape)

def attend_backward(queries, key_rows, value_rows, key_valid, out_grads):
    block_rows = min(512, queries.shape[0])
    block_count = queries.shape[0] // block_rows
    blocks = (queries.reshape(block_count, block_rows, queries.shape[1]), out_grads.reshape(block_count, block_rows, out_grads.shape[1]))
    score_scale = queries.shape[1] ** (-0.5)

    def one_block(running, pieces):
        query_block, grad_block = pieces
        attn_probs = soft_weights(query_block, key_rows, key_valid)
        probs_low = attn_probs.astype(jnp.bfloat16)
        prob_grads = contract_rows(grad_block, value_rows)
        row_delta = lax.optimization_barrier(jnp.sum(attn_probs * prob_grads, axis=1, keepdims=True))
        score_grads = (attn_probs * (prob_grads - row_delta) * score_scale).astype(jnp.bfloat16)
        query_grads = jnp.dot(score_grads, key_rows, preferred_element_type=jnp.float32).astype(jnp.bfloat16)
        key_sum = running[0] + contract_cols(score_grads, query_block)
        value_sum = running[1] + contract_cols(probs_low, grad_block)
        return ((key_sum, value_sum), query_grads)
    zero_rows = jnp.zeros(key_rows.shape, jnp.float32)
    totals, query_grads = lax.scan(one_block, (zero_rows, zero_rows), blocks)
    return (query_grads.reshape(queries.shape), totals[0], totals[1])

def depthwise(padded, kernel, frame_count):
    total = jnp.zeros((frame_count, padded.shape[1]), jnp.float32)
    for tap_index in range(kernel.shape[0]):
        total = total + padded[tap_index:tap_index + frame_count].astype(jnp.float32) * kernel[tap_index]
    return total

def kernel_grad(padded, grads, tap_count):
    frame_count = grads.shape[0]
    grads_wide = grads.astype(jnp.float32)
    sums = [lax.optimization_barrier(jnp.sum(padded[tap_index:tap_index + frame_count].astype(jnp.float32) * grads_wide, axis=0)) for tap_index in range(tap_count)]
    return jnp.stack(sums)

def head_cols(matrix, block_index, head_width, head_size, head_index):
    column_first = block_index * head_width + head_index * head_size
    return matrix[:, column_first:column_first + head_size]

def reference(frames_in, lengths, first_gain, second_gain, qkv_weight, out_weight, conv_kernel, layer_cotangent):
    head_width = out_weight.shape[1]
    head_size = head_width // HEADS
    tap_count = conv_kernel.shape[0]
    half_taps = (tap_count - 1) // 2
    frame_total = frames_in.shape[1]
    model_width = frames_in.shape[2]
    positions = jnp.arange(frame_total, dtype=jnp.int32)
    weight_total = jnp.zeros((model_width, 4 * head_width), jnp.float32)
    gain_total = jnp.zeros((2, model_width), jnp.float32)
    kernel_total = jnp.zeros(conv_kernel.shape, jnp.float32)
    out_list = []
    grad_list = []
    for record in range(NREC):
        inputs = frames_in[record].astype(jnp.float32)
        key_valid = positions < lengths[record]
        live_rows = key_valid.astype(jnp.float32)[:, None]
        normed, unit_one, inv_one = layer_norm(inputs, first_gain)
        normed_low = normed.astype(jnp.bfloat16)
        projected = jnp.dot(normed_low, qkv_weight, preferred_element_type=jnp.float32).astype(jnp.bfloat16)
        head_outs = []
        for head_index in range(HEADS):
            head_outs.append(attend_forward(head_cols(projected, 0, head_width, head_size, head_index), head_cols(projected, 1, head_width, head_size, head_index), head_cols(projected, 2, head_width, head_size, head_index), key_valid))
        attended = jnp.concatenate(head_outs, axis=1)
        resid = inputs + contract_rows(attended, out_weight)
        normed_two, unit_two, inv_two = layer_norm(resid, second_gain)
        conv_in = (live_rows * normed_two).astype(jnp.bfloat16)
        padded = jnp.pad(conv_in, ((half_taps, half_taps), (0, 0)))
        conv_sum = depthwise(padded, conv_kernel, frame_total)
        sigmoid_c = jax.nn.sigmoid(conv_sum)
        out_list.append((live_rows * (resid + conv_sum * sigmoid_c)).astype(jnp.bfloat16))
        outer_grad = live_rows * layer_cotangent[record].astype(jnp.float32)
        conv_grads = (outer_grad * sigmoid_c * (1.0 + conv_sum * (1.0 - sigmoid_c))).astype(jnp.bfloat16)
        kernel_total = kernel_total + kernel_grad(padded, conv_grads, tap_count)
        grad_padded = jnp.pad(conv_grads, ((half_taps, half_taps), (0, 0)))
        into_conv = depthwise(grad_padded, conv_kernel[::-1], frame_total) * live_rows
        second_part = lax.optimization_barrier(jnp.sum(into_conv * unit_two, axis=0))
        resid_grad = outer_grad + norm_backward(into_conv, unit_two, inv_two, second_gain)
        resid_low = resid_grad.astype(jnp.bfloat16)
        attended_grad = jnp.dot(resid_low, out_weight, preferred_element_type=jnp.float32).astype(jnp.bfloat16)
        query_list, key_list, value_list = ([], [], [])
        for head_index in range(HEADS):
            query_grads, key_sum, value_sum = attend_backward(head_cols(projected, 0, head_width, head_size, head_index), head_cols(projected, 1, head_width, head_size, head_index), head_cols(projected, 2, head_width, head_size, head_index), key_valid, head_cols(attended_grad, 0, head_width, head_size, head_index))
            query_list.append(query_grads)
            key_list.append(key_sum.astype(jnp.bfloat16))
            value_list.append(value_sum.astype(jnp.bfloat16))
        qkv_grads = jnp.concatenate(query_list + key_list + value_list, axis=1)
        normed_grad = contract_rows(qkv_grads, qkv_weight)
        first_part = lax.optimization_barrier(jnp.sum(normed_grad * unit_one, axis=0))
        grad_list.append((resid_grad + norm_backward(normed_grad, unit_one, inv_one, first_gain)).astype(jnp.bfloat16))
        weight_total = weight_total + jnp.concatenate([contract_cols(normed_low, qkv_grads), contract_cols(resid_low, attended)], axis=1)
        gain_total = gain_total + jnp.stack([first_part, second_part])
    return (jnp.stack(out_list), jnp.stack(grad_list), weight_total, gain_total, kernel_total)
```

```python
import jax
import jax.numpy as jnp
from jax import lax
from jax.experimental import pallas as pl
from jax.experimental.pallas import tpu as pltpu
from jax.sharding import PartitionSpec as P

HEADS = 8


epsilon = 1e-05


def padded_2(cells, sides, width):
    for axis, dim in sides:
        count = lax.axis_size(axis)
        ends = count - 1
        head = lax.slice_in_dim(cells, 0, width, axis=dim)
        tail = lax.slice_in_dim(cells, cells.shape[dim] - width, cells.shape[dim], axis=dim)
        cells = jnp.concatenate(
            [
                lax.ppermute(tail, axis, [(i, (i + 1) % count) for i in range(ends)]),
                cells,
                lax.ppermute(head, axis, [((i + 1) % count, i) for i in range(ends)]),
            ],
            axis=dim,
        )
    return cells


def layer_norm(rows, gain_vec):
    row_mean = jnp.mean(rows, axis=-1, keepdims=True)
    centered = rows - row_mean
    inv_std = lax.rsqrt(jnp.mean(centered * centered, axis=-1, keepdims=True) + epsilon)
    unit_rows = centered * inv_std
    return (unit_rows * gain_vec, unit_rows, inv_std)


def norm_backward(incoming, unit_rows, inv_std, gain_vec):
    scaled = incoming * gain_vec
    return inv_std * (
        scaled
        - jnp.mean(scaled, axis=-1, keepdims=True)
        - unit_rows * jnp.mean(scaled * unit_rows, axis=-1, keepdims=True)
    )


def contract_rows(left, right):
    return lax.dot_general(
        left, right, (((1,), (1,)), ((), ())), preferred_element_type=jnp.float32
    )


def contract_cols(left, right):
    return lax.dot_general(
        left, right, (((0,), (0,)), ((), ())), preferred_element_type=jnp.float32
    )


def soft_weights(queries, key_rows, key_valid):
    score_scale = queries.shape[1] ** (-0.5)
    scores = contract_rows(queries, key_rows) * score_scale
    scores = jnp.where(key_valid[None, :], scores, -jnp.inf)
    row_max = jnp.max(scores, axis=1, keepdims=True)
    exp_scores = jnp.exp(scores - row_max)
    return exp_scores / jnp.sum(exp_scores, axis=1, keepdims=True)


def attend_forward(queries, key_rows, value_rows, key_valid):
    block_rows = min(512, queries.shape[0])
    blocks = queries.reshape(queries.shape[0] // block_rows, block_rows, queries.shape[1])

    def one_block(query_block):
        attn_probs = soft_weights(query_block, key_rows, key_valid).astype(jnp.bfloat16)
        return jnp.dot(attn_probs, value_rows, preferred_element_type=jnp.float32).astype(
            jnp.bfloat16
        )

    return lax.map(one_block, blocks).reshape(queries.shape)


def attend_backward(queries, key_rows, value_rows, key_valid, out_grads):
    block_rows = min(512, queries.shape[0])
    block_count = queries.shape[0] // block_rows
    blocks = (
        queries.reshape(block_count, block_rows, queries.shape[1]),
        out_grads.reshape(block_count, block_rows, out_grads.shape[1]),
    )
    score_scale = queries.shape[1] ** (-0.5)

    def one_block(running, pieces):
        query_block, grad_block = pieces
        attn_probs = soft_weights(query_block, key_rows, key_valid)
        probs_low = attn_probs.astype(jnp.bfloat16)
        prob_grads = contract_rows(grad_block, value_rows)
        row_delta = jnp.sum(attn_probs * prob_grads, axis=1, keepdims=True)
        score_grads = (attn_probs * (prob_grads - row_delta) * score_scale).astype(jnp.bfloat16)
        query_grads = jnp.dot(score_grads, key_rows, preferred_element_type=jnp.float32).astype(
            jnp.bfloat16
        )
        key_sum = running[0] + contract_cols(score_grads, query_block)
        value_sum = running[1] + contract_cols(probs_low, grad_block)
        return ((key_sum, value_sum), query_grads)

    zero_rows = jnp.zeros(key_rows.shape, jnp.float32)
    totals, query_grads = lax.scan(one_block, (zero_rows, zero_rows), blocks)
    return (query_grads.reshape(queries.shape), totals[0], totals[1])


def depthwise(padded, kernel, frame_count):
    total = jnp.zeros((frame_count, padded.shape[1]), jnp.float32)
    for tap_index in range(kernel.shape[0]):
        total = (
            total
            + padded[tap_index : tap_index + frame_count].astype(jnp.float32) * kernel[tap_index]
        )
    return total


def kernel_grad(padded, grads, tap_count):
    frame_count = grads.shape[0]
    grads_wide = grads.astype(jnp.float32)
    sums = [
        jnp.sum(
            padded[tap_index : tap_index + frame_count].astype(jnp.float32) * grads_wide, axis=0
        )
        for tap_index in range(tap_count)
    ]
    return jnp.stack(sums)


def pack_queries(matrix, repeats, groups, channel):
    frames_dev = matrix.shape[0]
    shaped = matrix.reshape(repeats, frames_dev // repeats, groups, channel)
    return shaped.transpose(2, 0, 1, 3).reshape(groups * repeats, frames_dev // repeats, channel)


def pack_keys(matrix, repeats, groups, channel):
    frames_dev = matrix.shape[0]
    shaped = matrix.reshape(frames_dev, groups, channel).transpose(1, 0, 2)[:, None]
    widened = jnp.broadcast_to(shaped, (groups, repeats, frames_dev, channel))
    return widened.reshape(groups * repeats, frames_dev, channel)


def unpack_rows(stacked, repeats, groups):
    rows_each = stacked.shape[1]
    channel = stacked.shape[2]
    shaped = stacked.reshape(groups, repeats, rows_each, channel).transpose(1, 2, 0, 3)
    return shaped.reshape(repeats * rows_each, groups * channel)


def local_forward(query_rows, key_rows, value_rows, key_valid):
    outputs = attend_forward(query_rows, key_rows, value_rows, key_valid)
    return outputs


def local_backward(query_rows, key_rows, value_rows, key_valid, out_grads):
    query_list, key_list, value_list = ([], [], [])
    query_grads, key_sum, value_sum = attend_backward(
        query_rows, key_rows, value_rows, key_valid, out_grads
    )
    query_list.append(query_grads)
    key_list.append(key_sum)
    value_list.append(value_sum)
    return (query_list[0], key_list[0], value_list[0])


def general_shards(
    frames_in,
    lengths,
    first_gain,
    second_gain,
    qkv_weight,
    out_weight,
    conv_kernel,
    layer_cotangent,
):
    seq_count = lax.axis_size("seq")
    frames_dev = frames_in.shape[1]
    head_width = out_weight.shape[1]
    head_size = head_width // HEADS
    repeats = max(seq_count // HEADS, 1)
    per_device = max(HEADS // seq_count, 1)
    groups = seq_count // repeats
    channel = per_device * head_size
    tap_count = conv_kernel.shape[0]
    half_taps = (tap_count - 1) // 2
    my_index = lax.axis_index("seq")
    positions = my_index * frames_dev + jnp.arange(frames_dev, dtype=jnp.int32)
    live_rows = (positions < lengths[0]).astype(jnp.float32)[:, None]
    key_valid = jnp.arange(seq_count * frames_dev, dtype=jnp.int32) < lengths[0]
    inputs = frames_in[0].astype(jnp.float32)
    normed, unit_one, inv_one = layer_norm(inputs, first_gain)
    normed_low = normed.astype(jnp.bfloat16)
    projected = jnp.dot(normed_low, qkv_weight, preferred_element_type=jnp.float32).astype(
        jnp.bfloat16
    )
    query_send = pack_queries(projected[:, :head_width], repeats, groups, channel)
    key_send = pack_keys(projected[:, head_width : 2 * head_width], repeats, groups, channel)
    value_send = pack_keys(projected[:, 2 * head_width :], repeats, groups, channel)
    got_queries, got_keys, got_values = (
        lax.all_to_all(query_send, "seq", split_axis=0, concat_axis=1, tiled=True),
        lax.all_to_all(key_send, "seq", split_axis=0, concat_axis=1, tiled=True),
        lax.all_to_all(value_send, "seq", split_axis=0, concat_axis=1, tiled=True),
    )
    query_rows = got_queries[0]
    key_rows = got_keys[0]
    value_rows = got_values[0]
    head_out = local_forward(query_rows, key_rows, value_rows, key_valid)
    returned = lax.all_to_all(head_out[None], "seq", split_axis=1, concat_axis=0, tiled=True)
    attended = unpack_rows(returned, repeats, groups)
    resid = inputs + contract_rows(attended, out_weight)
    normed_two, unit_two, inv_two = layer_norm(resid, second_gain)
    conv_in = (live_rows * normed_two).astype(jnp.bfloat16)
    padded = padded_2(conv_in, (("seq", 0),), half_taps)
    conv_sum = depthwise(padded, conv_kernel, frames_dev)
    sigmoid_c = jax.nn.sigmoid(conv_sum)
    layer_out = (live_rows * (resid + conv_sum * sigmoid_c)).astype(jnp.bfloat16)
    outer_grad = live_rows * layer_cotangent[0].astype(jnp.float32)
    conv_grads = (outer_grad * sigmoid_c * (1.0 + conv_sum * (1.0 - sigmoid_c))).astype(
        jnp.bfloat16
    )
    kernel_part = kernel_grad(padded, conv_grads, tap_count)
    grad_padded = padded_2(conv_grads, (("seq", 0),), half_taps)
    into_conv = depthwise(grad_padded, conv_kernel[::-1], frames_dev) * live_rows
    second_part = jnp.sum(into_conv * unit_two, axis=0)
    resid_grad = outer_grad + norm_backward(into_conv, unit_two, inv_two, second_gain)
    resid_low = resid_grad.astype(jnp.bfloat16)
    attended_grad = jnp.dot(resid_low, out_weight, preferred_element_type=jnp.float32).astype(
        jnp.bfloat16
    )
    sent_grads = lax.all_to_all(
        pack_queries(attended_grad, repeats, groups, channel),
        "seq",
        split_axis=0,
        concat_axis=1,
        tiled=True,
    )
    query_grads, key_sums, value_sums = local_backward(
        query_rows, key_rows, value_rows, key_valid, sent_grads[0]
    )
    query_back = lax.all_to_all(query_grads[None], "seq", split_axis=1, concat_axis=0, tiled=True)
    key_back, value_back = (
        lax.all_to_all(
            key_sums[None].astype(jnp.bfloat16), "seq", split_axis=1, concat_axis=0, tiled=True
        ).astype(jnp.float32),
        lax.all_to_all(
            value_sums[None].astype(jnp.bfloat16), "seq", split_axis=1, concat_axis=0, tiled=True
        ).astype(jnp.float32),
    )

    def fold_parts(stacked):
        shaped = stacked.reshape(groups, repeats, frames_dev, channel)
        summed = jnp.sum(shaped, axis=1).transpose(1, 0, 2)
        return summed.reshape(frames_dev, head_width).astype(jnp.bfloat16)

    query_grad_rows = unpack_rows(query_back, repeats, groups)
    key_grad_rows = fold_parts(key_back)
    value_grad_rows = fold_parts(value_back)
    qkv_grads = jnp.concatenate([query_grad_rows, key_grad_rows, value_grad_rows], axis=1)
    normed_grad = contract_rows(qkv_grads, qkv_weight)
    first_part = jnp.sum(normed_grad * unit_one, axis=0)
    input_grad = (resid_grad + norm_backward(normed_grad, unit_one, inv_one, first_gain)).astype(
        jnp.bfloat16
    )
    weight_grads = lax.psum_scatter(
        jnp.concatenate(
            [contract_cols(normed_low, qkv_grads), contract_cols(resid_low, attended)], axis=1
        ),
        ("dp", "seq"),
        scatter_dimension=0,
        tiled=True,
    )
    gain_sum, kernel_sum = lax.psum(
        (jnp.stack([first_part, second_part]), kernel_part), ("dp", "seq")
    )
    return (layer_out[None], input_grad[None], weight_grads, gain_sum, kernel_sum)


HALO = 32
BF16 = jnp.bfloat16
F32 = jnp.float32
VMEM_LIMIT = 56 * 2**20
CHUNK = 128
QUERY_BLOCK = 256


def vmem(count):
    return [pl.BlockSpec(memory_space=pltpu.VMEM)] * count


def smem():
    return pl.BlockSpec(memory_space=pltpu.SMEM)


def cost(flops, nbytes):
    return pl.CostEstimate(flops=int(flops), bytes_accessed=int(nbytes), transcendentals=0)


def dot_nn(left, right):
    return lax.dot_general(left, right, (((1,), (0,)), ((), ())), preferred_element_type=F32)


def dot_nt(left, right):
    return lax.dot_general(left, right, (((1,), (1,)), ((), ())), preferred_element_type=F32)


def unit_norm(rows):
    centered = rows - jnp.mean(rows, axis=-1, keepdims=True)
    inv_std = lax.rsqrt(jnp.mean(centered * centered, axis=-1, keepdims=True) + epsilon)
    return centered * inv_std, inv_std


def first_norm_kernel(x_ref, gain_ref, out_ref):
    unit, _ = unit_norm(x_ref[...].astype(F32))
    out_ref[...] = (unit * gain_ref[...]).astype(BF16)


def first_norm(frames, gain):
    return pl.pallas_call(
        first_norm_kernel,
        out_shape=jax.ShapeDtypeStruct(frames.shape, BF16),
        in_specs=vmem(2),
        out_specs=vmem(1)[0],
        compiler_params=pltpu.CompilerParams(vmem_limit_bytes=VMEM_LIMIT),
        cost_estimate=cost(frames.size * 10, frames.size * 4),
        name="first_norm",
    )(frames, gain)


def key_weights(scores, length, scale):
    live = lax.broadcasted_iota(jnp.int32, scores.shape, 0) < length
    return jnp.where(live, scores * scale, -jnp.inf)


def forward_kernel(len_ref, normed_ref, weight_ref, qkv_ref, stats_ref, out_ref, att_ref, wide_ref):
    size = weight_ref.shape[0] // 3
    frames = normed_ref.shape[0]
    length = len_ref[0]
    scale = size**-0.5
    qkv = dot_nt(weight_ref[...], normed_ref[...])
    qkv_ref[...] = qkv.astype(BF16)
    keys = qkv_ref[size : 2 * size, :].astype(F32).T.astype(BF16)
    values = qkv_ref[2 * size :, :]
    for start in range(0, frames, QUERY_BLOCK):
        cols = slice(start, start + QUERY_BLOCK)
        scores = key_weights(dot_nn(keys, qkv_ref[0:size, cols]), length, scale)
        top = jnp.max(scores, axis=0, keepdims=True)
        exps = jnp.exp(scores - top)
        inverse = 1.0 / jnp.sum(exps, axis=0, keepdims=True)
        attended = dot_nn(values, (exps * inverse).astype(BF16)).astype(BF16)
        att_ref[:, cols] = attended
        wide_ref[:, cols] = attended.astype(F32)
        stats_ref[0:1, cols] = top
        stats_ref[1:2, cols] = inverse
    peers, rows, width = out_ref.shape
    half = size // 2
    blank = jnp.zeros((size, HALO), F32)
    for peer in range(peers):
        first, last = peer * width, (peer + 1) * width
        out_ref[peer, 0:size, :] = att_ref[:, first:last]
        before = wide_ref[:, first - width : first][:, width - HALO :] if peer else blank
        after = wide_ref[:, last : last + width][:, :HALO] if peer < peers - 1 else blank
        edges = jnp.concatenate([before, after], axis=1)
        packed = jnp.concatenate([edges[:half], edges[half:]], axis=1)
        out_ref[peer, size:, :] = packed.astype(BF16)


def attention_forward(length, normed_all, head_weight, peers):
    frames, model = normed_all.shape
    size = head_weight.shape[0] // 3
    return pl.pallas_call(
        forward_kernel,
        out_shape=(
            jax.ShapeDtypeStruct((3 * size, frames), BF16),
            jax.ShapeDtypeStruct((8, frames), F32),
            jax.ShapeDtypeStruct((peers, size + size // 2, frames // peers), BF16),
            jax.ShapeDtypeStruct((size, frames), BF16),
        ),
        in_specs=[smem()] + vmem(2),
        out_specs=tuple(vmem(4)),
        scratch_shapes=[pltpu.VMEM((size, frames), F32)],
        compiler_params=pltpu.CompilerParams(vmem_limit_bytes=VMEM_LIMIT),
        cost_estimate=cost(6 * size * frames * model + 4 * frames * frames * size, 2 * frames * model),
        name="attention_forward",
    )(length, normed_all, head_weight)


def middle_kernel(
    info_ref,
    att_ref,
    x_ref,
    before_ref,
    after_ref,
    cot_ref,
    weight_ref,
    gain_ref,
    taps_ref,
    layer_ref,
    resid_grad_ref,
    low_ref,
    send_ref,
    taps_out_ref,
    resid_ref,
    unit_ref,
    conv_ref,
    grads_ref,
    into_ref,
    sum_ref,
    dot_ref,
):
    heads, packed_rows, width = att_ref.shape
    size = packed_rows * 2 // 3
    half = size // 2
    model = x_ref.shape[1]
    tap_count = taps_ref.shape[0]
    reach = (tap_count - 1) // 2
    near = HALO // 2
    main, edges = [], []
    for head in range(heads):
        main.append(att_ref[head, 0:size, :].astype(F32))
        packed = att_ref[head, size:, :].astype(F32)
        edges.append(packed[:, 0 : 2 * HALO])
        edges.append(packed[:, 2 * HALO :])
    att = jnp.concatenate(
        [jnp.concatenate(main, axis=0).T, jnp.concatenate(edges, axis=0).T], axis=0
    ).astype(BF16)
    product = dot_nt(att, weight_ref[...])
    resid_ref[0:HALO, :] = before_ref[0:HALO, :].astype(F32) + product[width : width + HALO]
    resid_ref[HALO : HALO + width, :] = x_ref[...].astype(F32) + product[:width]
    resid_ref[HALO + width :, :] = after_ref[0:HALO, :].astype(F32) + product[width + HALO :]
    unit, inv_std = unit_norm(resid_ref[...])
    unit_ref[...] = unit[HALO : HALO + width]
    rows = width + 2 * HALO
    place = lax.broadcasted_iota(jnp.int32, (rows, 1), 0) - HALO + info_ref[0]
    live = jnp.where((place >= 0) & (place < info_ref[1]), 1.0, 0.0).astype(F32)
    conv_ref[...] = (live * (unit * gain_ref[...])).astype(BF16).astype(F32)
    span = width + 2 * near
    live_span = live[near : near + span]
    live_main = live[HALO : HALO + width]
    sum_ref[...] = jnp.zeros_like(sum_ref)
    dot_ref[...] = jnp.zeros_like(dot_ref)

    @pl.loop(0, model // CHUNK)
    def _(step):
        cols = pl.ds(pl.multiple_of(step * CHUNK, CHUNK), CHUNK)
        taps = taps_ref[:, cols]
        total = jnp.zeros((span, CHUNK), F32)
        for tap in range(tap_count):
            total = total + conv_ref[pl.ds(HALO - near - reach + tap, span), cols] * taps[tap : tap + 1]
        gate = 1.0 / (1.0 + jnp.exp(-total))
        resid = resid_ref[pl.ds(HALO, width), cols]
        layer_ref[:, cols] = (
            live_main * (resid + total[near : near + width] * gate[near : near + width])
        ).astype(BF16)
        outer = live_span * jnp.concatenate(
            [before_ref[HALO:, cols], cot_ref[:, cols], after_ref[HALO:, cols]], axis=0
        ).astype(F32)
        grads = (outer * gate * (1.0 + total * (1.0 - gate))).astype(BF16).astype(F32)
        grads_ref[...] = grads
        inner = grads[near : near + width]
        for tap in range(tap_count):
            terms = conv_ref[pl.ds(HALO - reach + tap, width), cols] * inner
            taps_out_ref[tap : tap + 1, cols] = jnp.sum(terms, axis=0, keepdims=True)
        into = jnp.zeros((width, CHUNK), F32)
        for tap in range(tap_count):
            into = into + grads_ref[pl.ds(near + reach - tap, width), :] * taps[tap : tap + 1]
        into = into * live_main
        unit_part = unit_ref[:, cols]
        taps_out_ref[tap_count : tap_count + 1, cols] = jnp.sum(into * unit_part, axis=0, keepdims=True)
        scaled = into * gain_ref[:, cols]
        into_ref[:, cols] = scaled
        sum_ref[...] += scaled
        dot_ref[...] += scaled * unit_part

    mean = jnp.sum(sum_ref[...], axis=1, keepdims=True) / model
    mean_dot = jnp.sum(dot_ref[...], axis=1, keepdims=True) / model
    resid_grad = live_main * cot_ref[...].astype(F32) + inv_std[HALO : HALO + width] * (
        into_ref[...] - mean - unit_ref[...] * mean_dot
    )
    resid_grad_ref[...] = resid_grad
    low = resid_grad.astype(BF16)
    low_ref[...] = low
    send = dot_nn(low, weight_ref[...]).T.astype(BF16)
    send_ref[...] = send.reshape(send_ref.shape)


def middle(info, attended, frames, before, after, cotangent, out_weight, gain, taps):
    heads, packed_rows, width = attended.shape
    size = packed_rows * 2 // 3
    model = frames.shape[1]
    rows = width + 2 * HALO
    return pl.pallas_call(
        middle_kernel,
        out_shape=(
            jax.ShapeDtypeStruct((width, model), BF16),
            jax.ShapeDtypeStruct((width, model), F32),
            jax.ShapeDtypeStruct((width, model), BF16),
            jax.ShapeDtypeStruct((heads, size, width), BF16),
            jax.ShapeDtypeStruct((taps.shape[0] + 1, model), F32),
        ),
        in_specs=[smem()] + vmem(8),
        out_specs=tuple(vmem(5)),
        scratch_shapes=[
            pltpu.VMEM((rows, model), F32),
            pltpu.VMEM((width, model), F32),
            pltpu.VMEM((rows, model), F32),
            pltpu.VMEM((width + HALO, CHUNK), F32),
            pltpu.VMEM((width, model), F32),
            pltpu.VMEM((width, CHUNK), F32),
            pltpu.VMEM((width, CHUNK), F32),
        ],
        compiler_params=pltpu.CompilerParams(vmem_limit_bytes=VMEM_LIMIT),
        cost_estimate=cost(4 * rows * model * heads * size * 8, 2 * model * heads * size),
        name="middle",
    )(info, attended, frames, before, after, cotangent, out_weight, gain, taps)


def backward_kernel(len_ref, qkv_ref, stats_ref, grad_ref, send_ref, out_ref):
    size = qkv_ref.shape[0] // 3
    frames = qkv_ref.shape[1]
    peers, _, width = grad_ref.shape
    length = len_ref[0]
    scale = size**-0.5
    keys_turned = qkv_ref[size : 2 * size, :]
    keys = keys_turned.astype(F32).T.astype(BF16)
    values = qkv_ref[2 * size :, :].astype(F32).T.astype(BF16)
    grads = jnp.concatenate([grad_ref[peer] for peer in range(peers)], axis=1)
    key_sum = jnp.zeros((size, frames), F32)
    value_sum = jnp.zeros((size, frames), F32)
    for start in range(0, frames, QUERY_BLOCK):
        cols = slice(start, start + QUERY_BLOCK)
        queries = qkv_ref[0:size, cols]
        block = grads[:, cols]
        scores = key_weights(dot_nn(keys, queries), length, scale)
        probs = jnp.exp(scores - stats_ref[0:1, cols]) * stats_ref[1:2, cols]
        prob_grads = dot_nn(values, block)
        delta = jnp.sum(probs * prob_grads, axis=0, keepdims=True)
        score_grads = (probs * (prob_grads - delta) * scale).astype(BF16)
        out_ref[0:size, cols] = dot_nn(keys_turned, score_grads).astype(BF16)
        key_sum = key_sum + dot_nt(queries, score_grads)
        value_sum = value_sum + dot_nt(block, probs.astype(BF16))
    out_ref[size : 2 * size, :] = key_sum.astype(BF16)
    out_ref[2 * size :, :] = value_sum.astype(BF16)
    for peer in range(peers):
        send_ref[peer] = out_ref[:, peer * width : (peer + 1) * width]


def attention_backward(length, qkv, stats, grads):
    peers, size, width = grads.shape
    frames = peers * width
    return pl.pallas_call(
        backward_kernel,
        out_shape=(
            jax.ShapeDtypeStruct((peers, 3 * size, width), BF16),
            jax.ShapeDtypeStruct((3 * size, frames), BF16),
        ),
        in_specs=[smem()] + vmem(3),
        out_specs=tuple(vmem(2)),
        compiler_params=pltpu.CompilerParams(vmem_limit_bytes=VMEM_LIMIT),
        cost_estimate=cost(20 * frames * frames * size, 2 * frames * size * 10),
        name="attention_backward",
    )(length, qkv, stats, grads)


def weight_kernel(qkv_grad_ref, att_ref, normed_ref, low_ref, out_ref):
    size = att_ref.shape[0]
    model = normed_ref.shape[1]

    @pl.loop(0, model // (2 * CHUNK))
    def _(step):
        cols = pl.ds(pl.multiple_of(step * 2 * CHUNK, 2 * CHUNK), 2 * CHUNK)
        turned = jnp.concatenate(
            [dot_nn(qkv_grad_ref[...], normed_ref[:, cols]), dot_nn(att_ref[...], low_ref[:, cols])],
            axis=0,
        )
        out_ref[cols, :] = turned.T.astype(BF16)


def weight_parts(qkv_grads, attended, normed_all, low_all):
    frames, model = normed_all.shape
    size = attended.shape[0]
    return pl.pallas_call(
        weight_kernel,
        out_shape=jax.ShapeDtypeStruct((model, 4 * size), BF16),
        in_specs=vmem(4),
        out_specs=vmem(1)[0],
        compiler_params=pltpu.CompilerParams(vmem_limit_bytes=VMEM_LIMIT),
        cost_estimate=cost(8 * frames * model * size, 6 * frames * model),
        name="weight_parts",
    )(qkv_grads, attended, normed_all, low_all)


def input_kernel(grad_ref, weight_ref, x_ref, resid_grad_ref, gain_ref, out_ref, rows_ref, normed_ref):
    step = pl.program_id(0)
    heads, triple, width = grad_ref.shape
    size = triple // 3
    block = weight_ref.shape[0]

    @pl.when(step == 0)
    def _():
        turned = jnp.concatenate(
            [
                grad_ref[head, part * size : (part + 1) * size, :].astype(F32)
                for part in range(3)
                for head in range(heads)
            ],
            axis=0,
        )
        rows_ref[...] = turned.T.astype(BF16)

    cols = pl.ds(pl.multiple_of(step * block, block), block)
    normed_ref[:, cols] = dot_nt(rows_ref[...], weight_ref[...])

    @pl.when(step == pl.num_programs(0) - 1)
    def _():
        unit, inv_std = unit_norm(x_ref[...].astype(F32))
        scaled = normed_ref[...] * gain_ref[...]
        out_ref[...] = (
            resid_grad_ref[...]
            + inv_std
            * (
                scaled
                - jnp.mean(scaled, axis=-1, keepdims=True)
                - unit * jnp.mean(scaled * unit, axis=-1, keepdims=True)
            )
        ).astype(BF16)


def input_grads(grads, weight, frames, resid_grad, gain):
    heads, triple, width = grads.shape
    model, columns = weight.shape
    block = 2 * CHUNK
    return pl.pallas_call(
        input_kernel,
        grid=(model // block,),
        out_shape=jax.ShapeDtypeStruct((width, model), BF16),
        in_specs=[
            pl.BlockSpec((heads, triple, width), lambda i: (0, 0, 0)),
            pl.BlockSpec((block, columns), lambda i: (i, 0)),
            pl.BlockSpec((width, model), lambda i: (0, 0)),
            pl.BlockSpec((width, model), lambda i: (0, 0)),
            pl.BlockSpec((1, model), lambda i: (0, 0)),
        ],
        out_specs=pl.BlockSpec((width, model), lambda i: (0, 0)),
        scratch_shapes=[pltpu.VMEM((width, columns), BF16), pltpu.VMEM((width, model), F32)],
        compiler_params=pltpu.CompilerParams(vmem_limit_bytes=VMEM_LIMIT),
        cost_estimate=cost(2 * width * model * columns, 2 * model * columns),
        name="input_grads",
    )(grads, weight, frames, resid_grad, gain)


def final_kernel(heads, got_ref, weight_ref, gain_ref, out_ref, part_ref):
    groups = got_ref.shape[0] // heads
    size = got_ref.shape[2] // 4
    sums = []
    for head in range(heads):
        total = got_ref[head].astype(F32)
        for group in range(1, groups):
            total = total + got_ref[group * heads + head].astype(F32)
        sums.append(total)
    out_ref[...] = jnp.concatenate(
        [total[:, part * size : (part + 1) * size] for part in range(4) for total in sums], axis=1
    )
    columns = weight_ref.shape[1]
    products = out_ref[:, 0:columns] * weight_ref[...].astype(F32)
    part_ref[...] = jnp.sum(products, axis=1, keepdims=True) / gain_ref[...]


def final_sums(got, weight_rows, gain_rows, heads):
    rows = got.shape[1]
    width = heads * got.shape[2]
    return pl.pallas_call(
        lambda *refs: final_kernel(heads, *refs),
        out_shape=(
            jax.ShapeDtypeStruct((rows, width), F32),
            jax.ShapeDtypeStruct((rows, 1), F32),
        ),
        in_specs=vmem(3),
        out_specs=tuple(vmem(2)),
        compiler_params=pltpu.CompilerParams(vmem_limit_bytes=VMEM_LIMIT),
        cost_estimate=cost(got.size * 4, got.size * 2),
        name="final_sums",
    )(got, weight_rows, gain_rows)


def exchange(blocks, axes):
    return lax.all_to_all(blocks, axes, split_axis=0, concat_axis=0, tiled=True)


def head_shards(
    frames_in,
    lengths,
    first_gain,
    second_gain,
    qkv_weight,
    out_weight,
    conv_kernel,
    layer_cotangent,
):
    both = ("dp", "seq")
    peers = lax.axis_size("seq")
    everyone = peers * lax.axis_size("dp")
    width, model = frames_in.shape[1:]
    size = out_weight.shape[1] // HEADS
    mine = lax.axis_index("seq")
    number = lax.axis_index("dp") * peers + mine
    share = model // everyone
    frames, cotangent = frames_in[0], layer_cotangent[0]
    gain_one, gain_two = first_gain[None], second_gain[None]
    normed = first_norm(frames, gain_one)
    normed_all = lax.all_gather(normed, "seq", axis=0, tiled=True)
    head_weight = jnp.concatenate(
        [
            lax.dynamic_slice_in_dim(qkv_weight, part * HEADS * size + mine * size, size, axis=1)
            for part in range(3)
        ],
        axis=1,
    ).T
    near = HALO // 2
    tails = jnp.concatenate([frames[width - HALO :], cotangent[width - near :]], axis=0)
    fronts = jnp.concatenate([frames[:HALO], cotangent[:near]], axis=0)
    before = lax.ppermute(tails, "seq", [(i, i + 1) for i in range(peers - 1)])
    after = lax.ppermute(fronts, "seq", [(i + 1, i) for i in range(peers - 1)])
    qkv, stats, att_send, att_head = attention_forward(lengths, normed_all, head_weight, peers)
    attended = exchange(att_send, "seq")
    info = jnp.stack([mine * width, lengths[0]]).astype(jnp.int32)
    layer_out, resid_grad, low, grad_send, taps_part = middle(
        info, attended, frames, before, after, cotangent, out_weight, gain_two, conv_kernel
    )
    low_all = lax.all_gather(low, "seq", axis=0, tiled=True)
    grads, taps_part = lax.optimization_barrier((exchange(grad_send, "seq"), taps_part))
    taps_got = exchange(taps_part, both)
    back_send, back_head = attention_backward(lengths, qkv, stats, grads)
    back_send, taps_got = lax.optimization_barrier((back_send, taps_got))
    taps_row = jnp.sum(taps_got, axis=0)
    back, back_head, low_all = lax.optimization_barrier(
        (exchange(back_send, "seq"), back_head, low_all)
    )
    parts = weight_parts(back_head, att_head, normed_all, low_all)
    got = exchange(parts.reshape(everyone, share, 4 * size), both)
    input_grad = input_grads(back, qkv_weight, frames, resid_grad, gain_one)
    got, input_grad = lax.optimization_barrier((got, input_grad))
    weight_rows = lax.dynamic_slice_in_dim(qkv_weight, number * share, share, axis=0)
    gain_rows = lax.dynamic_slice_in_dim(first_gain, number * share, share, axis=0)[:, None]
    weight_grads, gain_part = final_sums(got, weight_rows, gain_rows, HEADS)
    row = jnp.concatenate([taps_row, gain_part.reshape(-1)])
    rows = exchange(jnp.broadcast_to(row[None], (everyone, row.shape[0])), both)
    tap_count = conv_kernel.shape[0]
    conv_grad = rows[:tap_count, :model]
    gain_grads = jnp.stack([rows[:, model:].reshape(-1), rows[tap_count, :model]])
    return (layer_out[None], input_grad[None], weight_grads, gain_grads, conv_grad)


def solution(mesh):
    in_specs = (P("dp", "seq", None), P("dp"), P(), P(), P(), P(), P(), P("dp", "seq", None))
    out_specs = (P("dp", "seq", None), P("dp", "seq", None), P(("dp", "seq"), None), P(), P())
    seq_count = mesh.shape["seq"]
    device_count = seq_count * mesh.shape["dp"]

    def program(*args):
        frames_dev = args[0].shape[1] // seq_count
        fits = seq_count == HEADS and frames_dev == 128 and device_count == args[6].shape[0] + 1
        plan = head_shards if fits else general_shards
        return jax.shard_map(
            plan, mesh=mesh, in_specs=in_specs, out_specs=out_specs, check_vma=False
        )(*args)

    return program
```

```python
import jax
import jax.numpy as jnp
from jax import lax
from jax.experimental import pallas as pl
from jax.experimental.pallas import tpu as pltpu
from jax.sharding import PartitionSpec as P

HEADS = 8


epsilon = 1e-05


def padded_2(cells, sides, width):
    for axis, dim in sides:
        count = lax.axis_size(axis)
        ends = count - 1
        head = lax.slice_in_dim(cells, 0, width, axis=dim)
        tail = lax.slice_in_dim(cells, cells.shape[dim] - width, cells.shape[dim], axis=dim)
        cells = jnp.concatenate(
            [
                lax.ppermute(tail, axis, [(i, (i + 1) % count) for i in range(ends)]),
                cells,
                lax.ppermute(head, axis, [((i + 1) % count, i) for i in range(ends)]),
            ],
            axis=dim,
        )
    return cells


def layer_norm(rows, gain_vec):
    row_mean = jnp.mean(rows, axis=-1, keepdims=True)
    centered = rows - row_mean
    inv_std = lax.rsqrt(jnp.mean(centered * centered, axis=-1, keepdims=True) + epsilon)
    unit_rows = centered * inv_std
    return (unit_rows * gain_vec, unit_rows, inv_std)


def norm_backward(incoming, unit_rows, inv_std, gain_vec):
    scaled = incoming * gain_vec
    return inv_std * (
        scaled
        - jnp.mean(scaled, axis=-1, keepdims=True)
        - unit_rows * jnp.mean(scaled * unit_rows, axis=-1, keepdims=True)
    )


def contract_rows(left, right):
    return lax.dot_general(
        left, right, (((1,), (1,)), ((), ())), preferred_element_type=jnp.float32
    )


def contract_cols(left, right):
    return lax.dot_general(
        left, right, (((0,), (0,)), ((), ())), preferred_element_type=jnp.float32
    )


def soft_weights(queries, key_rows, key_valid):
    score_scale = queries.shape[1] ** (-0.5)
    scores = contract_rows(queries, key_rows) * score_scale
    scores = jnp.where(key_valid[None, :], scores, -jnp.inf)
    row_max = jnp.max(scores, axis=1, keepdims=True)
    exp_scores = jnp.exp(scores - row_max)
    return exp_scores / jnp.sum(exp_scores, axis=1, keepdims=True)


def attend_forward(queries, key_rows, value_rows, key_valid):
    block_rows = min(512, queries.shape[0])
    blocks = queries.reshape(queries.shape[0] // block_rows, block_rows, queries.shape[1])

    def one_block(query_block):
        attn_probs = soft_weights(query_block, key_rows, key_valid).astype(jnp.bfloat16)
        return jnp.dot(attn_probs, value_rows, preferred_element_type=jnp.float32).astype(
            jnp.bfloat16
        )

    return lax.map(one_block, blocks).reshape(queries.shape)


def attend_backward(queries, key_rows, value_rows, key_valid, out_grads):
    block_rows = min(512, queries.shape[0])
    block_count = queries.shape[0] // block_rows
    blocks = (
        queries.reshape(block_count, block_rows, queries.shape[1]),
        out_grads.reshape(block_count, block_rows, out_grads.shape[1]),
    )
    score_scale = queries.shape[1] ** (-0.5)

    def one_block(running, pieces):
        query_block, grad_block = pieces
        attn_probs = soft_weights(query_block, key_rows, key_valid)
        probs_low = attn_probs.astype(jnp.bfloat16)
        prob_grads = contract_rows(grad_block, value_rows)
        row_delta = jnp.sum(attn_probs * prob_grads, axis=1, keepdims=True)
        score_grads = (attn_probs * (prob_grads - row_delta) * score_scale).astype(jnp.bfloat16)
        query_grads = jnp.dot(score_grads, key_rows, preferred_element_type=jnp.float32).astype(
            jnp.bfloat16
        )
        key_sum = running[0] + contract_cols(score_grads, query_block)
        value_sum = running[1] + contract_cols(probs_low, grad_block)
        return ((key_sum, value_sum), query_grads)

    zero_rows = jnp.zeros(key_rows.shape, jnp.float32)
    totals, query_grads = lax.scan(one_block, (zero_rows, zero_rows), blocks)
    return (query_grads.reshape(queries.shape), totals[0], totals[1])


def depthwise(padded, kernel, frame_count):
    total = jnp.zeros((frame_count, padded.shape[1]), jnp.float32)
    for tap_index in range(kernel.shape[0]):
        total = (
            total
            + padded[tap_index : tap_index + frame_count].astype(jnp.float32) * kernel[tap_index]
        )
    return total


def kernel_grad(padded, grads, tap_count):
    frame_count = grads.shape[0]
    grads_wide = grads.astype(jnp.float32)
    sums = [
        jnp.sum(
            padded[tap_index : tap_index + frame_count].astype(jnp.float32) * grads_wide, axis=0
        )
        for tap_index in range(tap_count)
    ]
    return jnp.stack(sums)


def pack_queries(matrix, repeats, groups, channel):
    frames_dev = matrix.shape[0]
    shaped = matrix.reshape(repeats, frames_dev // repeats, groups, channel)
    return shaped.transpose(2, 0, 1, 3).reshape(groups * repeats, frames_dev // repeats, channel)


def pack_keys(matrix, repeats, groups, channel):
    frames_dev = matrix.shape[0]
    shaped = matrix.reshape(frames_dev, groups, channel).transpose(1, 0, 2)[:, None]
    widened = jnp.broadcast_to(shaped, (groups, repeats, frames_dev, channel))
    return widened.reshape(groups * repeats, frames_dev, channel)


def unpack_rows(stacked, repeats, groups):
    rows_each = stacked.shape[1]
    channel = stacked.shape[2]
    shaped = stacked.reshape(groups, repeats, rows_each, channel).transpose(1, 2, 0, 3)
    return shaped.reshape(repeats * rows_each, groups * channel)


def local_forward(query_rows, key_rows, value_rows, key_valid):
    outputs = attend_forward(query_rows, key_rows, value_rows, key_valid)
    return outputs


def local_backward(query_rows, key_rows, value_rows, key_valid, out_grads):
    query_list, key_list, value_list = ([], [], [])
    query_grads, key_sum, value_sum = attend_backward(
        query_rows, key_rows, value_rows, key_valid, out_grads
    )
    query_list.append(query_grads)
    key_list.append(key_sum)
    value_list.append(value_sum)
    return (query_list[0], key_list[0], value_list[0])


def general_shards(
    frames_in,
    lengths,
    first_gain,
    second_gain,
    qkv_weight,
    out_weight,
    conv_kernel,
    layer_cotangent,
):
    seq_count = lax.axis_size("seq")
    frames_dev = frames_in.shape[1]
    head_width = out_weight.shape[1]
    head_size = head_width // HEADS
    repeats = max(seq_count // HEADS, 1)
    per_device = max(HEADS // seq_count, 1)
    groups = seq_count // repeats
    channel = per_device * head_size
    tap_count = conv_kernel.shape[0]
    half_taps = (tap_count - 1) // 2
    my_index = lax.axis_index("seq")
    positions = my_index * frames_dev + jnp.arange(frames_dev, dtype=jnp.int32)
    live_rows = (positions < lengths[0]).astype(jnp.float32)[:, None]
    key_valid = jnp.arange(seq_count * frames_dev, dtype=jnp.int32) < lengths[0]
    inputs = frames_in[0].astype(jnp.float32)
    normed, unit_one, inv_one = layer_norm(inputs, first_gain)
    normed_low = normed.astype(jnp.bfloat16)
    projected = jnp.dot(normed_low, qkv_weight, preferred_element_type=jnp.float32).astype(
        jnp.bfloat16
    )
    query_send = pack_queries(projected[:, :head_width], repeats, groups, channel)
    key_send = pack_keys(projected[:, head_width : 2 * head_width], repeats, groups, channel)
    value_send = pack_keys(projected[:, 2 * head_width :], repeats, groups, channel)
    got_queries, got_keys, got_values = (
        lax.all_to_all(query_send, "seq", split_axis=0, concat_axis=1, tiled=True),
        lax.all_to_all(key_send, "seq", split_axis=0, concat_axis=1, tiled=True),
        lax.all_to_all(value_send, "seq", split_axis=0, concat_axis=1, tiled=True),
    )
    query_rows = got_queries[0]
    key_rows = got_keys[0]
    value_rows = got_values[0]
    head_out = local_forward(query_rows, key_rows, value_rows, key_valid)
    returned = lax.all_to_all(head_out[None], "seq", split_axis=1, concat_axis=0, tiled=True)
    attended = unpack_rows(returned, repeats, groups)
    resid = inputs + contract_rows(attended, out_weight)
    normed_two, unit_two, inv_two = layer_norm(resid, second_gain)
    conv_in = (live_rows * normed_two).astype(jnp.bfloat16)
    padded = padded_2(conv_in, (("seq", 0),), half_taps)
    conv_sum = depthwise(padded, conv_kernel, frames_dev)
    sigmoid_c = jax.nn.sigmoid(conv_sum)
    layer_out = (live_rows * (resid + conv_sum * sigmoid_c)).astype(jnp.bfloat16)
    outer_grad = live_rows * layer_cotangent[0].astype(jnp.float32)
    conv_grads = (outer_grad * sigmoid_c * (1.0 + conv_sum * (1.0 - sigmoid_c))).astype(
        jnp.bfloat16
    )
    kernel_part = kernel_grad(padded, conv_grads, tap_count)
    grad_padded = padded_2(conv_grads, (("seq", 0),), half_taps)
    into_conv = depthwise(grad_padded, conv_kernel[::-1], frames_dev) * live_rows
    second_part = jnp.sum(into_conv * unit_two, axis=0)
    resid_grad = outer_grad + norm_backward(into_conv, unit_two, inv_two, second_gain)
    resid_low = resid_grad.astype(jnp.bfloat16)
    attended_grad = jnp.dot(resid_low, out_weight, preferred_element_type=jnp.float32).astype(
        jnp.bfloat16
    )
    sent_grads = lax.all_to_all(
        pack_queries(attended_grad, repeats, groups, channel),
        "seq",
        split_axis=0,
        concat_axis=1,
        tiled=True,
    )
    query_grads, key_sums, value_sums = local_backward(
        query_rows, key_rows, value_rows, key_valid, sent_grads[0]
    )
    query_back = lax.all_to_all(query_grads[None], "seq", split_axis=1, concat_axis=0, tiled=True)
    key_back, value_back = (
        lax.all_to_all(
            key_sums[None].astype(jnp.bfloat16), "seq", split_axis=1, concat_axis=0, tiled=True
        ).astype(jnp.float32),
        lax.all_to_all(
            value_sums[None].astype(jnp.bfloat16), "seq", split_axis=1, concat_axis=0, tiled=True
        ).astype(jnp.float32),
    )

    def fold_parts(stacked):
        shaped = stacked.reshape(groups, repeats, frames_dev, channel)
        summed = jnp.sum(shaped, axis=1).transpose(1, 0, 2)
        return summed.reshape(frames_dev, head_width).astype(jnp.bfloat16)

    query_grad_rows = unpack_rows(query_back, repeats, groups)
    key_grad_rows = fold_parts(key_back)
    value_grad_rows = fold_parts(value_back)
    qkv_grads = jnp.concatenate([query_grad_rows, key_grad_rows, value_grad_rows], axis=1)
    normed_grad = contract_rows(qkv_grads, qkv_weight)
    first_part = jnp.sum(normed_grad * unit_one, axis=0)
    input_grad = (resid_grad + norm_backward(normed_grad, unit_one, inv_one, first_gain)).astype(
        jnp.bfloat16
    )
    weight_grads = lax.psum_scatter(
        jnp.concatenate(
            [contract_cols(normed_low, qkv_grads), contract_cols(resid_low, attended)], axis=1
        ),
        ("dp", "seq"),
        scatter_dimension=0,
        tiled=True,
    )
    gain_sum, kernel_sum = lax.psum(
        (jnp.stack([first_part, second_part]), kernel_part), ("dp", "seq")
    )
    return (layer_out[None], input_grad[None], weight_grads, gain_sum, kernel_sum)


HALO = 32
BF16 = jnp.bfloat16
F32 = jnp.float32
VMEM_LIMIT = 56 * 2**20
CHUNK = 128
QUERY_BLOCK = 256
TAP_ROWS = 16


def vmem(count):
    return [pl.BlockSpec(memory_space=pltpu.VMEM)] * count


def smem():
    return pl.BlockSpec(memory_space=pltpu.SMEM)


def cost(*_):
    return pl.CostEstimate(flops=1000, bytes_accessed=1000, transcendentals=0)


def dot_nn(left, right):
    return lax.dot_general(left, right, (((1,), (0,)), ((), ())), preferred_element_type=F32)


def dot_nt(left, right):
    return lax.dot_general(left, right, (((1,), (1,)), ((), ())), preferred_element_type=F32)


def unit_norm(rows):
    centered = rows - jnp.mean(rows, axis=-1, keepdims=True)
    inv_std = lax.rsqrt(jnp.mean(centered * centered, axis=-1, keepdims=True) + epsilon)
    return centered * inv_std, inv_std


def project_kernel(x_ref, gain_ref, weight_ref, send_ref, normed_ref):
    @pl.when(pl.program_id(0) == 0)
    def _():
        unit, _ = unit_norm(x_ref[...].astype(F32))
        normed_ref[...] = (unit * gain_ref[...]).astype(BF16)

    product = dot_nn(normed_ref[...], weight_ref[...])
    send_ref[...] = product.T.astype(BF16).reshape(send_ref.shape)


def project(frames, gain, weight, peers):
    width, model = frames.shape
    columns = weight.shape[1]
    size = columns // (3 * peers)
    heads = peers // 2
    return pl.pallas_call(
        project_kernel,
        grid=(6,),
        out_shape=(
            jax.ShapeDtypeStruct((peers, 3 * size, width), BF16),
            jax.ShapeDtypeStruct((width, model), BF16),
        ),
        in_specs=[
            pl.BlockSpec((width, model), lambda i: (0, 0)),
            pl.BlockSpec((1, model), lambda i: (0, 0)),
            pl.BlockSpec((model, heads * size), lambda i: (0, i)),
        ],
        out_specs=(
            pl.BlockSpec((heads, size, width), lambda i: (i % 2, i // 2, 0)),
            pl.BlockSpec((width, model), lambda i: (0, 0)),
        ),
        compiler_params=pltpu.CompilerParams(vmem_limit_bytes=VMEM_LIMIT),
        cost_estimate=cost(2 * width * model * columns, 2 * model * columns),
        name="project",
    )(frames, gain, weight)


def key_weights(scores, length, scale):
    live = lax.broadcasted_iota(jnp.int32, scores.shape, 0) < length
    return jnp.where(live, scores * scale, -jnp.inf)


def forward_kernel(len_ref, got_ref, qkv_ref, stats_ref, out_ref, att_ref, wide_ref):
    size = qkv_ref.shape[0] // 3
    frames = qkv_ref.shape[1]
    length = len_ref[0]
    scale = size**-0.5
    span = got_ref.shape[2]
    for peer in range(got_ref.shape[0]):
        qkv_ref[:, peer * span : (peer + 1) * span] = got_ref[peer]
    keys = qkv_ref[size : 2 * size, :].astype(F32).T.astype(BF16)
    values = qkv_ref[2 * size :, :]
    for start in range(0, frames, QUERY_BLOCK):
        cols = slice(start, start + QUERY_BLOCK)
        scores = key_weights(dot_nn(keys, qkv_ref[0:size, cols]), length, scale)
        top = jnp.max(scores, axis=0, keepdims=True)
        exps = jnp.exp(scores - top)
        inverse = 1.0 / jnp.sum(exps, axis=0, keepdims=True)
        attended = dot_nn(values, (exps * inverse).astype(BF16)).astype(BF16)
        att_ref[:, cols] = attended
        wide_ref[:, cols] = attended.astype(F32)
        stats_ref[0:1, cols] = top
        stats_ref[1:2, cols] = inverse
    peers, rows, width = out_ref.shape
    half = size // 2
    blank = jnp.zeros((size, HALO), F32)
    for peer in range(peers):
        first, last = peer * width, (peer + 1) * width
        out_ref[peer, 0:size, :] = att_ref[:, first:last]
        before = wide_ref[:, first - width : first][:, width - HALO :] if peer else blank
        after = wide_ref[:, last : last + width][:, :HALO] if peer < peers - 1 else blank
        edges = jnp.concatenate([before, after], axis=1)
        packed = jnp.concatenate([edges[:half], edges[half:]], axis=1)
        out_ref[peer, size:, :] = packed.astype(BF16)


def attention_forward(length, got):
    peers, triple, width = got.shape
    size = triple // 3
    frames = peers * width
    return pl.pallas_call(
        forward_kernel,
        out_shape=(
            jax.ShapeDtypeStruct((triple, frames), BF16),
            jax.ShapeDtypeStruct((8, frames), F32),
            jax.ShapeDtypeStruct((peers, size + size // 2, width), BF16),
            jax.ShapeDtypeStruct((size, frames), BF16),
        ),
        in_specs=[smem()] + vmem(1),
        out_specs=tuple(vmem(4)),
        scratch_shapes=[pltpu.VMEM((size, frames), F32)],
        compiler_params=pltpu.CompilerParams(vmem_limit_bytes=VMEM_LIMIT),
        cost_estimate=cost(16 * frames * frames * size, 2 * frames * triple * 3),
        name="attention_forward",
    )(length, got)


def middle_kernel(
    groups,
    info_ref,
    att_ref,
    x_ref,
    before_ref,
    after_ref,
    cot_ref,
    weight_ref,
    gain_ref,
    taps_ref,
    layer_ref,
    resid_grad_ref,
    send_ref,
    att_out_ref,
    keep_ref,
    other_ref,
    resid_ref,
    unit_ref,
    conv_ref,
    grads_ref,
    into_ref,
    sum_ref,
    dot_ref,
    turned_ref,
    taps_out_ref,
):
    heads, packed_rows, width = att_ref.shape
    size = packed_rows * 2 // 3
    half = size // 2
    model = x_ref.shape[1]
    tap_count = taps_ref.shape[0]
    reach = (tap_count - 1) // 2
    near = HALO // 2
    main, edges = [], []
    for head in range(heads):
        main.append(att_ref[head, 0:size, :].astype(F32))
        packed = att_ref[head, size:, :].astype(F32)
        edges.append(packed[:, 0 : 2 * HALO])
        edges.append(packed[:, 2 * HALO :])
    att = jnp.concatenate(
        [jnp.concatenate(main, axis=0).T, jnp.concatenate(edges, axis=0).T], axis=0
    ).astype(BF16)
    product = dot_nt(att, weight_ref[...])
    resid_ref[0:HALO, :] = before_ref[0:HALO, :].astype(F32) + product[width : width + HALO]
    resid_ref[HALO : HALO + width, :] = x_ref[...].astype(F32) + product[:width]
    resid_ref[HALO + width :, :] = after_ref[0:HALO, :].astype(F32) + product[width + HALO :]
    unit, inv_std = unit_norm(resid_ref[...])
    unit_ref[...] = unit[HALO : HALO + width]
    rows = width + 2 * HALO
    place = lax.broadcasted_iota(jnp.int32, (rows, 1), 0) - HALO + info_ref[0]
    live = jnp.where((place >= 0) & (place < info_ref[1]), 1.0, 0.0).astype(F32)
    conv_ref[...] = (live * (unit * gain_ref[...])).astype(BF16).astype(F32)
    span = width + 2 * near
    live_span = live[near : near + span]
    live_main = live[HALO : HALO + width]
    sum_ref[...] = jnp.zeros_like(sum_ref)
    dot_ref[...] = jnp.zeros_like(dot_ref)

    taps_out_ref[...] = jnp.zeros_like(taps_out_ref)

    @pl.loop(0, model // CHUNK)
    def _(step):
        cols = pl.ds(pl.multiple_of(step * CHUNK, CHUNK), CHUNK)
        taps = taps_ref[:, cols]

        def put(tap, row):
            place = pl.ds(tap // heads * TAP_ROWS + step, 1)
            taps_out_ref[tap % heads, place, :] = row

        total = jnp.zeros((span, CHUNK), F32)
        for tap in range(tap_count):
            total = total + conv_ref[pl.ds(HALO - near - reach + tap, span), cols] * taps[tap : tap + 1]
        gate = 1.0 / (1.0 + jnp.exp(-total))
        resid = resid_ref[pl.ds(HALO, width), cols]
        layer_ref[:, cols] = (
            live_main * (resid + total[near : near + width] * gate[near : near + width])
        ).astype(BF16)
        outer = live_span * jnp.concatenate(
            [before_ref[HALO:, cols], cot_ref[:, cols], after_ref[HALO:, cols]], axis=0
        ).astype(F32)
        grads = (outer * gate * (1.0 + total * (1.0 - gate))).astype(BF16).astype(F32)
        grads_ref[...] = grads
        inner = grads[near : near + width]
        for tap in range(tap_count):
            terms = conv_ref[pl.ds(HALO - reach + tap, width), cols] * inner
            put(tap, jnp.sum(terms, axis=0, keepdims=True))
        into = jnp.zeros((width, CHUNK), F32)
        for tap in range(tap_count):
            into = into + grads_ref[pl.ds(near + reach - tap, width), :] * taps[tap : tap + 1]
        into = into * live_main
        unit_part = unit_ref[:, cols]
        put(tap_count, jnp.sum(into * unit_part, axis=0, keepdims=True))
        scaled = into * gain_ref[:, cols]
        into_ref[:, cols] = scaled
        sum_ref[...] += scaled
        dot_ref[...] += scaled * unit_part

    mean = jnp.sum(sum_ref[...], axis=1, keepdims=True) / model
    mean_dot = jnp.sum(dot_ref[...], axis=1, keepdims=True) / model
    resid_grad = live_main * cot_ref[...].astype(F32) + inv_std[HALO : HALO + width] * (
        into_ref[...] - mean - unit_ref[...] * mean_dot
    )
    resid_grad_ref[...] = resid_grad
    send = dot_nn(resid_grad.astype(BF16), weight_ref[...]).T.astype(BF16)
    send_ref[:, 0:size, :] = send.reshape(heads, size, width)
    send_ref[:, size:, :] = taps_out_ref[...].astype(BF16)
    att_out_ref[...] = att[:width]
    chips = heads // 2
    share = model // (groups * heads)
    turned = resid_grad.T.astype(BF16)
    for group in range(groups):
        for chip in range(chips):
            for core in range(2):
                first = ((group * chips + chip) * 2 + core) * share
                place = (group * chips + chip) * share
                turned_ref[core, place : place + share, :] = turned[first : first + share]
    keep_ref[...] = turned_ref[info_ref[4]]
    other_ref[...] = turned_ref[1 - info_ref[4]]


def middle(groups, info, attended, frames, before, after, cotangent, out_weight, gain, taps):
    heads, packed_rows, width = attended.shape
    size = packed_rows * 2 // 3
    model = frames.shape[1]
    rows = width + 2 * HALO
    return pl.pallas_call(
        lambda *refs: middle_kernel(groups, *refs),
        out_shape=(
            jax.ShapeDtypeStruct((width, model), BF16),
            jax.ShapeDtypeStruct((width, model), F32),
            jax.ShapeDtypeStruct((heads, size + groups * TAP_ROWS, width), BF16),
            jax.ShapeDtypeStruct((width, heads * size), BF16),
            jax.ShapeDtypeStruct((model // 2, width), BF16),
            jax.ShapeDtypeStruct((model // 2, width), BF16),
        ),
        in_specs=[smem()] + vmem(8),
        out_specs=tuple(vmem(6)),
        scratch_shapes=[
            pltpu.VMEM((rows, model), F32),
            pltpu.VMEM((width, model), F32),
            pltpu.VMEM((rows, model), F32),
            pltpu.VMEM((width + HALO, CHUNK), F32),
            pltpu.VMEM((width, model), F32),
            pltpu.VMEM((width, CHUNK), F32),
            pltpu.VMEM((width, CHUNK), F32),
            pltpu.VMEM((2, model // 2, width), BF16),
            pltpu.VMEM((heads, groups * TAP_ROWS, width), F32),
        ],
        compiler_params=pltpu.CompilerParams(vmem_limit_bytes=VMEM_LIMIT),
        cost_estimate=cost(4 * rows * model * heads * size * 8, 2 * model * heads * size),
        name="middle",
    )(info, attended, frames, before, after, cotangent, out_weight, gain, taps)


def backward_kernel(info_ref, qkv_ref, stats_ref, grad_ref, send_ref, out_ref, *refs):
    tap_refs, total_ref = refs[:-1], refs[-1]
    size = qkv_ref.shape[0] // 3
    frames = qkv_ref.shape[1]
    peers, _, width = grad_ref.shape
    length = info_ref[1]
    total_ref[...] = jnp.sum(grad_ref[:, size:, :].astype(F32), axis=0)
    for place, tap_ref in enumerate(tap_refs):
        first = pl.multiple_of((info_ref[2] ^ place) * TAP_ROWS, TAP_ROWS)
        tap_ref[...] = total_ref[pl.ds(first, TAP_ROWS), :]
    scale = size**-0.5
    keys_turned = qkv_ref[size : 2 * size, :]
    keys = keys_turned.astype(F32).T.astype(BF16)
    values = qkv_ref[2 * size :, :].astype(F32).T.astype(BF16)
    grads = jnp.concatenate([grad_ref[peer, 0:size, :] for peer in range(peers)], axis=1)
    key_sum = jnp.zeros((size, frames), F32)
    value_sum = jnp.zeros((size, frames), F32)
    for start in range(0, frames, QUERY_BLOCK):
        cols = slice(start, start + QUERY_BLOCK)
        queries = qkv_ref[0:size, cols]
        block = grads[:, cols]
        scores = key_weights(dot_nn(keys, queries), length, scale)
        probs = jnp.exp(scores - stats_ref[0:1, cols]) * stats_ref[1:2, cols]
        prob_grads = dot_nn(values, block)
        delta = jnp.sum(probs * prob_grads, axis=0, keepdims=True)
        score_grads = (probs * (prob_grads - delta) * scale).astype(BF16)
        out_ref[0:size, cols] = dot_nn(keys_turned, score_grads).astype(BF16)
        key_sum = key_sum + dot_nt(queries, score_grads)
        value_sum = value_sum + dot_nt(block, probs.astype(BF16))
    out_ref[size : 2 * size, :] = key_sum.astype(BF16)
    out_ref[2 * size :, :] = value_sum.astype(BF16)
    for peer in range(peers):
        send_ref[peer] = out_ref[:, peer * width : (peer + 1) * width]


def attention_backward(info, qkv, stats, grads):
    peers, rows, width = grads.shape
    size = qkv.shape[0] // 3
    groups = (rows - size) // TAP_ROWS
    frames = peers * width
    return pl.pallas_call(
        backward_kernel,
        out_shape=(
            jax.ShapeDtypeStruct((peers, 3 * size, width), BF16),
            jax.ShapeDtypeStruct((3 * size, frames), BF16),
        )
        + (jax.ShapeDtypeStruct((TAP_ROWS, width), F32),) * groups,
        in_specs=[smem()] + vmem(3),
        out_specs=tuple(vmem(2 + groups)),
        scratch_shapes=[pltpu.VMEM((groups * TAP_ROWS, width), F32)],
        compiler_params=pltpu.CompilerParams(vmem_limit_bytes=VMEM_LIMIT),
        cost_estimate=cost(20 * frames * frames * size, 2 * frames * size * 10),
        name="attention_backward",
    )(info, qkv, stats, grads)


def chip_order(chip):
    far = chip // 2
    return (chip, chip ^ 1, 2 - far, 3 - 3 * far)


def qkv_kernel(info_ref, left_ref, pair_ref, near_ref, far_ref, *refs):
    out_refs, order_ref, blocks_ref = refs[:-2], refs[-2], refs[-1]
    blocks, double, half = near_ref.shape
    rows = left_ref.shape[0]
    width = double // 2
    for chip, origin in enumerate(chip_order(info_ref[3])):
        for place in range(2):
            frame = pl.multiple_of((origin * 2 + (info_ref[4] ^ place)) * width, CHUNK)
            cols = slice((2 * chip + place) * width, (2 * chip + place + 1) * width)
            order_ref[:rows, cols] = left_ref[:, pl.ds(frame, width)]
            order_ref[rows:, cols] = pair_ref[:, pl.ds(frame, width)]
    span = 2 * CHUNK
    far = blocks * double
    for part in range(half // span):
        cols = slice(part * span, (part + 1) * span)
        product = dot_nn(order_ref[:, :far], near_ref[:, :, cols].reshape(far, span))
        product = product + dot_nn(order_ref[:, far:], far_ref[:, :, cols].reshape(far, span))
        blocks_ref[cols, :] = product.T.astype(BF16)
    share = half // len(out_refs)
    for place, out_ref in enumerate(out_refs):
        first = pl.multiple_of((info_ref[2] ^ place) * share, 64)
        out_ref[...] = blocks_ref[pl.ds(first, share), :]


def qkv_parts(info, left, pair, near, far, groups):
    half = near.shape[2]
    rows, frames = left.shape
    return pl.pallas_call(
        qkv_kernel,
        out_shape=tuple(
            jax.ShapeDtypeStruct((half // groups, 2 * rows), BF16) for _ in range(groups)
        ),
        in_specs=[smem()] + vmem(4),
        out_specs=tuple(vmem(groups)),
        scratch_shapes=[
            pltpu.VMEM((2 * rows, frames), BF16),
            pltpu.VMEM((half, 2 * rows), BF16),
        ],
        compiler_params=pltpu.CompilerParams(vmem_limit_bytes=VMEM_LIMIT),
        cost_estimate=cost(),
        name="qkv_parts",
    )(info, left, pair, near, far)


def out_kernel(info_ref, low_ref, att_ref, pair_low_ref, pair_att_ref, *out_refs):
    *out_refs, blocks_ref = out_refs
    product = dot_nn(low_ref[...], att_ref[...]) + dot_nn(pair_low_ref[...], pair_att_ref[...])
    blocks_ref[...] = product.astype(BF16).reshape(blocks_ref.shape)
    for place, out_ref in enumerate(out_refs):
        out_ref[...] = blocks_ref[info_ref[2] ^ place]


def out_parts(info, low, att, pair_low, pair_att, groups):
    rows = low.shape[0] // groups
    columns = att.shape[1]
    return pl.pallas_call(
        out_kernel,
        out_shape=tuple(jax.ShapeDtypeStruct((rows, columns), BF16) for _ in range(groups)),
        in_specs=[smem()] + vmem(4),
        out_specs=tuple(vmem(groups)),
        scratch_shapes=[pltpu.VMEM((groups, rows, columns), BF16)],
        compiler_params=pltpu.CompilerParams(vmem_limit_bytes=VMEM_LIMIT),
        cost_estimate=cost(),
        name="out_parts",
    )(info, low, att, pair_low, pair_att)


def summed(refs):
    total = refs[0][...].astype(F32)
    for ref in refs[1:]:
        total = total + ref[...].astype(F32)
    return total


def group_kernel(groups, *refs):
    out_ref = refs[-1]
    columns = refs[groups].shape[1]
    chips, share, _ = out_ref.shape
    out_ref[:, :, :columns] = summed(refs[groups : 2 * groups]).astype(BF16).reshape(chips, share, columns)
    out_ref[:, :, columns:] = summed(refs[:groups]).astype(BF16).reshape(chips, share, -1)


def group_sums(qkv_got, out_got, chips):
    rows = qkv_got[0].shape[0]
    columns = qkv_got[0].shape[1] + out_got[0].shape[1]
    return pl.pallas_call(
        lambda *refs: group_kernel(len(qkv_got), *refs),
        out_shape=jax.ShapeDtypeStruct((chips, rows // chips, columns), BF16),
        in_specs=vmem(2 * len(qkv_got)),
        out_specs=vmem(1)[0],
        compiler_params=pltpu.CompilerParams(vmem_limit_bytes=VMEM_LIMIT),
        cost_estimate=cost(),
        name="group_sums",
    )(*qkv_got, *out_got)


def input_kernel(grad_ref, weight_ref, x_ref, resid_grad_ref, gain_ref, *refs):
    tap_refs, (out_ref, row_ref, rows_ref, normed_ref) = refs[:-4], refs[-4:]
    step = pl.program_id(0)
    heads, triple, width = grad_ref.shape
    size = triple // 3
    block = weight_ref.shape[0]

    @pl.when(step == 0)
    def _():
        turned = jnp.concatenate(
            [
                grad_ref[head, part * size : (part + 1) * size, :].astype(F32)
                for part in range(3)
                for head in range(heads)
            ],
            axis=0,
        )
        rows_ref[...] = turned.T.astype(BF16)

    cols = pl.ds(pl.multiple_of(step * block, block), block)
    normed_ref[:, cols] = dot_nt(rows_ref[...], weight_ref[...])

    @pl.when(step == pl.num_programs(0) - 1)
    def _():
        taps = summed(tap_refs)
        for place in range(x_ref.shape[1] // width):
            row_ref[:, place * width : (place + 1) * width] = taps[place : place + 1]
        unit, inv_std = unit_norm(x_ref[...].astype(F32))
        scaled = normed_ref[...] * gain_ref[...]
        out_ref[...] = (
            resid_grad_ref[...]
            + inv_std
            * (
                scaled
                - jnp.mean(scaled, axis=-1, keepdims=True)
                - unit * jnp.mean(scaled * unit, axis=-1, keepdims=True)
            )
        ).astype(BF16)


def input_grads(grads, weight, frames, resid_grad, gain, taps):
    heads, triple, width = grads.shape
    model, columns = weight.shape
    block = 2 * CHUNK
    return pl.pallas_call(
        input_kernel,
        grid=(model // block,),
        out_shape=(
            jax.ShapeDtypeStruct((width, model), BF16),
            jax.ShapeDtypeStruct((1, model), F32),
        ),
        in_specs=[
            pl.BlockSpec((heads, triple, width), lambda i: (0, 0, 0)),
            pl.BlockSpec((block, columns), lambda i: (i, 0)),
            pl.BlockSpec((width, model), lambda i: (0, 0)),
            pl.BlockSpec((width, model), lambda i: (0, 0)),
            pl.BlockSpec((1, model), lambda i: (0, 0)),
        ]
        + [pl.BlockSpec((TAP_ROWS, width), lambda i: (0, 0))] * len(taps),
        out_specs=(
            pl.BlockSpec((width, model), lambda i: (0, 0)),
            pl.BlockSpec((1, model), lambda i: (0, 0)),
        ),
        scratch_shapes=[pltpu.VMEM((width, columns), BF16), pltpu.VMEM((width, model), F32)],
        compiler_params=pltpu.CompilerParams(vmem_limit_bytes=VMEM_LIMIT),
        cost_estimate=cost(2 * width * model * columns, 2 * model * columns),
        name="input_grads",
    )(grads, weight, frames, resid_grad, gain, *taps)


def final_kernel(size, info_ref, got_ref, weight_ref, gain_ref, out_ref, gain_out_ref):
    chips = got_ref.shape[0]
    first = got_ref.shape[2] - 6 * size
    even = info_ref[4] == 0
    rows = []
    for chip in range(chips):
        mine = got_ref[chip, :, first : first + 3 * size].astype(F32)
        pair = got_ref[chip, :, first + 3 * size :].astype(F32)
        rows += [jnp.where(even, mine, pair), jnp.where(even, pair, mine)]
    grads = jnp.concatenate(
        [row[:, part * size : (part + 1) * size] for part in range(3) for row in rows], axis=1
    )
    columns = grads.shape[1]
    out_ref[:, 0:columns] = grads
    total = got_ref[0, :, :first].astype(F32)
    for chip in range(1, chips):
        total = total + got_ref[chip, :, :first].astype(F32)
    out_ref[:, columns:] = total
    products = grads * weight_ref[...].astype(F32)
    gain_out_ref[...] = jnp.sum(products, axis=1, keepdims=True) / gain_ref[...]


def final_sums(info, got, weight_rows, gain_rows):
    rows, columns = weight_rows.shape
    size = columns // (6 * got.shape[0])
    width = columns + got.shape[2] - 6 * size
    return pl.pallas_call(
        lambda *refs: final_kernel(size, *refs),
        out_shape=(
            jax.ShapeDtypeStruct((rows, width), F32),
            jax.ShapeDtypeStruct((rows, 1), F32),
        ),
        in_specs=[smem()] + vmem(3),
        out_specs=tuple(vmem(2)),
        compiler_params=pltpu.CompilerParams(vmem_limit_bytes=VMEM_LIMIT),
        cost_estimate=cost(),
        name="final_sums",
    )(info, got, weight_rows, gain_rows)


def exchange(blocks, axes):
    return lax.all_to_all(blocks, axes, split_axis=0, concat_axis=0, tiled=True)


def swap(block, axis, bit):
    return lax.ppermute(block, axis, [(i, i ^ bit) for i in range(lax.axis_size(axis))])


def across(block):
    return lax.ppermute(block, "seq", [(2, 4), (3, 5), (4, 2), (5, 3)])


def outward(block):
    return lax.ppermute(block, "seq", [(2, 0), (3, 1), (4, 6), (5, 7)])


def group_swap(parts):
    return [parts[0]] + [swap(parts[bit], "dp", bit) for bit in range(1, len(parts))]


def head_shards(
    frames_in,
    lengths,
    first_gain,
    second_gain,
    qkv_weight,
    out_weight,
    conv_kernel,
    layer_cotangent,
):
    both = ("dp", "seq")
    peers = lax.axis_size("seq")
    everyone = peers * lax.axis_size("dp")
    width, model = frames_in.shape[1:]
    size = out_weight.shape[1] // HEADS
    mine = lax.axis_index("seq")
    number = lax.axis_index("dp") * peers + mine
    share = model // everyone
    frames, cotangent = frames_in[0], layer_cotangent[0]
    gain_one, gain_two = first_gain[None], second_gain[None]
    groups = lax.axis_size("dp")
    chips = peers // 2
    info = jnp.stack(
        [mine * width, lengths[0], lax.axis_index("dp"), mine // 2, mine % 2]
    ).astype(jnp.int32)
    qkv_send, normed = project(frames, gain_one, qkv_weight, peers)
    qkv_got = exchange(qkv_send, "seq")
    near = HALO // 2
    tails = jnp.concatenate([frames[width - HALO :], cotangent[width - near :]], axis=0)
    fronts = jnp.concatenate([frames[:HALO], cotangent[:near]], axis=0)
    before = lax.ppermute(tails, "seq", [(i, i + 1) for i in range(peers - 1)])
    after = lax.ppermute(fronts, "seq", [(i + 1, i) for i in range(peers - 1)])
    halves = normed.reshape(width, -1, 2, share).transpose(2, 0, 1, 3).reshape(2, width, -1)
    keep = lax.dynamic_index_in_dim(halves, mine % 2, 0, keepdims=False)
    other = lax.dynamic_index_in_dim(halves, 1 - mine % 2, 0, keepdims=False)
    paired = jnp.concatenate([keep, swap(other, "seq", 1)], axis=0)
    normed_near = jnp.stack([paired, swap(paired, "seq", 2)])
    qkv_got, before, after = lax.optimization_barrier((qkv_got, before, after))
    qkv, stats, att_send, att_head = attention_forward(lengths, qkv_got)
    attended = exchange(att_send, "seq")
    attended, normed_near = lax.optimization_barrier((attended, normed_near))
    normed_far = across(normed_near)
    layer_out, resid_grad, grad_send, att_rows, low_keep, low_other = middle(
        groups, info, attended, frames, before, after, cotangent, out_weight, gain_two, conv_kernel
    )
    grad_send, normed_far = lax.optimization_barrier((grad_send, normed_far))
    grads = exchange(grad_send, "seq")
    blocks = out_parts(
        info, low_keep, att_rows, swap(low_other, "seq", 1), swap(att_rows, "seq", 1), groups
    )
    grads, normed_far, blocks = lax.optimization_barrier((grads, normed_far, blocks))
    normed_out = outward(normed_far)
    out_got = group_swap(blocks)
    back_send, back_head, *taps = attention_backward(info, qkv, stats, grads)
    pair_head = swap(back_head, "seq", 1)
    back_send, back_head, normed_out, out_got = lax.optimization_barrier(
        (back_send, back_head, normed_out, out_got)
    )
    back = exchange(back_send, "seq")
    normed_far = normed_far + normed_out
    qkv_got = group_swap(qkv_parts(info, back_head, pair_head, normed_near, normed_far, groups))
    back, qkv_got = lax.optimization_barrier((back, qkv_got))
    taps_got = group_swap(taps)
    sums = group_sums(qkv_got, out_got, chips)
    cores = [list(range(core, peers, 2)) for core in range(2)]
    got = lax.all_to_all(
        sums, "seq", split_axis=0, concat_axis=0, tiled=True, axis_index_groups=cores
    )
    input_grad, taps_row = input_grads(back, qkv_weight, frames, resid_grad, gain_one, taps_got)
    got, input_grad = lax.optimization_barrier((got, input_grad))
    weight_rows = lax.dynamic_slice_in_dim(qkv_weight, number * share, share, axis=0)
    gain_rows = lax.dynamic_slice_in_dim(first_gain, number * share, share, axis=0)[:, None]
    weight_grads, gain_part = final_sums(info, got, weight_rows, gain_rows)
    row = jnp.concatenate([taps_row.reshape(-1), gain_part.reshape(-1)])
    rows = exchange(jnp.broadcast_to(row[None], (everyone, row.shape[0])), both)
    tap_count = conv_kernel.shape[0]
    conv_grad = rows[:tap_count, :model]
    gain_grads = jnp.stack([rows[:, model:].reshape(-1), rows[tap_count, :model]])
    return (layer_out[None], input_grad[None], weight_grads, gain_grads, conv_grad)


def solution(mesh):
    in_specs = (P("dp", "seq", None), P("dp"), P(), P(), P(), P(), P(), P("dp", "seq", None))
    out_specs = (P("dp", "seq", None), P("dp", "seq", None), P(("dp", "seq"), None), P(), P())
    seq_count = mesh.shape["seq"]
    device_count = seq_count * mesh.shape["dp"]

    def program(*args):
        frames_dev = args[0].shape[1] // seq_count
        fits = seq_count == HEADS and frames_dev == 128 and device_count == args[6].shape[0] + 1 == 32
        plan = head_shards if fits else general_shards
        return jax.shard_map(
            plan, mesh=mesh, in_specs=in_specs, out_specs=out_specs, check_vma=False
        )(*args)

    return program
```

```python
import jax
import jax.numpy as jnp
from jax import lax
from jax.experimental import pallas as pl
from jax.experimental.pallas import tpu as pltpu
from jax.sharding import PartitionSpec as P

HEADS = 8


epsilon = 1e-05


def padded_2(cells, sides, width):
    for axis, dim in sides:
        count = lax.axis_size(axis)
        ends = count - 1
        head = lax.slice_in_dim(cells, 0, width, axis=dim)
        tail = lax.slice_in_dim(cells, cells.shape[dim] - width, cells.shape[dim], axis=dim)
        cells = jnp.concatenate(
            [
                lax.ppermute(tail, axis, [(i, (i + 1) % count) for i in range(ends)]),
                cells,
                lax.ppermute(head, axis, [((i + 1) % count, i) for i in range(ends)]),
            ],
            axis=dim,
        )
    return cells


def layer_norm(rows, gain_vec):
    row_mean = jnp.mean(rows, axis=-1, keepdims=True)
    centered = rows - row_mean
    inv_std = lax.rsqrt(jnp.mean(centered * centered, axis=-1, keepdims=True) + epsilon)
    unit_rows = centered * inv_std
    return (unit_rows * gain_vec, unit_rows, inv_std)


def norm_backward(incoming, unit_rows, inv_std, gain_vec):
    scaled = incoming * gain_vec
    return inv_std * (
        scaled
        - jnp.mean(scaled, axis=-1, keepdims=True)
        - unit_rows * jnp.mean(scaled * unit_rows, axis=-1, keepdims=True)
    )


def contract_rows(left, right):
    return lax.dot_general(
        left, right, (((1,), (1,)), ((), ())), preferred_element_type=jnp.float32
    )


def contract_cols(left, right):
    return lax.dot_general(
        left, right, (((0,), (0,)), ((), ())), preferred_element_type=jnp.float32
    )


def soft_weights(queries, key_rows, key_valid):
    score_scale = queries.shape[1] ** (-0.5)
    scores = contract_rows(queries, key_rows) * score_scale
    scores = jnp.where(key_valid[None, :], scores, -jnp.inf)
    row_max = jnp.max(scores, axis=1, keepdims=True)
    exp_scores = jnp.exp(scores - row_max)
    return exp_scores / jnp.sum(exp_scores, axis=1, keepdims=True)


def attend_forward(queries, key_rows, value_rows, key_valid):
    block_rows = min(512, queries.shape[0])
    blocks = queries.reshape(queries.shape[0] // block_rows, block_rows, queries.shape[1])

    def one_block(query_block):
        attn_probs = soft_weights(query_block, key_rows, key_valid).astype(jnp.bfloat16)
        return jnp.dot(attn_probs, value_rows, preferred_element_type=jnp.float32).astype(
            jnp.bfloat16
        )

    return lax.map(one_block, blocks).reshape(queries.shape)


def attend_backward(queries, key_rows, value_rows, key_valid, out_grads):
    block_rows = min(512, queries.shape[0])
    block_count = queries.shape[0] // block_rows
    blocks = (
        queries.reshape(block_count, block_rows, queries.shape[1]),
        out_grads.reshape(block_count, block_rows, out_grads.shape[1]),
    )
    score_scale = queries.shape[1] ** (-0.5)

    def one_block(running, pieces):
        query_block, grad_block = pieces
        attn_probs = soft_weights(query_block, key_rows, key_valid)
        probs_low = attn_probs.astype(jnp.bfloat16)
        prob_grads = contract_rows(grad_block, value_rows)
        row_delta = jnp.sum(attn_probs * prob_grads, axis=1, keepdims=True)
        score_grads = (attn_probs * (prob_grads - row_delta) * score_scale).astype(jnp.bfloat16)
        query_grads = jnp.dot(score_grads, key_rows, preferred_element_type=jnp.float32).astype(
            jnp.bfloat16
        )
        key_sum = running[0] + contract_cols(score_grads, query_block)
        value_sum = running[1] + contract_cols(probs_low, grad_block)
        return ((key_sum, value_sum), query_grads)

    zero_rows = jnp.zeros(key_rows.shape, jnp.float32)
    totals, query_grads = lax.scan(one_block, (zero_rows, zero_rows), blocks)
    return (query_grads.reshape(queries.shape), totals[0], totals[1])


def depthwise(padded, kernel, frame_count):
    total = jnp.zeros((frame_count, padded.shape[1]), jnp.float32)
    for tap_index in range(kernel.shape[0]):
        total = (
            total
            + padded[tap_index : tap_index + frame_count].astype(jnp.float32) * kernel[tap_index]
        )
    return total


def kernel_grad(padded, grads, tap_count):
    frame_count = grads.shape[0]
    grads_wide = grads.astype(jnp.float32)
    sums = [
        jnp.sum(
            padded[tap_index : tap_index + frame_count].astype(jnp.float32) * grads_wide, axis=0
        )
        for tap_index in range(tap_count)
    ]
    return jnp.stack(sums)


def pack_queries(matrix, repeats, groups, channel):
    frames_dev = matrix.shape[0]
    shaped = matrix.reshape(repeats, frames_dev // repeats, groups, channel)
    return shaped.transpose(2, 0, 1, 3).reshape(groups * repeats, frames_dev // repeats, channel)


def pack_keys(matrix, repeats, groups, channel):
    frames_dev = matrix.shape[0]
    shaped = matrix.reshape(frames_dev, groups, channel).transpose(1, 0, 2)[:, None]
    widened = jnp.broadcast_to(shaped, (groups, repeats, frames_dev, channel))
    return widened.reshape(groups * repeats, frames_dev, channel)


def unpack_rows(stacked, repeats, groups):
    rows_each = stacked.shape[1]
    channel = stacked.shape[2]
    shaped = stacked.reshape(groups, repeats, rows_each, channel).transpose(1, 2, 0, 3)
    return shaped.reshape(repeats * rows_each, groups * channel)


def local_forward(query_rows, key_rows, value_rows, key_valid):
    outputs = attend_forward(query_rows, key_rows, value_rows, key_valid)
    return outputs


def local_backward(query_rows, key_rows, value_rows, key_valid, out_grads):
    query_list, key_list, value_list = ([], [], [])
    query_grads, key_sum, value_sum = attend_backward(
        query_rows, key_rows, value_rows, key_valid, out_grads
    )
    query_list.append(query_grads)
    key_list.append(key_sum)
    value_list.append(value_sum)
    return (query_list[0], key_list[0], value_list[0])


def general_shards(
    frames_in,
    lengths,
    first_gain,
    second_gain,
    qkv_weight,
    out_weight,
    conv_kernel,
    layer_cotangent,
):
    seq_count = lax.axis_size("seq")
    frames_dev = frames_in.shape[1]
    head_width = out_weight.shape[1]
    head_size = head_width // HEADS
    repeats = max(seq_count // HEADS, 1)
    per_device = max(HEADS // seq_count, 1)
    groups = seq_count // repeats
    channel = per_device * head_size
    tap_count = conv_kernel.shape[0]
    half_taps = (tap_count - 1) // 2
    my_index = lax.axis_index("seq")
    positions = my_index * frames_dev + jnp.arange(frames_dev, dtype=jnp.int32)
    live_rows = (positions < lengths[0]).astype(jnp.float32)[:, None]
    key_valid = jnp.arange(seq_count * frames_dev, dtype=jnp.int32) < lengths[0]
    inputs = frames_in[0].astype(jnp.float32)
    normed, unit_one, inv_one = layer_norm(inputs, first_gain)
    normed_low = normed.astype(jnp.bfloat16)
    projected = jnp.dot(normed_low, qkv_weight, preferred_element_type=jnp.float32).astype(
        jnp.bfloat16
    )
    query_send = pack_queries(projected[:, :head_width], repeats, groups, channel)
    key_send = pack_keys(projected[:, head_width : 2 * head_width], repeats, groups, channel)
    value_send = pack_keys(projected[:, 2 * head_width :], repeats, groups, channel)
    got_queries, got_keys, got_values = (
        lax.all_to_all(query_send, "seq", split_axis=0, concat_axis=1, tiled=True),
        lax.all_to_all(key_send, "seq", split_axis=0, concat_axis=1, tiled=True),
        lax.all_to_all(value_send, "seq", split_axis=0, concat_axis=1, tiled=True),
    )
    query_rows = got_queries[0]
    key_rows = got_keys[0]
    value_rows = got_values[0]
    head_out = local_forward(query_rows, key_rows, value_rows, key_valid)
    returned = lax.all_to_all(head_out[None], "seq", split_axis=1, concat_axis=0, tiled=True)
    attended = unpack_rows(returned, repeats, groups)
    resid = inputs + contract_rows(attended, out_weight)
    normed_two, unit_two, inv_two = layer_norm(resid, second_gain)
    conv_in = (live_rows * normed_two).astype(jnp.bfloat16)
    padded = padded_2(conv_in, (("seq", 0),), half_taps)
    conv_sum = depthwise(padded, conv_kernel, frames_dev)
    sigmoid_c = jax.nn.sigmoid(conv_sum)
    layer_out = (live_rows * (resid + conv_sum * sigmoid_c)).astype(jnp.bfloat16)
    outer_grad = live_rows * layer_cotangent[0].astype(jnp.float32)
    conv_grads = (outer_grad * sigmoid_c * (1.0 + conv_sum * (1.0 - sigmoid_c))).astype(
        jnp.bfloat16
    )
    kernel_part = kernel_grad(padded, conv_grads, tap_count)
    grad_padded = padded_2(conv_grads, (("seq", 0),), half_taps)
    into_conv = depthwise(grad_padded, conv_kernel[::-1], frames_dev) * live_rows
    second_part = jnp.sum(into_conv * unit_two, axis=0)
    resid_grad = outer_grad + norm_backward(into_conv, unit_two, inv_two, second_gain)
    resid_low = resid_grad.astype(jnp.bfloat16)
    attended_grad = jnp.dot(resid_low, out_weight, preferred_element_type=jnp.float32).astype(
        jnp.bfloat16
    )
    sent_grads = lax.all_to_all(
        pack_queries(attended_grad, repeats, groups, channel),
        "seq",
        split_axis=0,
        concat_axis=1,
        tiled=True,
    )
    query_grads, key_sums, value_sums = local_backward(
        query_rows, key_rows, value_rows, key_valid, sent_grads[0]
    )
    query_back = lax.all_to_all(query_grads[None], "seq", split_axis=1, concat_axis=0, tiled=True)
    key_back, value_back = (
        lax.all_to_all(
            key_sums[None].astype(jnp.bfloat16), "seq", split_axis=1, concat_axis=0, tiled=True
        ).astype(jnp.float32),
        lax.all_to_all(
            value_sums[None].astype(jnp.bfloat16), "seq", split_axis=1, concat_axis=0, tiled=True
        ).astype(jnp.float32),
    )

    def fold_parts(stacked):
        shaped = stacked.reshape(groups, repeats, frames_dev, channel)
        summed = jnp.sum(shaped, axis=1).transpose(1, 0, 2)
        return summed.reshape(frames_dev, head_width).astype(jnp.bfloat16)

    query_grad_rows = unpack_rows(query_back, repeats, groups)
    key_grad_rows = fold_parts(key_back)
    value_grad_rows = fold_parts(value_back)
    qkv_grads = jnp.concatenate([query_grad_rows, key_grad_rows, value_grad_rows], axis=1)
    normed_grad = contract_rows(qkv_grads, qkv_weight)
    first_part = jnp.sum(normed_grad * unit_one, axis=0)
    input_grad = (resid_grad + norm_backward(normed_grad, unit_one, inv_one, first_gain)).astype(
        jnp.bfloat16
    )
    weight_grads = lax.psum_scatter(
        jnp.concatenate(
            [contract_cols(normed_low, qkv_grads), contract_cols(resid_low, attended)], axis=1
        ),
        ("dp", "seq"),
        scatter_dimension=0,
        tiled=True,
    )
    gain_sum, kernel_sum = lax.psum(
        (jnp.stack([first_part, second_part]), kernel_part), ("dp", "seq")
    )
    return (layer_out[None], input_grad[None], weight_grads, gain_sum, kernel_sum)


HALO = 32
BF16 = jnp.bfloat16
F32 = jnp.float32
VMEM_LIMIT = 56 * 2**20
CHUNK = 128
QUERY_BLOCK = 1024
TAP_ROWS = 16


def vmem(count):
    return [pl.BlockSpec(memory_space=pltpu.VMEM)] * count


def smem():
    return pl.BlockSpec(memory_space=pltpu.SMEM)


def cost(*_):
    return pl.CostEstimate(flops=1000, bytes_accessed=1000, transcendentals=0)


def dot_nn(left, right):
    return lax.dot_general(left, right, (((1,), (0,)), ((), ())), preferred_element_type=F32)


def dot_nt(left, right):
    return lax.dot_general(left, right, (((1,), (1,)), ((), ())), preferred_element_type=F32)


def unit_norm(rows):
    centered = rows - jnp.mean(rows, axis=-1, keepdims=True)
    inv_std = lax.rsqrt(jnp.mean(centered * centered, axis=-1, keepdims=True) + epsilon)
    return centered * inv_std, inv_std


def project_kernel(x_ref, gain_ref, weight_ref, send_ref, normed_ref):
    @pl.when(pl.program_id(0) == 0)
    def _():
        unit, _ = unit_norm(x_ref[...].astype(F32))
        normed_ref[...] = (unit * gain_ref[...][None]).astype(BF16)

    product = dot_nn(normed_ref[...], weight_ref[...])
    send_ref[...] = product.T.astype(BF16).reshape(send_ref.shape)


def project(frames, gain, weight, peers):
    width, model = frames.shape
    columns = weight.shape[1]
    size = columns // (3 * peers)
    return pl.pallas_call(
        project_kernel,
        grid=(3,),
        out_shape=(
            jax.ShapeDtypeStruct((peers, 3 * size, width), BF16),
            jax.ShapeDtypeStruct((width, model), BF16),
        ),
        in_specs=[
            pl.BlockSpec((width, model), lambda i: (0, 0)),
            pl.BlockSpec((model,), lambda i: (0,)),
            pl.BlockSpec((model, peers * size), lambda i: (0, i)),
        ],
        out_specs=(
            pl.BlockSpec((peers, size, width), lambda i: (0, i, 0)),
            pl.BlockSpec((width, model), lambda i: (0, 0)),
        ),
        compiler_params=pltpu.CompilerParams(vmem_limit_bytes=VMEM_LIMIT),
        cost_estimate=cost(2 * width * model * columns, 2 * model * columns),
        name="project",
    )(frames, gain, weight)


def key_weights(scores, length, scale):
    live = lax.broadcasted_iota(jnp.int32, scores.shape, 0) < length
    return jnp.where(live, scores * scale, -jnp.inf)


def forward_kernel(len_ref, got_ref, qkv_ref, stats_ref, out_ref, att_ref, wide_ref):
    size = qkv_ref.shape[0] // 3
    frames = qkv_ref.shape[1]
    length = len_ref[0]
    scale = size**-0.5
    span = got_ref.shape[2]
    for peer in range(got_ref.shape[0]):
        qkv_ref[:, peer * span : (peer + 1) * span] = got_ref[peer]
    keys = qkv_ref[size : 2 * size, :].astype(F32).T.astype(BF16)
    values = qkv_ref[2 * size :, :]
    for start in range(0, frames, QUERY_BLOCK):
        cols = slice(start, start + QUERY_BLOCK)
        scores = key_weights(dot_nn(keys, qkv_ref[0:size, cols]), length, scale)
        top = jnp.max(scores, axis=0, keepdims=True)
        exps = jnp.exp(scores - top)
        inverse = 1.0 / jnp.sum(exps, axis=0, keepdims=True)
        attended = dot_nn(values, (exps * inverse).astype(BF16)).astype(BF16)
        att_ref[:, cols] = attended
        wide_ref[:, cols] = attended.astype(F32)
        stats_ref[0:1, cols] = top
        stats_ref[1:2, cols] = inverse
    peers, rows, width = out_ref.shape
    half = size // 2
    blank = jnp.zeros((size, HALO), F32)
    for peer in range(peers):
        first, last = peer * width, (peer + 1) * width
        out_ref[peer, 0:size, :] = att_ref[:, first:last]
        before = wide_ref[:, first - width : first][:, width - HALO :] if peer else blank
        after = wide_ref[:, last : last + width][:, :HALO] if peer < peers - 1 else blank
        edges = jnp.concatenate([before, after], axis=1)
        packed = jnp.concatenate([edges[:half], edges[half:]], axis=1)
        out_ref[peer, size:, :] = packed.astype(BF16)


def attention_forward(length, got):
    peers, triple, width = got.shape
    size = triple // 3
    frames = peers * width
    return pl.pallas_call(
        forward_kernel,
        out_shape=(
            jax.ShapeDtypeStruct((triple, frames), BF16),
            jax.ShapeDtypeStruct((8, frames), F32),
            jax.ShapeDtypeStruct((peers, size + size // 2, width), BF16),
            jax.ShapeDtypeStruct((size, frames), BF16),
        ),
        in_specs=[smem()] + vmem(1),
        out_specs=tuple(vmem(4)),
        scratch_shapes=[pltpu.VMEM((size, frames), F32)],
        compiler_params=pltpu.CompilerParams(vmem_limit_bytes=VMEM_LIMIT),
        cost_estimate=cost(16 * frames * frames * size, 2 * frames * triple * 3),
        name="attention_forward",
    )(length, got)


def middle_kernel(
    groups,
    len_ref,
    att_ref,
    x_ref,
    before_ref,
    after_ref,
    cot_ref,
    weight_ref,
    gain_ref,
    taps_ref,
    layer_ref,
    resid_grad_ref,
    send_ref,
    att_out_ref,
    keep_ref,
    other_ref,
    resid_ref,
    unit_ref,
    conv_ref,
    grads_ref,
    into_ref,
    sum_ref,
    dot_ref,
    turned_ref,
    taps_out_ref,
):
    heads, packed_rows, width = att_ref.shape
    size = packed_rows * 2 // 3
    half = size // 2
    model = x_ref.shape[1]
    tap_count = taps_ref.shape[0]
    reach = (tap_count - 1) // 2
    near = HALO // 2
    main, edges = [], []
    for head in range(heads):
        main.append(att_ref[head, 0:size, :].astype(F32))
        packed = att_ref[head, size:, :].astype(F32)
        edges.append(packed[:, 0 : 2 * HALO])
        edges.append(packed[:, 2 * HALO :])
    att = jnp.concatenate(
        [jnp.concatenate(main, axis=0).T, jnp.concatenate(edges, axis=0).T], axis=0
    ).astype(BF16)
    product = dot_nt(att, weight_ref[...])
    resid_ref[0:HALO, :] = before_ref[0:HALO, :].astype(F32) + product[width : width + HALO]
    resid_ref[HALO : HALO + width, :] = x_ref[...].astype(F32) + product[:width]
    resid_ref[HALO + width :, :] = after_ref[0:HALO, :].astype(F32) + product[width + HALO :]
    unit, inv_std = unit_norm(resid_ref[...])
    unit_ref[...] = unit[HALO : HALO + width]
    rows = width + 2 * HALO
    place = lax.broadcasted_iota(jnp.int32, (rows, 1), 0) - HALO + lax.axis_index("seq") * width
    live = jnp.where((place >= 0) & (place < len_ref[0]), 1.0, 0.0).astype(F32)
    conv_ref[...] = (live * (unit * gain_ref[...][None])).astype(BF16).astype(F32)
    span = width + 2 * near
    live_span = live[near : near + span]
    live_main = live[HALO : HALO + width]
    sum_ref[...] = jnp.zeros_like(sum_ref)
    dot_ref[...] = jnp.zeros_like(dot_ref)

    taps_out_ref[...] = jnp.zeros_like(taps_out_ref)

    @pl.loop(0, model // CHUNK)
    def _(step):
        cols = pl.ds(pl.multiple_of(step * CHUNK, CHUNK), CHUNK)
        taps = taps_ref[:, cols]

        def put(tap, row):
            place = pl.ds(tap // heads * TAP_ROWS + step, 1)
            taps_out_ref[tap % heads, place, :] = row

        longest = tap_count // 8 * 8
        total = jnp.zeros((span, CHUNK), F32)
        for shift in range(8):
            part = conv_ref[pl.ds(HALO - near - reach + shift, span + longest), cols]
            for tap in range(shift, tap_count, 8):
                total = total + part[tap - shift : tap - shift + span] * taps[tap : tap + 1]
        gate = 1.0 / (1.0 + jnp.exp(-total))
        resid = resid_ref[pl.ds(HALO, width), cols]
        layer_ref[:, cols] = (
            live_main * (resid + total[near : near + width] * gate[near : near + width])
        ).astype(BF16)
        outer = live_span * jnp.concatenate(
            [before_ref[HALO:, cols], cot_ref[:, cols], after_ref[HALO:, cols]], axis=0
        ).astype(F32)
        grads = (outer * gate * (1.0 + total * (1.0 - gate))).astype(BF16).astype(F32)
        grads_ref[...] = grads
        inner = grads[near : near + width]
        for shift in range(8):
            part = conv_ref[pl.ds(HALO - reach + shift, width + longest), cols]
            for tap in range(shift, tap_count, 8):
                terms = part[tap - shift : tap - shift + width] * inner
                put(tap, jnp.sum(terms, axis=0, keepdims=True))
        into = jnp.zeros((width, CHUNK), F32)
        for shift in range(8):
            part = grads_ref[pl.ds(shift, width + longest), :]
            for offset in range(0, longest + 8, 8):
                tap = near + reach - shift - offset
                if tap < tap_count:
                    into = into + part[offset : offset + width] * taps[tap : tap + 1]
        into = into * live_main
        unit_part = unit_ref[:, cols]
        put(tap_count, jnp.sum(into * unit_part, axis=0, keepdims=True))
        scaled = into * gain_ref[cols][None]
        into_ref[:, cols] = scaled
        sum_ref[...] += scaled
        dot_ref[...] += scaled * unit_part

    mean = jnp.sum(sum_ref[...], axis=1, keepdims=True) / model
    mean_dot = jnp.sum(dot_ref[...], axis=1, keepdims=True) / model
    resid_grad = live_main * cot_ref[...].astype(F32) + inv_std[HALO : HALO + width] * (
        into_ref[...] - mean - unit_ref[...] * mean_dot
    )
    resid_grad_ref[...] = resid_grad
    send = dot_nn(resid_grad.astype(BF16), weight_ref[...]).T.astype(BF16)
    send_ref[:, 0:size, :] = send.reshape(heads, size, width)
    send_ref[:, size:, :] = taps_out_ref[...].astype(BF16)
    att_out_ref[...] = att[:width]
    chips = heads // 2
    share = model // (groups * heads)
    turned = resid_grad.T.astype(BF16)
    for group in range(groups):
        for chip in range(chips):
            for core in range(2):
                first = ((group * chips + chip) * 2 + core) * share
                place = (group * chips + chip) * share
                turned_ref[core, place : place + share, :] = turned[first : first + share]
    keep_ref[...] = turned_ref[(lax.axis_index("seq") % 2)]
    other_ref[...] = turned_ref[1 - (lax.axis_index("seq") % 2)]


def middle(groups, lengths, attended, frames, before, after, cotangent, out_weight, gain, taps):
    heads, packed_rows, width = attended.shape
    size = packed_rows * 2 // 3
    model = frames.shape[1]
    rows = width + 2 * HALO
    return pl.pallas_call(
        lambda *refs: middle_kernel(groups, *refs),
        out_shape=(
            jax.ShapeDtypeStruct((width, model), BF16),
            jax.ShapeDtypeStruct((width, model), F32),
            jax.ShapeDtypeStruct((heads, size + groups * TAP_ROWS, width), BF16),
            jax.ShapeDtypeStruct((width, heads * size), BF16),
            jax.ShapeDtypeStruct((model // 2, width), BF16),
            jax.ShapeDtypeStruct((model // 2, width), BF16),
        ),
        in_specs=[smem()] + vmem(8),
        out_specs=tuple(vmem(6)),
        scratch_shapes=[
            pltpu.VMEM((rows, model), F32),
            pltpu.VMEM((width, model), F32),
            pltpu.VMEM((rows, model), F32),
            pltpu.VMEM((width + HALO, CHUNK), F32),
            pltpu.VMEM((width, model), F32),
            pltpu.VMEM((width, CHUNK), F32),
            pltpu.VMEM((width, CHUNK), F32),
            pltpu.VMEM((2, model // 2, width), BF16),
            pltpu.VMEM((heads, groups * TAP_ROWS, width), F32),
        ],
        compiler_params=pltpu.CompilerParams(vmem_limit_bytes=VMEM_LIMIT),
        cost_estimate=cost(4 * rows * model * heads * size * 8, 2 * model * heads * size),
        name="middle",
    )(lengths, attended, frames, before, after, cotangent, out_weight, gain, taps)


def backward_kernel(len_ref, qkv_ref, stats_ref, grad_ref, send_ref, out_ref, *refs):
    tap_refs, total_ref = refs[:-1], refs[-1]
    size = qkv_ref.shape[0] // 3
    frames = qkv_ref.shape[1]
    peers, _, width = grad_ref.shape
    length = len_ref[0]
    total_ref[...] = jnp.sum(grad_ref[:, size:, :].astype(F32), axis=0)
    for place, tap_ref in enumerate(tap_refs):
        first = pl.multiple_of((lax.axis_index("dp") ^ place) * TAP_ROWS, TAP_ROWS)
        tap_ref[...] = total_ref[pl.ds(first, TAP_ROWS), :]
    scale = size**-0.5
    keys_turned = qkv_ref[size : 2 * size, :]
    keys = keys_turned.astype(F32).T.astype(BF16)
    values = qkv_ref[2 * size :, :].astype(F32).T.astype(BF16)
    grads = jnp.concatenate([grad_ref[peer, 0:size, :] for peer in range(peers)], axis=1)
    key_sum = jnp.zeros((size, frames), F32)
    value_sum = jnp.zeros((size, frames), F32)
    for start in range(0, frames, QUERY_BLOCK):
        cols = slice(start, start + QUERY_BLOCK)
        queries = qkv_ref[0:size, cols]
        block = grads[:, cols]
        scores = key_weights(dot_nn(keys, queries), length, scale)
        probs = jnp.exp(scores - stats_ref[0:1, cols]) * stats_ref[1:2, cols]
        prob_grads = dot_nn(values, block)
        delta = jnp.sum(probs * prob_grads, axis=0, keepdims=True)
        score_grads = (probs * (prob_grads - delta) * scale).astype(BF16)
        out_ref[0:size, cols] = dot_nn(keys_turned, score_grads).astype(BF16)
        key_sum = key_sum + dot_nt(queries, score_grads)
        value_sum = value_sum + dot_nt(block, probs.astype(BF16))
    out_ref[size : 2 * size, :] = key_sum.astype(BF16)
    out_ref[2 * size :, :] = value_sum.astype(BF16)
    for peer in range(peers):
        send_ref[peer] = out_ref[:, peer * width : (peer + 1) * width]


def attention_backward(lengths, qkv, stats, grads):
    peers, rows, width = grads.shape
    size = qkv.shape[0] // 3
    groups = (rows - size) // TAP_ROWS
    frames = peers * width
    return pl.pallas_call(
        backward_kernel,
        out_shape=(
            jax.ShapeDtypeStruct((peers, 3 * size, width), BF16),
            jax.ShapeDtypeStruct((3 * size, frames), BF16),
        )
        + (jax.ShapeDtypeStruct((TAP_ROWS, width), F32),) * groups,
        in_specs=[smem()] + vmem(3),
        out_specs=tuple(vmem(2 + groups)),
        scratch_shapes=[pltpu.VMEM((groups * TAP_ROWS, width), F32)],
        compiler_params=pltpu.CompilerParams(vmem_limit_bytes=VMEM_LIMIT),
        cost_estimate=cost(20 * frames * frames * size, 2 * frames * size * 10),
        name="attention_backward",
    )(lengths, qkv, stats, grads)


def chip_order(chip):
    far = chip // 2
    return (chip, chip ^ 1, 2 - far, 3 - 3 * far)


def qkv_kernel(left_ref, pair_ref, near_ref, far_ref, relayed_ref, *refs):
    out_refs, order_ref, blocks_ref = refs[:-2], refs[-2], refs[-1]
    blocks, double, half = near_ref.shape
    rows = left_ref.shape[0]
    width = double // 2
    for chip, origin in enumerate(chip_order((lax.axis_index("seq") // 2))):
        for place in range(2):
            frame = pl.multiple_of((origin * 2 + ((lax.axis_index("seq") % 2) ^ place)) * width, CHUNK)
            cols = slice((2 * chip + place) * width, (2 * chip + place + 1) * width)
            order_ref[:rows, cols] = left_ref[:, pl.ds(frame, width)]
            order_ref[rows:, cols] = pair_ref[:, pl.ds(frame, width)]
    span = 2 * CHUNK
    far = blocks * double
    for part in range(half // span):
        cols = slice(part * span, (part + 1) * span)
        product = dot_nn(order_ref[:, :far], near_ref[:, :, cols].reshape(far, span))
        rest = (far_ref[:, :, cols] + relayed_ref[:, :, cols]).reshape(far, span)
        product = product + dot_nn(order_ref[:, far:], rest)
        blocks_ref[cols, :] = product.T.astype(BF16)
    share = half // len(out_refs)
    for place, out_ref in enumerate(out_refs):
        first = pl.multiple_of((lax.axis_index("dp") ^ place) * share, 64)
        out_ref[...] = blocks_ref[pl.ds(first, share), :]


def qkv_parts(left, pair, near, far, relayed, groups):
    half = near.shape[2]
    rows, frames = left.shape
    return pl.pallas_call(
        qkv_kernel,
        out_shape=tuple(
            jax.ShapeDtypeStruct((half // groups, 2 * rows), BF16) for _ in range(groups)
        ),
        in_specs=vmem(5),
        out_specs=tuple(vmem(groups)),
        scratch_shapes=[
            pltpu.VMEM((2 * rows, frames), BF16),
            pltpu.VMEM((half, 2 * rows), BF16),
        ],
        compiler_params=pltpu.CompilerParams(vmem_limit_bytes=VMEM_LIMIT),
        cost_estimate=cost(),
        name="qkv_parts",
    )(left, pair, near, far, relayed)


def out_kernel(low_ref, att_ref, pair_low_ref, pair_att_ref, *out_refs):
    *out_refs, blocks_ref = out_refs
    product = dot_nn(low_ref[...], att_ref[...]) + dot_nn(pair_low_ref[...], pair_att_ref[...])
    blocks_ref[...] = product.astype(BF16).reshape(blocks_ref.shape)
    for place, out_ref in enumerate(out_refs):
        out_ref[...] = blocks_ref[lax.axis_index("dp") ^ place]


def out_parts(low, att, pair_low, pair_att, groups):
    rows = low.shape[0] // groups
    columns = att.shape[1]
    return pl.pallas_call(
        out_kernel,
        out_shape=tuple(jax.ShapeDtypeStruct((rows, columns), BF16) for _ in range(groups)),
        in_specs=vmem(4),
        out_specs=tuple(vmem(groups)),
        scratch_shapes=[pltpu.VMEM((groups, rows, columns), BF16)],
        compiler_params=pltpu.CompilerParams(vmem_limit_bytes=VMEM_LIMIT),
        cost_estimate=cost(),
        name="out_parts",
    )(low, att, pair_low, pair_att)


def summed(refs):
    total = refs[0][...].astype(F32)
    for ref in refs[1:]:
        total = total + ref[...].astype(F32)
    return total


def group_kernel(groups, *refs):
    out_ref = refs[-1]
    columns = refs[groups].shape[1]
    chips, share, _ = out_ref.shape
    out_ref[:, :, :columns] = summed(refs[groups : 2 * groups]).astype(BF16).reshape(chips, share, columns)
    out_ref[:, :, columns:] = summed(refs[:groups]).astype(BF16).reshape(chips, share, -1)


def group_sums(qkv_got, out_got, chips):
    rows = qkv_got[0].shape[0]
    columns = qkv_got[0].shape[1] + out_got[0].shape[1]
    return pl.pallas_call(
        lambda *refs: group_kernel(len(qkv_got), *refs),
        out_shape=jax.ShapeDtypeStruct((chips, rows // chips, columns), BF16),
        in_specs=vmem(2 * len(qkv_got)),
        out_specs=vmem(1)[0],
        compiler_params=pltpu.CompilerParams(vmem_limit_bytes=VMEM_LIMIT),
        cost_estimate=cost(),
        name="group_sums",
    )(*qkv_got, *out_got)


def input_kernel(grad_ref, weight_ref, x_ref, resid_grad_ref, gain_ref, *refs):
    tap_refs, (out_ref, row_ref, rows_ref, normed_ref) = refs[:-4], refs[-4:]
    step = pl.program_id(0)
    heads, triple, width = grad_ref.shape
    size = triple // 3
    block = weight_ref.shape[0]

    @pl.when(step == 0)
    def _():
        turned = jnp.concatenate(
            [
                grad_ref[head, part * size : (part + 1) * size, :].astype(F32)
                for part in range(3)
                for head in range(heads)
            ],
            axis=0,
        )
        rows_ref[...] = turned.T.astype(BF16)

    cols = pl.ds(pl.multiple_of(step * block, block), block)
    normed_ref[:, cols] = dot_nt(rows_ref[...], weight_ref[...])

    @pl.when(step == pl.num_programs(0) - 1)
    def _():
        taps = summed(tap_refs)
        for place in range(x_ref.shape[1] // width):
            row_ref[:, place * width : (place + 1) * width] = taps[place : place + 1]
        unit, inv_std = unit_norm(x_ref[...].astype(F32))
        scaled = normed_ref[...] * gain_ref[...][None]
        out_ref[...] = (
            resid_grad_ref[...]
            + inv_std
            * (
                scaled
                - jnp.mean(scaled, axis=-1, keepdims=True)
                - unit * jnp.mean(scaled * unit, axis=-1, keepdims=True)
            )
        ).astype(BF16)


def input_grads(grads, weight, frames, resid_grad, gain, taps):
    heads, triple, width = grads.shape
    model, columns = weight.shape
    block = 4 * CHUNK
    return pl.pallas_call(
        input_kernel,
        grid=(model // block,),
        out_shape=(
            jax.ShapeDtypeStruct((width, model), BF16),
            jax.ShapeDtypeStruct((1, model), F32),
        ),
        in_specs=[
            pl.BlockSpec((heads, triple, width), lambda i: (0, 0, 0)),
            pl.BlockSpec((block, columns), lambda i: (i, 0)),
            pl.BlockSpec((width, model), lambda i: (0, 0)),
            pl.BlockSpec((width, model), lambda i: (0, 0)),
            pl.BlockSpec((model,), lambda i: (0,)),
        ]
        + [pl.BlockSpec((TAP_ROWS, width), lambda i: (0, 0))] * len(taps),
        out_specs=(
            pl.BlockSpec((width, model), lambda i: (0, 0)),
            pl.BlockSpec((1, model), lambda i: (0, 0)),
        ),
        scratch_shapes=[pltpu.VMEM((width, columns), BF16), pltpu.VMEM((width, model), F32)],
        compiler_params=pltpu.CompilerParams(vmem_limit_bytes=VMEM_LIMIT),
        cost_estimate=cost(2 * width * model * columns, 2 * model * columns),
        name="input_grads",
    )(grads, weight, frames, resid_grad, gain, *taps)


def final_kernel(size, got_ref, weight_ref, gain_ref, taps_ref, out_ref, row_ref):
    chips = got_ref.shape[0]
    first = got_ref.shape[2] - 6 * size
    even = (lax.axis_index("seq") % 2) == 0
    rows = []
    for chip in range(chips):
        mine = got_ref[chip, :, first : first + 3 * size].astype(F32)
        pair = got_ref[chip, :, first + 3 * size :].astype(F32)
        rows += [jnp.where(even, mine, pair), jnp.where(even, pair, mine)]
    grads = jnp.concatenate(
        [row[:, part * size : (part + 1) * size] for part in range(3) for row in rows], axis=1
    )
    columns = grads.shape[1]
    out_ref[:, 0:columns] = grads
    total = got_ref[0, :, :first].astype(F32)
    for chip in range(1, chips):
        total = total + got_ref[chip, :, :first].astype(F32)
    out_ref[:, columns:] = total
    products = grads * weight_ref[...].astype(F32)
    gains = jnp.sum(products, axis=1, keepdims=True) / gain_ref[...]
    spare = jnp.zeros((CHUNK - gains.shape[0], 1), F32)
    turned = jnp.broadcast_to(jnp.concatenate([gains, spare], axis=0), (CHUNK, CHUNK)).T
    row = jnp.concatenate([taps_ref[...], turned[0:1]], axis=1)
    row_ref[...] = jnp.broadcast_to(row[None], row_ref.shape)


def final_sums(got, weight_rows, gain_rows, taps_row, everyone):
    rows, columns = weight_rows.shape
    size = columns // (6 * got.shape[0])
    width = columns + got.shape[2] - 6 * size
    return pl.pallas_call(
        lambda *refs: final_kernel(size, *refs),
        out_shape=(
            jax.ShapeDtypeStruct((rows, width), F32),
            jax.ShapeDtypeStruct((everyone, 1, taps_row.shape[1] + CHUNK), F32),
        ),
        in_specs=vmem(4),
        out_specs=tuple(vmem(2)),
        compiler_params=pltpu.CompilerParams(vmem_limit_bytes=VMEM_LIMIT),
        cost_estimate=cost(),
        name="final_sums",
    )(got, weight_rows, gain_rows, taps_row)


def exchange(blocks, axes):
    return lax.all_to_all(blocks, axes, split_axis=0, concat_axis=0, tiled=True)


def swap(block, axis, bit):
    return lax.ppermute(block, axis, [(i, i ^ bit) for i in range(lax.axis_size(axis))])


def across(block):
    return lax.ppermute(block, "seq", [(2, 4), (3, 5), (4, 2), (5, 3)])


def outward(block):
    return lax.ppermute(block, "seq", [(2, 0), (3, 1), (4, 6), (5, 7)])


def group_swap(parts):
    return [parts[0]] + [swap(parts[bit], "dp", bit) for bit in range(1, len(parts))]


def head_shards(
    frames_in,
    lengths,
    first_gain,
    second_gain,
    qkv_weight,
    out_weight,
    conv_kernel,
    layer_cotangent,
):
    both = ("dp", "seq")
    peers = lax.axis_size("seq")
    everyone = peers * lax.axis_size("dp")
    width, model = frames_in.shape[1:]
    size = out_weight.shape[1] // HEADS
    mine = lax.axis_index("seq")
    number = lax.axis_index("dp") * peers + mine
    share = model // everyone
    frames, cotangent = frames_in[0], layer_cotangent[0]
    groups = lax.axis_size("dp")
    chips = peers // 2
    qkv_send, normed = project(frames, first_gain, qkv_weight, peers)
    qkv_got = exchange(qkv_send, "seq")
    near = HALO // 2
    tails = jnp.concatenate([frames[width - HALO :], cotangent[width - near :]], axis=0)
    fronts = jnp.concatenate([frames[:HALO], cotangent[:near]], axis=0)
    before = lax.ppermute(tails, "seq", [(i, i + 1) for i in range(peers - 1)])
    after = lax.ppermute(fronts, "seq", [(i + 1, i) for i in range(peers - 1)])
    halves = normed.reshape(width, -1, 2, share).transpose(2, 0, 1, 3).reshape(2, width, -1)
    keep = lax.dynamic_index_in_dim(halves, mine % 2, 0, keepdims=False)
    other = lax.dynamic_index_in_dim(halves, 1 - mine % 2, 0, keepdims=False)
    paired = jnp.concatenate([keep, swap(other, "seq", 1)], axis=0)
    normed_near = jnp.stack([paired, swap(paired, "seq", 2)])
    weight_rows = lax.dynamic_slice_in_dim(qkv_weight, number * share, share, axis=0)
    gain_rows = lax.dynamic_slice_in_dim(first_gain, number * share, share, axis=0)[:, None]
    qkv_got, before, after, weight_rows, gain_rows = lax.optimization_barrier(
        (qkv_got, before, after, weight_rows, gain_rows)
    )
    qkv, stats, att_send, att_head = attention_forward(lengths, qkv_got)
    attended = exchange(att_send, "seq")
    attended, normed_near = lax.optimization_barrier((attended, normed_near))
    normed_far = across(normed_near)
    layer_out, resid_grad, grad_send, att_rows, low_keep, low_other = middle(
        groups, lengths, attended, frames, before, after, cotangent, out_weight, second_gain, conv_kernel
    )
    grad_send, normed_far = lax.optimization_barrier((grad_send, normed_far))
    grads = exchange(grad_send, "seq")
    blocks = out_parts( low_keep, att_rows, swap(low_other, "seq", 1), swap(att_rows, "seq", 1), groups
    )
    grads, normed_far, blocks = lax.optimization_barrier((grads, normed_far, blocks))
    normed_out = outward(normed_far)
    out_got = group_swap(blocks)
    back_send, back_head, *taps = attention_backward(lengths, qkv, stats, grads)
    pair_head = swap(back_head, "seq", 1)
    back_send, back_head, normed_out, out_got = lax.optimization_barrier(
        (back_send, back_head, normed_out, out_got)
    )
    back = exchange(back_send, "seq")
    qkv_got = group_swap(
        qkv_parts(back_head, pair_head, normed_near, normed_far, normed_out, groups)
    )
    back, qkv_got = lax.optimization_barrier((back, qkv_got))
    taps_got = group_swap(taps)
    sums = group_sums(qkv_got, out_got, chips)
    cores = [list(range(core, peers, 2)) for core in range(2)]
    got = lax.all_to_all(
        sums, "seq", split_axis=0, concat_axis=0, tiled=True, axis_index_groups=cores
    )
    input_grad, taps_row = input_grads(back, qkv_weight, frames, resid_grad, first_gain, taps_got)
    got, input_grad = lax.optimization_barrier((got, input_grad))
    weight_grads, row = final_sums(got, weight_rows, gain_rows, taps_row, everyone)
    rows = exchange(row, both)[:, 0]
    tap_count = conv_kernel.shape[0]
    conv_grad = rows[:tap_count, :model]
    gain_grads = jnp.stack([rows[:, model : model + share].reshape(-1), rows[tap_count, :model]])
    return (layer_out[None], input_grad[None], weight_grads, gain_grads, conv_grad)


def solution(mesh):
    in_specs = (P("dp", "seq", None), P("dp"), P(), P(), P(), P(), P(), P("dp", "seq", None))
    out_specs = (P("dp", "seq", None), P("dp", "seq", None), P(("dp", "seq"), None), P(), P())
    seq_count = mesh.shape["seq"]
    device_count = seq_count * mesh.shape["dp"]

    def program(*args):
        frames_dev = args[0].shape[1] // seq_count
        fits = seq_count == HEADS and frames_dev == 128 and device_count == args[6].shape[0] + 1 == 32
        plan = head_shards if fits else general_shards
        return jax.shard_map(
            plan, mesh=mesh, in_specs=in_specs, out_specs=out_specs, check_vma=False
        )(*args)

    return program
```

```python
import jax
import jax.numpy as jnp
from jax import lax
from jax.experimental import pallas as pl
from jax.experimental.pallas import tpu as pltpu
from jax.sharding import PartitionSpec as P

HEADS = 8


epsilon = 1e-05


def padded_2(cells, sides, width):
    for axis, dim in sides:
        count = lax.axis_size(axis)
        ends = count - 1
        head = lax.slice_in_dim(cells, 0, width, axis=dim)
        tail = lax.slice_in_dim(cells, cells.shape[dim] - width, cells.shape[dim], axis=dim)
        cells = jnp.concatenate(
            [
                lax.ppermute(tail, axis, [(i, (i + 1) % count) for i in range(ends)]),
                cells,
                lax.ppermute(head, axis, [((i + 1) % count, i) for i in range(ends)]),
            ],
            axis=dim,
        )
    return cells


def layer_norm(rows, gain_vec):
    row_mean = jnp.mean(rows, axis=-1, keepdims=True)
    centered = rows - row_mean
    inv_std = lax.rsqrt(jnp.mean(centered * centered, axis=-1, keepdims=True) + epsilon)
    unit_rows = centered * inv_std
    return (unit_rows * gain_vec, unit_rows, inv_std)


def norm_backward(incoming, unit_rows, inv_std, gain_vec):
    scaled = incoming * gain_vec
    return inv_std * (
        scaled
        - jnp.mean(scaled, axis=-1, keepdims=True)
        - unit_rows * jnp.mean(scaled * unit_rows, axis=-1, keepdims=True)
    )


def contract_rows(left, right):
    return lax.dot_general(
        left, right, (((1,), (1,)), ((), ())), preferred_element_type=jnp.float32
    )


def contract_cols(left, right):
    return lax.dot_general(
        left, right, (((0,), (0,)), ((), ())), preferred_element_type=jnp.float32
    )


def soft_weights(queries, key_rows, key_valid):
    score_scale = queries.shape[1] ** (-0.5)
    scores = contract_rows(queries, key_rows) * score_scale
    scores = jnp.where(key_valid[None, :], scores, -jnp.inf)
    row_max = jnp.max(scores, axis=1, keepdims=True)
    exp_scores = jnp.exp(scores - row_max)
    return exp_scores / jnp.sum(exp_scores, axis=1, keepdims=True)


def attend_forward(queries, key_rows, value_rows, key_valid):
    block_rows = min(512, queries.shape[0])
    blocks = queries.reshape(queries.shape[0] // block_rows, block_rows, queries.shape[1])

    def one_block(query_block):
        attn_probs = soft_weights(query_block, key_rows, key_valid).astype(jnp.bfloat16)
        return jnp.dot(attn_probs, value_rows, preferred_element_type=jnp.float32).astype(
            jnp.bfloat16
        )

    return lax.map(one_block, blocks).reshape(queries.shape)


def attend_backward(queries, key_rows, value_rows, key_valid, out_grads):
    block_rows = min(512, queries.shape[0])
    block_count = queries.shape[0] // block_rows
    blocks = (
        queries.reshape(block_count, block_rows, queries.shape[1]),
        out_grads.reshape(block_count, block_rows, out_grads.shape[1]),
    )
    score_scale = queries.shape[1] ** (-0.5)

    def one_block(running, pieces):
        query_block, grad_block = pieces
        attn_probs = soft_weights(query_block, key_rows, key_valid)
        probs_low = attn_probs.astype(jnp.bfloat16)
        prob_grads = contract_rows(grad_block, value_rows)
        row_delta = jnp.sum(attn_probs * prob_grads, axis=1, keepdims=True)
        score_grads = (attn_probs * (prob_grads - row_delta) * score_scale).astype(jnp.bfloat16)
        query_grads = jnp.dot(score_grads, key_rows, preferred_element_type=jnp.float32).astype(
            jnp.bfloat16
        )
        key_sum = running[0] + contract_cols(score_grads, query_block)
        value_sum = running[1] + contract_cols(probs_low, grad_block)
        return ((key_sum, value_sum), query_grads)

    zero_rows = jnp.zeros(key_rows.shape, jnp.float32)
    totals, query_grads = lax.scan(one_block, (zero_rows, zero_rows), blocks)
    return (query_grads.reshape(queries.shape), totals[0], totals[1])


def depthwise(padded, kernel, frame_count):
    total = jnp.zeros((frame_count, padded.shape[1]), jnp.float32)
    for tap_index in range(kernel.shape[0]):
        total = (
            total
            + padded[tap_index : tap_index + frame_count].astype(jnp.float32) * kernel[tap_index]
        )
    return total


def kernel_grad(padded, grads, tap_count):
    frame_count = grads.shape[0]
    grads_wide = grads.astype(jnp.float32)
    sums = [
        jnp.sum(
            padded[tap_index : tap_index + frame_count].astype(jnp.float32) * grads_wide, axis=0
        )
        for tap_index in range(tap_count)
    ]
    return jnp.stack(sums)


def pack_queries(matrix, repeats, groups, channel):
    frames_dev = matrix.shape[0]
    shaped = matrix.reshape(repeats, frames_dev // repeats, groups, channel)
    return shaped.transpose(2, 0, 1, 3).reshape(groups * repeats, frames_dev // repeats, channel)


def pack_keys(matrix, repeats, groups, channel):
    frames_dev = matrix.shape[0]
    shaped = matrix.reshape(frames_dev, groups, channel).transpose(1, 0, 2)[:, None]
    widened = jnp.broadcast_to(shaped, (groups, repeats, frames_dev, channel))
    return widened.reshape(groups * repeats, frames_dev, channel)


def unpack_rows(stacked, repeats, groups):
    rows_each = stacked.shape[1]
    channel = stacked.shape[2]
    shaped = stacked.reshape(groups, repeats, rows_each, channel).transpose(1, 2, 0, 3)
    return shaped.reshape(repeats * rows_each, groups * channel)


def local_forward(query_rows, key_rows, value_rows, key_valid):
    outputs = attend_forward(query_rows, key_rows, value_rows, key_valid)
    return outputs


def local_backward(query_rows, key_rows, value_rows, key_valid, out_grads):
    query_list, key_list, value_list = ([], [], [])
    query_grads, key_sum, value_sum = attend_backward(
        query_rows, key_rows, value_rows, key_valid, out_grads
    )
    query_list.append(query_grads)
    key_list.append(key_sum)
    value_list.append(value_sum)
    return (query_list[0], key_list[0], value_list[0])


def general_shards(
    frames_in,
    lengths,
    first_gain,
    second_gain,
    qkv_weight,
    out_weight,
    conv_kernel,
    layer_cotangent,
):
    seq_count = lax.axis_size("seq")
    frames_dev = frames_in.shape[1]
    head_width = out_weight.shape[1]
    head_size = head_width // HEADS
    repeats = max(seq_count // HEADS, 1)
    per_device = max(HEADS // seq_count, 1)
    groups = seq_count // repeats
    channel = per_device * head_size
    tap_count = conv_kernel.shape[0]
    half_taps = (tap_count - 1) // 2
    my_index = lax.axis_index("seq")
    positions = my_index * frames_dev + jnp.arange(frames_dev, dtype=jnp.int32)
    live_rows = (positions < lengths[0]).astype(jnp.float32)[:, None]
    key_valid = jnp.arange(seq_count * frames_dev, dtype=jnp.int32) < lengths[0]
    inputs = frames_in[0].astype(jnp.float32)
    normed, unit_one, inv_one = layer_norm(inputs, first_gain)
    normed_low = normed.astype(jnp.bfloat16)
    projected = jnp.dot(normed_low, qkv_weight, preferred_element_type=jnp.float32).astype(
        jnp.bfloat16
    )
    query_send = pack_queries(projected[:, :head_width], repeats, groups, channel)
    key_send = pack_keys(projected[:, head_width : 2 * head_width], repeats, groups, channel)
    value_send = pack_keys(projected[:, 2 * head_width :], repeats, groups, channel)
    got_queries, got_keys, got_values = (
        lax.all_to_all(query_send, "seq", split_axis=0, concat_axis=1, tiled=True),
        lax.all_to_all(key_send, "seq", split_axis=0, concat_axis=1, tiled=True),
        lax.all_to_all(value_send, "seq", split_axis=0, concat_axis=1, tiled=True),
    )
    query_rows = got_queries[0]
    key_rows = got_keys[0]
    value_rows = got_values[0]
    head_out = local_forward(query_rows, key_rows, value_rows, key_valid)
    returned = lax.all_to_all(head_out[None], "seq", split_axis=1, concat_axis=0, tiled=True)
    attended = unpack_rows(returned, repeats, groups)
    resid = inputs + contract_rows(attended, out_weight)
    normed_two, unit_two, inv_two = layer_norm(resid, second_gain)
    conv_in = (live_rows * normed_two).astype(jnp.bfloat16)
    padded = padded_2(conv_in, (("seq", 0),), half_taps)
    conv_sum = depthwise(padded, conv_kernel, frames_dev)
    sigmoid_c = jax.nn.sigmoid(conv_sum)
    layer_out = (live_rows * (resid + conv_sum * sigmoid_c)).astype(jnp.bfloat16)
    outer_grad = live_rows * layer_cotangent[0].astype(jnp.float32)
    conv_grads = (outer_grad * sigmoid_c * (1.0 + conv_sum * (1.0 - sigmoid_c))).astype(
        jnp.bfloat16
    )
    kernel_part = kernel_grad(padded, conv_grads, tap_count)
    grad_padded = padded_2(conv_grads, (("seq", 0),), half_taps)
    into_conv = depthwise(grad_padded, conv_kernel[::-1], frames_dev) * live_rows
    second_part = jnp.sum(into_conv * unit_two, axis=0)
    resid_grad = outer_grad + norm_backward(into_conv, unit_two, inv_two, second_gain)
    resid_low = resid_grad.astype(jnp.bfloat16)
    attended_grad = jnp.dot(resid_low, out_weight, preferred_element_type=jnp.float32).astype(
        jnp.bfloat16
    )
    sent_grads = lax.all_to_all(
        pack_queries(attended_grad, repeats, groups, channel),
        "seq",
        split_axis=0,
        concat_axis=1,
        tiled=True,
    )
    query_grads, key_sums, value_sums = local_backward(
        query_rows, key_rows, value_rows, key_valid, sent_grads[0]
    )
    query_back = lax.all_to_all(query_grads[None], "seq", split_axis=1, concat_axis=0, tiled=True)
    key_back, value_back = (
        lax.all_to_all(
            key_sums[None].astype(jnp.bfloat16), "seq", split_axis=1, concat_axis=0, tiled=True
        ).astype(jnp.float32),
        lax.all_to_all(
            value_sums[None].astype(jnp.bfloat16), "seq", split_axis=1, concat_axis=0, tiled=True
        ).astype(jnp.float32),
    )

    def fold_parts(stacked):
        shaped = stacked.reshape(groups, repeats, frames_dev, channel)
        summed = jnp.sum(shaped, axis=1).transpose(1, 0, 2)
        return summed.reshape(frames_dev, head_width).astype(jnp.bfloat16)

    query_grad_rows = unpack_rows(query_back, repeats, groups)
    key_grad_rows = fold_parts(key_back)
    value_grad_rows = fold_parts(value_back)
    qkv_grads = jnp.concatenate([query_grad_rows, key_grad_rows, value_grad_rows], axis=1)
    normed_grad = contract_rows(qkv_grads, qkv_weight)
    first_part = jnp.sum(normed_grad * unit_one, axis=0)
    input_grad = (resid_grad + norm_backward(normed_grad, unit_one, inv_one, first_gain)).astype(
        jnp.bfloat16
    )
    weight_grads = lax.psum_scatter(
        jnp.concatenate(
            [contract_cols(normed_low, qkv_grads), contract_cols(resid_low, attended)], axis=1
        ),
        ("dp", "seq"),
        scatter_dimension=0,
        tiled=True,
    )
    gain_sum, kernel_sum = lax.psum(
        (jnp.stack([first_part, second_part]), kernel_part), ("dp", "seq")
    )
    return (layer_out[None], input_grad[None], weight_grads, gain_sum, kernel_sum)


HALO = 32
BF16 = jnp.bfloat16
F32 = jnp.float32
VMEM_LIMIT = 56 * 2**20
CHUNK = 128
QUERY_BLOCK = 1024
TAP_ROWS = 16


def vmem(count):
    return [pl.BlockSpec(memory_space=pltpu.VMEM)] * count


def smem():
    return pl.BlockSpec(memory_space=pltpu.SMEM)


def cost(flops=1000, nbytes=1000):
    return pl.CostEstimate(flops=flops, bytes_accessed=nbytes, transcendentals=0)


def dot_nn(left, right):
    return lax.dot_general(left, right, (((1,), (0,)), ((), ())), preferred_element_type=F32)


def dot_nt(left, right):
    return lax.dot_general(left, right, (((1,), (1,)), ((), ())), preferred_element_type=F32)


def unit_norm(rows):
    centered = rows - jnp.mean(rows, axis=-1, keepdims=True)
    inv_std = lax.rsqrt(jnp.mean(centered * centered, axis=-1, keepdims=True) + epsilon)
    return centered * inv_std, inv_std


def project_kernel(x_ref, gain_ref, weight_ref, send_ref, normed_ref):
    @pl.when(pl.program_id(0) == 0)
    def _():
        unit, _ = unit_norm(x_ref[...].astype(F32))
        normed_ref[...] = (unit * gain_ref[...][None]).astype(BF16)

    product = dot_nn(normed_ref[...], weight_ref[...])
    send_ref[...] = product.T.astype(BF16).reshape(send_ref.shape)


def project(frames, gain, weight, peers):
    width, model = frames.shape
    columns = weight.shape[1]
    size = columns // (3 * peers)
    return pl.pallas_call(
        project_kernel,
        grid=(3,),
        out_shape=(
            jax.ShapeDtypeStruct((peers, 3 * size, width), BF16),
            jax.ShapeDtypeStruct((width, model), BF16),
        ),
        in_specs=[
            pl.BlockSpec((width, model), lambda i: (0, 0)),
            pl.BlockSpec((model,), lambda i: (0,)),
            pl.BlockSpec((model, peers * size), lambda i: (0, i)),
        ],
        out_specs=(
            pl.BlockSpec((peers, size, width), lambda i: (0, i, 0)),
            pl.BlockSpec((width, model), lambda i: (0, 0)),
        ),
        compiler_params=pltpu.CompilerParams(vmem_limit_bytes=VMEM_LIMIT),
        cost_estimate=cost(),
        name="project",
    )(frames, gain, weight)


def key_weights(scores, length, scale):
    live = lax.broadcasted_iota(jnp.int32, scores.shape, 0) < length
    return jnp.where(live, scores * scale, -jnp.inf)


def forward_kernel(len_ref, got_ref, qkv_ref, stats_ref, out_ref, att_ref, wide_ref):
    size = qkv_ref.shape[0] // 3
    frames = qkv_ref.shape[1]
    length = len_ref[0]
    scale = size**-0.5
    span = got_ref.shape[2]
    for peer in range(got_ref.shape[0]):
        qkv_ref[:, peer * span : (peer + 1) * span] = got_ref[peer]
    keys = qkv_ref[size : 2 * size, :].astype(F32).T.astype(BF16)
    values = qkv_ref[2 * size :, :]
    for start in range(0, frames, QUERY_BLOCK):
        cols = slice(start, start + QUERY_BLOCK)
        scores = key_weights(dot_nn(keys, qkv_ref[0:size, cols]), length, scale)
        top = jnp.max(scores, axis=0, keepdims=True)
        exps = jnp.exp(scores - top)
        inverse = 1.0 / jnp.sum(exps, axis=0, keepdims=True)
        attended = dot_nn(values, (exps * inverse).astype(BF16)).astype(BF16)
        att_ref[:, cols] = attended
        wide_ref[:, cols] = attended.astype(F32)
        stats_ref[0:1, cols] = top
        stats_ref[1:2, cols] = inverse
    peers, rows, width = out_ref.shape
    half = size // 2
    blank = jnp.zeros((size, HALO), F32)
    for peer in range(peers):
        first, last = peer * width, (peer + 1) * width
        out_ref[peer, 0:size, :] = att_ref[:, first:last]
        before = wide_ref[:, first - width : first][:, width - HALO :] if peer else blank
        after = wide_ref[:, last : last + width][:, :HALO] if peer < peers - 1 else blank
        edges = jnp.concatenate([before, after], axis=1)
        packed = jnp.concatenate([edges[:half], edges[half:]], axis=1)
        out_ref[peer, size:, :] = packed.astype(BF16)


def attention_forward(length, got):
    peers, triple, width = got.shape
    size = triple // 3
    frames = peers * width
    return pl.pallas_call(
        forward_kernel,
        out_shape=(
            jax.ShapeDtypeStruct((triple, frames), BF16),
            jax.ShapeDtypeStruct((8, frames), F32),
            jax.ShapeDtypeStruct((peers, size + size // 2, width), BF16),
            jax.ShapeDtypeStruct((size, frames), BF16),
        ),
        in_specs=[smem()] + vmem(1),
        out_specs=tuple(vmem(4)),
        scratch_shapes=[pltpu.VMEM((size, frames), F32)],
        compiler_params=pltpu.CompilerParams(vmem_limit_bytes=VMEM_LIMIT),
        cost_estimate=cost(),
        name="attention_forward",
    )(length, got)


def middle_kernel(
    groups,
    len_ref,
    att_ref,
    x_ref,
    before_ref,
    after_ref,
    cot_ref,
    weight_ref,
    gain_ref,
    taps_ref,
    layer_ref,
    resid_grad_ref,
    send_ref,
    att_out_ref,
    keep_ref,
    other_ref,
    resid_ref,
    unit_ref,
    conv_ref,
    grads_ref,
    into_ref,
    sum_ref,
    dot_ref,
    turned_ref,
    taps_out_ref,
):
    heads, packed_rows, width = att_ref.shape
    size = packed_rows * 2 // 3
    half = size // 2
    model = x_ref.shape[1]
    tap_count = taps_ref.shape[0]
    reach = (tap_count - 1) // 2
    near = HALO // 2
    main, edges = [], []
    for head in range(heads):
        main.append(att_ref[head, 0:size, :].astype(F32))
        packed = att_ref[head, size:, :].astype(F32)
        edges.append(packed[:, 0 : 2 * HALO])
        edges.append(packed[:, 2 * HALO :])
    att = jnp.concatenate(
        [jnp.concatenate(main, axis=0).T, jnp.concatenate(edges, axis=0).T], axis=0
    ).astype(BF16)
    product = dot_nt(att, weight_ref[...])
    resid_ref[0:HALO, :] = before_ref[0:HALO, :].astype(F32) + product[width : width + HALO]
    resid_ref[HALO : HALO + width, :] = x_ref[...].astype(F32) + product[:width]
    resid_ref[HALO + width :, :] = after_ref[0:HALO, :].astype(F32) + product[width + HALO :]
    unit, inv_std = unit_norm(resid_ref[...])
    unit_ref[...] = unit[HALO : HALO + width]
    rows = width + 2 * HALO
    place = lax.broadcasted_iota(jnp.int32, (rows, 1), 0) - HALO + lax.axis_index("seq") * width
    live = jnp.where((place >= 0) & (place < len_ref[0]), 1.0, 0.0).astype(F32)
    conv_ref[...] = (live * (unit * gain_ref[...][None])).astype(BF16).astype(F32)
    span = width + 2 * near
    live_span = live[near : near + span]
    live_main = live[HALO : HALO + width]
    sum_ref[...] = jnp.zeros_like(sum_ref)
    dot_ref[...] = jnp.zeros_like(dot_ref)

    taps_out_ref[...] = jnp.zeros_like(taps_out_ref)

    @pl.loop(0, model // CHUNK)
    def _(step):
        cols = pl.ds(pl.multiple_of(step * CHUNK, CHUNK), CHUNK)
        taps = taps_ref[:, cols]

        def put(tap, row):
            place = pl.ds(tap // heads * TAP_ROWS + step, 1)
            taps_out_ref[tap % heads, place, :] = row

        longest = tap_count // 8 * 8
        total = jnp.zeros((span, CHUNK), F32)
        for shift in range(8):
            part = conv_ref[pl.ds(HALO - near - reach + shift, span + longest), cols]
            for tap in range(shift, tap_count, 8):
                total = total + part[tap - shift : tap - shift + span] * taps[tap : tap + 1]
        gate = 1.0 / (1.0 + jnp.exp(-total))
        resid = resid_ref[pl.ds(HALO, width), cols]
        layer_ref[:, cols] = (
            live_main * (resid + total[near : near + width] * gate[near : near + width])
        ).astype(BF16)
        outer = live_span * jnp.concatenate(
            [before_ref[HALO:, cols], cot_ref[:, cols], after_ref[HALO:, cols]], axis=0
        ).astype(F32)
        grads = (outer * gate * (1.0 + total * (1.0 - gate))).astype(BF16).astype(F32)
        grads_ref[...] = grads
        inner = grads[near : near + width]
        for shift in range(8):
            part = conv_ref[pl.ds(HALO - reach + shift, width + longest), cols]
            for tap in range(shift, tap_count, 8):
                terms = part[tap - shift : tap - shift + width] * inner
                put(tap, jnp.sum(terms, axis=0, keepdims=True))
        into = jnp.zeros((width, CHUNK), F32)
        for shift in range(8):
            part = grads_ref[pl.ds(shift, width + longest), :]
            for offset in range(0, longest + 8, 8):
                tap = near + reach - shift - offset
                if tap < tap_count:
                    into = into + part[offset : offset + width] * taps[tap : tap + 1]
        into = into * live_main
        unit_part = unit_ref[:, cols]
        put(tap_count, jnp.sum(into * unit_part, axis=0, keepdims=True))
        scaled = into * gain_ref[cols][None]
        into_ref[:, cols] = scaled
        sum_ref[...] += scaled
        dot_ref[...] += scaled * unit_part

    mean = jnp.sum(sum_ref[...], axis=1, keepdims=True) / model
    mean_dot = jnp.sum(dot_ref[...], axis=1, keepdims=True) / model
    resid_grad = live_main * cot_ref[...].astype(F32) + inv_std[HALO : HALO + width] * (
        into_ref[...] - mean - unit_ref[...] * mean_dot
    )
    resid_grad_ref[...] = resid_grad
    send = dot_nn(resid_grad.astype(BF16), weight_ref[...]).T.astype(BF16)
    send_ref[:, 0:size, :] = send.reshape(heads, size, width)
    send_ref[:, size:, :] = taps_out_ref[...].astype(BF16)
    att_out_ref[...] = att[:width]
    chips = heads // 2
    share = model // (groups * heads)
    turned = resid_grad.T.astype(BF16)
    for group in range(groups):
        for chip in range(chips):
            for core in range(2):
                first = ((group * chips + chip) * 2 + core) * share
                place = (group * chips + chip) * share
                turned_ref[core, place : place + share, :] = turned[first : first + share]
    keep_ref[...] = turned_ref[(lax.axis_index("seq") % 2)]
    other_ref[...] = turned_ref[1 - (lax.axis_index("seq") % 2)]


def middle(groups, lengths, attended, frames, before, after, cotangent, out_weight, gain, taps):
    heads, packed_rows, width = attended.shape
    size = packed_rows * 2 // 3
    model = frames.shape[1]
    rows = width + 2 * HALO
    return pl.pallas_call(
        lambda *refs: middle_kernel(groups, *refs),
        out_shape=(
            jax.ShapeDtypeStruct((width, model), BF16),
            jax.ShapeDtypeStruct((width, model), F32),
            jax.ShapeDtypeStruct((heads, size + groups * TAP_ROWS, width), BF16),
            jax.ShapeDtypeStruct((width, heads * size), BF16),
            jax.ShapeDtypeStruct((model // 2, width), BF16),
            jax.ShapeDtypeStruct((model // 2, width), BF16),
        ),
        in_specs=[smem()] + vmem(8),
        out_specs=tuple(vmem(6)),
        scratch_shapes=[
            pltpu.VMEM((rows, model), F32),
            pltpu.VMEM((width, model), F32),
            pltpu.VMEM((rows, model), F32),
            pltpu.VMEM((width + HALO, CHUNK), F32),
            pltpu.VMEM((width, model), F32),
            pltpu.VMEM((width, CHUNK), F32),
            pltpu.VMEM((width, CHUNK), F32),
            pltpu.VMEM((2, model // 2, width), BF16),
            pltpu.VMEM((heads, groups * TAP_ROWS, width), F32),
        ],
        compiler_params=pltpu.CompilerParams(vmem_limit_bytes=VMEM_LIMIT),
        cost_estimate=cost(),
        name="middle",
    )(lengths, attended, frames, before, after, cotangent, out_weight, gain, taps)


def backward_kernel(len_ref, qkv_ref, stats_ref, grad_ref, send_ref, out_ref, *refs):
    tap_refs, total_ref = refs[:-1], refs[-1]
    size = qkv_ref.shape[0] // 3
    frames = qkv_ref.shape[1]
    peers, _, width = grad_ref.shape
    length = len_ref[0]
    total_ref[...] = jnp.sum(grad_ref[:, size:, :].astype(F32), axis=0)
    for place, tap_ref in enumerate(tap_refs):
        first = pl.multiple_of((lax.axis_index("dp") ^ place) * TAP_ROWS, TAP_ROWS)
        tap_ref[...] = total_ref[pl.ds(first, TAP_ROWS), :]
    scale = size**-0.5
    keys_turned = qkv_ref[size : 2 * size, :]
    keys = keys_turned.astype(F32).T.astype(BF16)
    values = qkv_ref[2 * size :, :].astype(F32).T.astype(BF16)
    grads = jnp.concatenate([grad_ref[peer, 0:size, :] for peer in range(peers)], axis=1)
    key_sum = jnp.zeros((size, frames), F32)
    value_sum = jnp.zeros((size, frames), F32)
    for start in range(0, frames, QUERY_BLOCK):
        cols = slice(start, start + QUERY_BLOCK)
        queries = qkv_ref[0:size, cols]
        block = grads[:, cols]
        scores = key_weights(dot_nn(keys, queries), length, scale)
        probs = jnp.exp(scores - stats_ref[0:1, cols]) * stats_ref[1:2, cols]
        prob_grads = dot_nn(values, block)
        delta = jnp.sum(probs * prob_grads, axis=0, keepdims=True)
        score_grads = (probs * (prob_grads - delta) * scale).astype(BF16)
        out_ref[0:size, cols] = dot_nn(keys_turned, score_grads).astype(BF16)
        key_sum = key_sum + dot_nt(queries, score_grads)
        value_sum = value_sum + dot_nt(block, probs.astype(BF16))
    out_ref[size : 2 * size, :] = key_sum.astype(BF16)
    out_ref[2 * size :, :] = value_sum.astype(BF16)
    for peer in range(peers):
        send_ref[peer] = out_ref[:, peer * width : (peer + 1) * width]


def attention_backward(lengths, qkv, stats, grads):
    peers, rows, width = grads.shape
    size = qkv.shape[0] // 3
    groups = (rows - size) // TAP_ROWS
    frames = peers * width
    return pl.pallas_call(
        backward_kernel,
        out_shape=(
            jax.ShapeDtypeStruct((peers, 3 * size, width), BF16),
            jax.ShapeDtypeStruct((3 * size, frames), BF16),
        )
        + (jax.ShapeDtypeStruct((TAP_ROWS, width), F32),) * groups,
        in_specs=[smem()] + vmem(3),
        out_specs=tuple(vmem(2 + groups)),
        scratch_shapes=[pltpu.VMEM((groups * TAP_ROWS, width), F32)],
        compiler_params=pltpu.CompilerParams(vmem_limit_bytes=VMEM_LIMIT),
        cost_estimate=cost(nbytes=22 * 10**6),
        name="attention_backward",
    )(lengths, qkv, stats, grads)


def chip_order(chip):
    far = chip // 2
    return (chip, chip ^ 1, 2 - far, 3 - 3 * far)


def qkv_kernel(left_ref, pair_ref, near_ref, far_ref, relayed_ref, *refs):
    out_refs, order_ref, blocks_ref = refs[:-2], refs[-2], refs[-1]
    blocks, double, half = near_ref.shape
    rows = left_ref.shape[0]
    width = double // 2
    for chip, origin in enumerate(chip_order((lax.axis_index("seq") // 2))):
        for place in range(2):
            frame = pl.multiple_of((origin * 2 + ((lax.axis_index("seq") % 2) ^ place)) * width, CHUNK)
            cols = slice((2 * chip + place) * width, (2 * chip + place + 1) * width)
            order_ref[:rows, cols] = left_ref[:, pl.ds(frame, width)]
            order_ref[rows:, cols] = pair_ref[:, pl.ds(frame, width)]
    span = 2 * CHUNK
    far = blocks * double
    for part in range(half // span):
        cols = slice(part * span, (part + 1) * span)
        product = dot_nn(order_ref[:, :far], near_ref[:, :, cols].reshape(far, span))
        rest = (far_ref[:, :, cols] + relayed_ref[:, :, cols]).reshape(far, span)
        product = product + dot_nn(order_ref[:, far:], rest)
        blocks_ref[cols, :] = product.T.astype(BF16)
    share = half // len(out_refs)
    for place, out_ref in enumerate(out_refs):
        first = pl.multiple_of((lax.axis_index("dp") ^ place) * share, 64)
        out_ref[...] = blocks_ref[pl.ds(first, share), :]


def qkv_parts(left, pair, near, far, relayed, groups):
    half = near.shape[2]
    rows, frames = left.shape
    return pl.pallas_call(
        qkv_kernel,
        out_shape=tuple(
            jax.ShapeDtypeStruct((half // groups, 2 * rows), BF16) for _ in range(groups)
        ),
        in_specs=vmem(5),
        out_specs=tuple(vmem(groups)),
        scratch_shapes=[
            pltpu.VMEM((2 * rows, frames), BF16),
            pltpu.VMEM((half, 2 * rows), BF16),
        ],
        compiler_params=pltpu.CompilerParams(vmem_limit_bytes=VMEM_LIMIT),
        cost_estimate=cost(),
        name="qkv_parts",
    )(left, pair, near, far, relayed)


def out_kernel(low_ref, att_ref, pair_low_ref, pair_att_ref, *out_refs):
    *out_refs, blocks_ref = out_refs
    product = dot_nn(low_ref[...], att_ref[...]) + dot_nn(pair_low_ref[...], pair_att_ref[...])
    blocks_ref[...] = product.astype(BF16).reshape(blocks_ref.shape)
    for place, out_ref in enumerate(out_refs):
        out_ref[...] = blocks_ref[lax.axis_index("dp") ^ place]


def out_parts(low, att, pair_low, pair_att, groups):
    rows = low.shape[0] // groups
    columns = att.shape[1]
    return pl.pallas_call(
        out_kernel,
        out_shape=tuple(jax.ShapeDtypeStruct((rows, columns), BF16) for _ in range(groups)),
        in_specs=vmem(4),
        out_specs=tuple(vmem(groups)),
        scratch_shapes=[pltpu.VMEM((groups, rows, columns), BF16)],
        compiler_params=pltpu.CompilerParams(vmem_limit_bytes=VMEM_LIMIT),
        cost_estimate=cost(),
        name="out_parts",
    )(low, att, pair_low, pair_att)


def summed(refs):
    total = refs[0][...].astype(F32)
    for ref in refs[1:]:
        total = total + ref[...].astype(F32)
    return total


def group_kernel(groups, *refs):
    out_ref = refs[-1]
    columns = refs[groups].shape[1]
    chips, share, _ = out_ref.shape
    out_ref[:, :, :columns] = summed(refs[groups : 2 * groups]).astype(BF16).reshape(chips, share, columns)
    out_ref[:, :, columns:] = summed(refs[:groups]).astype(BF16).reshape(chips, share, -1)


def group_sums(qkv_got, out_got, chips):
    rows = qkv_got[0].shape[0]
    columns = qkv_got[0].shape[1] + out_got[0].shape[1]
    return pl.pallas_call(
        lambda *refs: group_kernel(len(qkv_got), *refs),
        out_shape=jax.ShapeDtypeStruct((chips, rows // chips, columns), BF16),
        in_specs=vmem(2 * len(qkv_got)),
        out_specs=vmem(1)[0],
        compiler_params=pltpu.CompilerParams(vmem_limit_bytes=VMEM_LIMIT),
        cost_estimate=cost(),
        name="group_sums",
    )(*qkv_got, *out_got)


def input_kernel(grad_ref, weight_ref, x_ref, resid_grad_ref, gain_ref, *refs):
    tap_refs, (out_ref, row_ref, rows_ref, normed_ref) = refs[:-4], refs[-4:]
    step = pl.program_id(0)
    heads, triple, width = grad_ref.shape
    size = triple // 3
    block = weight_ref.shape[0]

    @pl.when(step == 0)
    def _():
        turned = jnp.concatenate(
            [
                grad_ref[head, part * size : (part + 1) * size, :].astype(F32)
                for part in range(3)
                for head in range(heads)
            ],
            axis=0,
        )
        rows_ref[...] = turned.T.astype(BF16)

    cols = pl.ds(pl.multiple_of(step * block, block), block)
    normed_ref[:, cols] = dot_nt(rows_ref[...], weight_ref[...])

    @pl.when(step == pl.num_programs(0) - 1)
    def _():
        taps = summed(tap_refs)
        for place in range(x_ref.shape[1] // width):
            row_ref[:, place * width : (place + 1) * width] = taps[place : place + 1]
        unit, inv_std = unit_norm(x_ref[...].astype(F32))
        scaled = normed_ref[...] * gain_ref[...][None]
        out_ref[...] = (
            resid_grad_ref[...]
            + inv_std
            * (
                scaled
                - jnp.mean(scaled, axis=-1, keepdims=True)
                - unit * jnp.mean(scaled * unit, axis=-1, keepdims=True)
            )
        ).astype(BF16)


def input_grads(grads, weight, frames, resid_grad, gain, taps):
    heads, triple, width = grads.shape
    model, columns = weight.shape
    block = 4 * CHUNK
    return pl.pallas_call(
        input_kernel,
        grid=(model // block,),
        out_shape=(
            jax.ShapeDtypeStruct((width, model), BF16),
            jax.ShapeDtypeStruct((1, model), F32),
        ),
        in_specs=[
            pl.BlockSpec((heads, triple, width), lambda i: (0, 0, 0)),
            pl.BlockSpec((block, columns), lambda i: (i, 0)),
            pl.BlockSpec((width, model), lambda i: (0, 0)),
            pl.BlockSpec((width, model), lambda i: (0, 0)),
            pl.BlockSpec((model,), lambda i: (0,)),
        ]
        + [pl.BlockSpec((TAP_ROWS, width), lambda i: (0, 0))] * len(taps),
        out_specs=(
            pl.BlockSpec((width, model), lambda i: (0, 0)),
            pl.BlockSpec((1, model), lambda i: (0, 0)),
        ),
        scratch_shapes=[pltpu.VMEM((width, columns), BF16), pltpu.VMEM((width, model), F32)],
        compiler_params=pltpu.CompilerParams(vmem_limit_bytes=VMEM_LIMIT),
        cost_estimate=cost(),
        name="input_grads",
    )(grads, weight, frames, resid_grad, gain, *taps)


def final_kernel(size, got_ref, weight_ref, gain_ref, taps_ref, out_ref, row_ref):
    chips = got_ref.shape[0]
    first = got_ref.shape[2] - 6 * size
    even = (lax.axis_index("seq") % 2) == 0
    rows = []
    for chip in range(chips):
        mine = got_ref[chip, :, first : first + 3 * size].astype(F32)
        pair = got_ref[chip, :, first + 3 * size :].astype(F32)
        rows += [jnp.where(even, mine, pair), jnp.where(even, pair, mine)]
    grads = jnp.concatenate(
        [row[:, part * size : (part + 1) * size] for part in range(3) for row in rows], axis=1
    )
    columns = grads.shape[1]
    out_ref[:, 0:columns] = grads
    total = got_ref[0, :, :first].astype(F32)
    for chip in range(1, chips):
        total = total + got_ref[chip, :, :first].astype(F32)
    out_ref[:, columns:] = total
    products = grads * weight_ref[...].astype(F32)
    gains = jnp.sum(products, axis=1, keepdims=True) / gain_ref[...]
    spare = jnp.zeros((CHUNK - gains.shape[0], 1), F32)
    turned = jnp.broadcast_to(jnp.concatenate([gains, spare], axis=0), (CHUNK, CHUNK)).T
    row = jnp.concatenate([taps_ref[...], turned[0:1]], axis=1)
    row_ref[...] = jnp.broadcast_to(row[None], row_ref.shape)


def final_sums(got, weight_rows, gain_rows, taps_row, everyone):
    rows, columns = weight_rows.shape
    size = columns // (6 * got.shape[0])
    width = columns + got.shape[2] - 6 * size
    return pl.pallas_call(
        lambda *refs: final_kernel(size, *refs),
        out_shape=(
            jax.ShapeDtypeStruct((rows, width), F32),
            jax.ShapeDtypeStruct((everyone, 1, taps_row.shape[1] + CHUNK), F32),
        ),
        in_specs=vmem(4),
        out_specs=tuple(vmem(2)),
        compiler_params=pltpu.CompilerParams(vmem_limit_bytes=VMEM_LIMIT),
        cost_estimate=cost(),
        name="final_sums",
    )(got, weight_rows, gain_rows, taps_row)


def exchange(blocks, axes):
    return lax.all_to_all(blocks, axes, split_axis=0, concat_axis=0, tiled=True)


def swap(block, axis, bit):
    return lax.ppermute(block, axis, [(i, i ^ bit) for i in range(lax.axis_size(axis))])


def across(block):
    return lax.ppermute(block, "seq", [(2, 4), (3, 5), (4, 2), (5, 3)])


def outward(block):
    return lax.ppermute(block, "seq", [(2, 0), (3, 1), (4, 6), (5, 7)])


def group_swap(parts):
    return [parts[0]] + [swap(parts[bit], "dp", bit) for bit in range(1, len(parts))]


def head_shards(
    frames_in,
    lengths,
    first_gain,
    second_gain,
    qkv_weight,
    out_weight,
    conv_kernel,
    layer_cotangent,
):
    both = ("dp", "seq")
    peers = lax.axis_size("seq")
    everyone = peers * lax.axis_size("dp")
    width, model = frames_in.shape[1:]
    size = out_weight.shape[1] // HEADS
    mine = lax.axis_index("seq")
    number = lax.axis_index("dp") * peers + mine
    share = model // everyone
    frames, cotangent = frames_in[0], layer_cotangent[0]
    groups = lax.axis_size("dp")
    chips = peers // 2
    qkv_send, normed = project(frames, first_gain, qkv_weight, peers)
    qkv_got = exchange(qkv_send, "seq")
    near = HALO // 2
    tails = jnp.concatenate([frames[width - HALO :], cotangent[width - near :]], axis=0)
    fronts = jnp.concatenate([frames[:HALO], cotangent[:near]], axis=0)
    before = lax.ppermute(tails, "seq", [(i, i + 1) for i in range(peers - 1)])
    after = lax.ppermute(fronts, "seq", [(i + 1, i) for i in range(peers - 1)])
    halves = normed.reshape(width, -1, 2, share).transpose(2, 0, 1, 3).reshape(2, width, -1)
    keep = lax.dynamic_index_in_dim(halves, mine % 2, 0, keepdims=False)
    other = lax.dynamic_index_in_dim(halves, 1 - mine % 2, 0, keepdims=False)
    paired = jnp.concatenate([keep, swap(other, "seq", 1)], axis=0)
    normed_near = jnp.stack([paired, swap(paired, "seq", 2)])
    weight_rows = lax.dynamic_slice_in_dim(qkv_weight, number * share, share, axis=0)
    gain_rows = lax.dynamic_slice_in_dim(first_gain, number * share, share, axis=0)[:, None]
    qkv_got, before, after, weight_rows, gain_rows = lax.optimization_barrier(
        (qkv_got, before, after, weight_rows, gain_rows)
    )
    qkv, stats, att_send, att_head = attention_forward(lengths, qkv_got)
    attended = exchange(att_send, "seq")
    attended, normed_near = lax.optimization_barrier((attended, normed_near))
    normed_far = across(normed_near)
    layer_out, resid_grad, grad_send, att_rows, low_keep, low_other = middle(
        groups, lengths, attended, frames, before, after, cotangent, out_weight, second_gain, conv_kernel
    )
    grad_send, normed_far = lax.optimization_barrier((grad_send, normed_far))
    grads = exchange(grad_send, "seq")
    blocks = out_parts( low_keep, att_rows, swap(low_other, "seq", 1), swap(att_rows, "seq", 1), groups
    )
    grads, blocks = lax.optimization_barrier((grads, blocks))
    normed_out = outward(normed_far)
    out_got = group_swap(blocks)
    back_send, back_head, *taps = attention_backward(lengths, qkv, stats, grads)
    pair_head = swap(back_head, "seq", 1)
    back_send, back_head, normed_out, out_got = lax.optimization_barrier(
        (back_send, back_head, normed_out, out_got)
    )
    back = exchange(back_send, "seq")
    qkv_got = group_swap(
        qkv_parts(back_head, pair_head, normed_near, normed_far, normed_out, groups)
    )
    back, qkv_got = lax.optimization_barrier((back, qkv_got))
    taps_got = group_swap(taps)
    sums = group_sums(qkv_got, out_got, chips)
    cores = [list(range(core, peers, 2)) for core in range(2)]
    got = lax.all_to_all(
        sums, "seq", split_axis=0, concat_axis=0, tiled=True, axis_index_groups=cores
    )
    input_grad, taps_row = input_grads(back, qkv_weight, frames, resid_grad, first_gain, taps_got)
    got, input_grad = lax.optimization_barrier((got, input_grad))
    weight_grads, row = final_sums(got, weight_rows, gain_rows, taps_row, everyone)
    rows = exchange(row, both)[:, 0]
    tap_count = conv_kernel.shape[0]
    conv_grad = rows[:tap_count, :model]
    gain_grads = jnp.stack([rows[:, model : model + share].reshape(-1), rows[tap_count, :model]])
    return (layer_out[None], input_grad[None], weight_grads, gain_grads, conv_grad)


def solution(mesh):
    in_specs = (P("dp", "seq", None), P("dp"), P(), P(), P(), P(), P(), P("dp", "seq", None))
    out_specs = (P("dp", "seq", None), P("dp", "seq", None), P(("dp", "seq"), None), P(), P())
    seq_count = mesh.shape["seq"]
    device_count = seq_count * mesh.shape["dp"]

    def program(*args):
        frames_dev = args[0].shape[1] // seq_count
        fits = seq_count == HEADS and frames_dev == 128 and device_count == args[6].shape[0] + 1 == 32
        plan = head_shards if fits else general_shards
        return jax.shard_map(
            plan, mesh=mesh, in_specs=in_specs, out_specs=out_specs, check_vma=False
        )(*args)

    return program
```

```python
import jax
import jax.numpy as jnp
from jax import lax
from jax.experimental import pallas as pl
from jax.experimental.pallas import tpu as pltpu
from jax.sharding import PartitionSpec as P

HEADS = 8


epsilon = 1e-05


def padded_2(cells, sides, width):
    for axis, dim in sides:
        count = lax.axis_size(axis)
        ends = count - 1
        head = lax.slice_in_dim(cells, 0, width, axis=dim)
        tail = lax.slice_in_dim(cells, cells.shape[dim] - width, cells.shape[dim], axis=dim)
        cells = jnp.concatenate(
            [
                lax.ppermute(tail, axis, [(i, (i + 1) % count) for i in range(ends)]),
                cells,
                lax.ppermute(head, axis, [((i + 1) % count, i) for i in range(ends)]),
            ],
            axis=dim,
        )
    return cells


def layer_norm(rows, gain_vec):
    row_mean = jnp.mean(rows, axis=-1, keepdims=True)
    centered = rows - row_mean
    inv_std = lax.rsqrt(jnp.mean(centered * centered, axis=-1, keepdims=True) + epsilon)
    unit_rows = centered * inv_std
    return (unit_rows * gain_vec, unit_rows, inv_std)


def norm_backward(incoming, unit_rows, inv_std, gain_vec):
    scaled = incoming * gain_vec
    return inv_std * (
        scaled
        - jnp.mean(scaled, axis=-1, keepdims=True)
        - unit_rows * jnp.mean(scaled * unit_rows, axis=-1, keepdims=True)
    )


def contract_rows(left, right):
    return lax.dot_general(
        left, right, (((1,), (1,)), ((), ())), preferred_element_type=jnp.float32
    )


def contract_cols(left, right):
    return lax.dot_general(
        left, right, (((0,), (0,)), ((), ())), preferred_element_type=jnp.float32
    )


def soft_weights(queries, key_rows, key_valid):
    score_scale = queries.shape[1] ** (-0.5)
    scores = contract_rows(queries, key_rows) * score_scale
    scores = jnp.where(key_valid[None, :], scores, -jnp.inf)
    row_max = jnp.max(scores, axis=1, keepdims=True)
    exp_scores = jnp.exp(scores - row_max)
    return exp_scores / jnp.sum(exp_scores, axis=1, keepdims=True)


def attend_forward(queries, key_rows, value_rows, key_valid):
    block_rows = min(512, queries.shape[0])
    blocks = queries.reshape(queries.shape[0] // block_rows, block_rows, queries.shape[1])

    def one_block(query_block):
        attn_probs = soft_weights(query_block, key_rows, key_valid).astype(jnp.bfloat16)
        return jnp.dot(attn_probs, value_rows, preferred_element_type=jnp.float32).astype(
            jnp.bfloat16
        )

    return lax.map(one_block, blocks).reshape(queries.shape)


def attend_backward(queries, key_rows, value_rows, key_valid, out_grads):
    block_rows = min(512, queries.shape[0])
    block_count = queries.shape[0] // block_rows
    blocks = (
        queries.reshape(block_count, block_rows, queries.shape[1]),
        out_grads.reshape(block_count, block_rows, out_grads.shape[1]),
    )
    score_scale = queries.shape[1] ** (-0.5)

    def one_block(running, pieces):
        query_block, grad_block = pieces
        attn_probs = soft_weights(query_block, key_rows, key_valid)
        probs_low = attn_probs.astype(jnp.bfloat16)
        prob_grads = contract_rows(grad_block, value_rows)
        row_delta = jnp.sum(attn_probs * prob_grads, axis=1, keepdims=True)
        score_grads = (attn_probs * (prob_grads - row_delta) * score_scale).astype(jnp.bfloat16)
        query_grads = jnp.dot(score_grads, key_rows, preferred_element_type=jnp.float32).astype(
            jnp.bfloat16
        )
        key_sum = running[0] + contract_cols(score_grads, query_block)
        value_sum = running[1] + contract_cols(probs_low, grad_block)
        return ((key_sum, value_sum), query_grads)

    zero_rows = jnp.zeros(key_rows.shape, jnp.float32)
    totals, query_grads = lax.scan(one_block, (zero_rows, zero_rows), blocks)
    return (query_grads.reshape(queries.shape), totals[0], totals[1])


def depthwise(padded, kernel, frame_count):
    total = jnp.zeros((frame_count, padded.shape[1]), jnp.float32)
    for tap_index in range(kernel.shape[0]):
        total = (
            total
            + padded[tap_index : tap_index + frame_count].astype(jnp.float32) * kernel[tap_index]
        )
    return total


def kernel_grad(padded, grads, tap_count):
    frame_count = grads.shape[0]
    grads_wide = grads.astype(jnp.float32)
    sums = [
        jnp.sum(
            padded[tap_index : tap_index + frame_count].astype(jnp.float32) * grads_wide, axis=0
        )
        for tap_index in range(tap_count)
    ]
    return jnp.stack(sums)


def pack_queries(matrix, repeats, groups, channel):
    frames_dev = matrix.shape[0]
    shaped = matrix.reshape(repeats, frames_dev // repeats, groups, channel)
    return shaped.transpose(2, 0, 1, 3).reshape(groups * repeats, frames_dev // repeats, channel)


def pack_keys(matrix, repeats, groups, channel):
    frames_dev = matrix.shape[0]
    shaped = matrix.reshape(frames_dev, groups, channel).transpose(1, 0, 2)[:, None]
    widened = jnp.broadcast_to(shaped, (groups, repeats, frames_dev, channel))
    return widened.reshape(groups * repeats, frames_dev, channel)


def unpack_rows(stacked, repeats, groups):
    rows_each = stacked.shape[1]
    channel = stacked.shape[2]
    shaped = stacked.reshape(groups, repeats, rows_each, channel).transpose(1, 2, 0, 3)
    return shaped.reshape(repeats * rows_each, groups * channel)


def local_forward(query_rows, key_rows, value_rows, key_valid):
    outputs = attend_forward(query_rows, key_rows, value_rows, key_valid)
    return outputs


def local_backward(query_rows, key_rows, value_rows, key_valid, out_grads):
    query_list, key_list, value_list = ([], [], [])
    query_grads, key_sum, value_sum = attend_backward(
        query_rows, key_rows, value_rows, key_valid, out_grads
    )
    query_list.append(query_grads)
    key_list.append(key_sum)
    value_list.append(value_sum)
    return (query_list[0], key_list[0], value_list[0])


def general_shards(
    frames_in,
    lengths,
    first_gain,
    second_gain,
    qkv_weight,
    out_weight,
    conv_kernel,
    layer_cotangent,
):
    seq_count = lax.axis_size("seq")
    frames_dev = frames_in.shape[1]
    head_width = out_weight.shape[1]
    head_size = head_width // HEADS
    repeats = max(seq_count // HEADS, 1)
    per_device = max(HEADS // seq_count, 1)
    groups = seq_count // repeats
    channel = per_device * head_size
    tap_count = conv_kernel.shape[0]
    half_taps = (tap_count - 1) // 2
    my_index = lax.axis_index("seq")
    positions = my_index * frames_dev + jnp.arange(frames_dev, dtype=jnp.int32)
    live_rows = (positions < lengths[0]).astype(jnp.float32)[:, None]
    key_valid = jnp.arange(seq_count * frames_dev, dtype=jnp.int32) < lengths[0]
    inputs = frames_in[0].astype(jnp.float32)
    normed, unit_one, inv_one = layer_norm(inputs, first_gain)
    normed_low = normed.astype(jnp.bfloat16)
    projected = jnp.dot(normed_low, qkv_weight, preferred_element_type=jnp.float32).astype(
        jnp.bfloat16
    )
    query_send = pack_queries(projected[:, :head_width], repeats, groups, channel)
    key_send = pack_keys(projected[:, head_width : 2 * head_width], repeats, groups, channel)
    value_send = pack_keys(projected[:, 2 * head_width :], repeats, groups, channel)
    got_queries, got_keys, got_values = (
        lax.all_to_all(query_send, "seq", split_axis=0, concat_axis=1, tiled=True),
        lax.all_to_all(key_send, "seq", split_axis=0, concat_axis=1, tiled=True),
        lax.all_to_all(value_send, "seq", split_axis=0, concat_axis=1, tiled=True),
    )
    query_rows = got_queries[0]
    key_rows = got_keys[0]
    value_rows = got_values[0]
    head_out = local_forward(query_rows, key_rows, value_rows, key_valid)
    returned = lax.all_to_all(head_out[None], "seq", split_axis=1, concat_axis=0, tiled=True)
    attended = unpack_rows(returned, repeats, groups)
    resid = inputs + contract_rows(attended, out_weight)
    normed_two, unit_two, inv_two = layer_norm(resid, second_gain)
    conv_in = (live_rows * normed_two).astype(jnp.bfloat16)
    padded = padded_2(conv_in, (("seq", 0),), half_taps)
    conv_sum = depthwise(padded, conv_kernel, frames_dev)
    sigmoid_c = jax.nn.sigmoid(conv_sum)
    layer_out = (live_rows * (resid + conv_sum * sigmoid_c)).astype(jnp.bfloat16)
    outer_grad = live_rows * layer_cotangent[0].astype(jnp.float32)
    conv_grads = (outer_grad * sigmoid_c * (1.0 + conv_sum * (1.0 - sigmoid_c))).astype(
        jnp.bfloat16
    )
    kernel_part = kernel_grad(padded, conv_grads, tap_count)
    grad_padded = padded_2(conv_grads, (("seq", 0),), half_taps)
    into_conv = depthwise(grad_padded, conv_kernel[::-1], frames_dev) * live_rows
    second_part = jnp.sum(into_conv * unit_two, axis=0)
    resid_grad = outer_grad + norm_backward(into_conv, unit_two, inv_two, second_gain)
    resid_low = resid_grad.astype(jnp.bfloat16)
    attended_grad = jnp.dot(resid_low, out_weight, preferred_element_type=jnp.float32).astype(
        jnp.bfloat16
    )
    sent_grads = lax.all_to_all(
        pack_queries(attended_grad, repeats, groups, channel),
        "seq",
        split_axis=0,
        concat_axis=1,
        tiled=True,
    )
    query_grads, key_sums, value_sums = local_backward(
        query_rows, key_rows, value_rows, key_valid, sent_grads[0]
    )
    query_back = lax.all_to_all(query_grads[None], "seq", split_axis=1, concat_axis=0, tiled=True)
    key_back, value_back = (
        lax.all_to_all(
            key_sums[None].astype(jnp.bfloat16), "seq", split_axis=1, concat_axis=0, tiled=True
        ).astype(jnp.float32),
        lax.all_to_all(
            value_sums[None].astype(jnp.bfloat16), "seq", split_axis=1, concat_axis=0, tiled=True
        ).astype(jnp.float32),
    )

    def fold_parts(stacked):
        shaped = stacked.reshape(groups, repeats, frames_dev, channel)
        summed = jnp.sum(shaped, axis=1).transpose(1, 0, 2)
        return summed.reshape(frames_dev, head_width).astype(jnp.bfloat16)

    query_grad_rows = unpack_rows(query_back, repeats, groups)
    key_grad_rows = fold_parts(key_back)
    value_grad_rows = fold_parts(value_back)
    qkv_grads = jnp.concatenate([query_grad_rows, key_grad_rows, value_grad_rows], axis=1)
    normed_grad = contract_rows(qkv_grads, qkv_weight)
    first_part = jnp.sum(normed_grad * unit_one, axis=0)
    input_grad = (resid_grad + norm_backward(normed_grad, unit_one, inv_one, first_gain)).astype(
        jnp.bfloat16
    )
    weight_grads = lax.psum_scatter(
        jnp.concatenate(
            [contract_cols(normed_low, qkv_grads), contract_cols(resid_low, attended)], axis=1
        ),
        ("dp", "seq"),
        scatter_dimension=0,
        tiled=True,
    )
    gain_sum, kernel_sum = lax.psum(
        (jnp.stack([first_part, second_part]), kernel_part), ("dp", "seq")
    )
    return (layer_out[None], input_grad[None], weight_grads, gain_sum, kernel_sum)


HALO = 32
BF16 = jnp.bfloat16
F32 = jnp.float32
VMEM_LIMIT = 56 * 2**20
CHUNK = 128
QUERY_BLOCK = 1024
TAP_ROWS = 16


def vmem(count):
    return [pl.BlockSpec(memory_space=pltpu.VMEM)] * count


def smem():
    return pl.BlockSpec(memory_space=pltpu.SMEM)


def cost(flops=1000, nbytes=1000):
    return pl.CostEstimate(flops=flops, bytes_accessed=nbytes, transcendentals=0)


def dot_nn(left, right):
    return lax.dot_general(left, right, (((1,), (0,)), ((), ())), preferred_element_type=F32)


def dot_nt(left, right):
    return lax.dot_general(left, right, (((1,), (1,)), ((), ())), preferred_element_type=F32)


def unit_norm(rows):
    centered = rows - jnp.mean(rows, axis=-1, keepdims=True)
    inv_std = lax.rsqrt(jnp.mean(centered * centered, axis=-1, keepdims=True) + epsilon)
    return centered * inv_std, inv_std


def project_kernel(x_ref, gain_ref, weight_ref, send_ref, normed_ref):
    @pl.when(pl.program_id(0) == 0)
    def _():
        unit, _ = unit_norm(x_ref[...].astype(F32))
        normed_ref[...] = (unit * gain_ref[...][None]).astype(BF16)

    product = dot_nn(normed_ref[...], weight_ref[...])
    send_ref[...] = product.T.astype(BF16).reshape(send_ref.shape)


def project(frames, gain, weight, peers):
    width, model = frames.shape
    columns = weight.shape[1]
    size = columns // (3 * peers)
    return pl.pallas_call(
        project_kernel,
        grid=(3,),
        out_shape=(
            jax.ShapeDtypeStruct((peers, 3 * size, width), BF16),
            jax.ShapeDtypeStruct((width, model), BF16),
        ),
        in_specs=[
            pl.BlockSpec((width, model), lambda i: (0, 0)),
            pl.BlockSpec((model,), lambda i: (0,)),
            pl.BlockSpec((model, peers * size), lambda i: (0, i)),
        ],
        out_specs=(
            pl.BlockSpec((peers, size, width), lambda i: (0, i, 0)),
            pl.BlockSpec((width, model), lambda i: (0, 0)),
        ),
        compiler_params=pltpu.CompilerParams(vmem_limit_bytes=VMEM_LIMIT),
        cost_estimate=cost(),
        name="project",
    )(frames, gain, weight)


def key_weights(scores, length, scale):
    live = lax.broadcasted_iota(jnp.int32, scores.shape, 0) < length
    return jnp.where(live, scores * scale, -jnp.inf)


def forward_kernel(len_ref, got_ref, qkv_ref, stats_ref, out_ref, att_ref, wide_ref):
    size = qkv_ref.shape[0] // 3
    frames = qkv_ref.shape[1]
    length = len_ref[0]
    scale = size**-0.5
    span = got_ref.shape[2]
    for peer in range(got_ref.shape[0]):
        qkv_ref[:, peer * span : (peer + 1) * span] = got_ref[peer]
    keys = qkv_ref[size : 2 * size, :].astype(F32).T.astype(BF16)
    values = qkv_ref[2 * size :, :]
    for start in range(0, frames, QUERY_BLOCK):
        cols = slice(start, start + QUERY_BLOCK)
        scores = key_weights(dot_nn(keys, qkv_ref[0:size, cols]), length, scale)
        top = jnp.max(scores, axis=0, keepdims=True)
        exps = jnp.exp(scores - top)
        inverse = 1.0 / jnp.sum(exps, axis=0, keepdims=True)
        attended = dot_nn(values, (exps * inverse).astype(BF16)).astype(BF16)
        att_ref[:, cols] = attended
        wide_ref[:, cols] = attended.astype(F32)
        stats_ref[0:1, cols] = top
        stats_ref[1:2, cols] = inverse
    peers, rows, width = out_ref.shape
    half = size // 2
    blank = jnp.zeros((size, HALO), F32)
    for peer in range(peers):
        first, last = peer * width, (peer + 1) * width
        out_ref[peer, 0:size, :] = att_ref[:, first:last]
        before = wide_ref[:, first - width : first][:, width - HALO :] if peer else blank
        after = wide_ref[:, last : last + width][:, :HALO] if peer < peers - 1 else blank
        edges = jnp.concatenate([before, after], axis=1)
        packed = jnp.concatenate([edges[:half], edges[half:]], axis=1)
        out_ref[peer, size:, :] = packed.astype(BF16)


def attention_forward(length, got):
    peers, triple, width = got.shape
    size = triple // 3
    frames = peers * width
    return pl.pallas_call(
        forward_kernel,
        out_shape=(
            jax.ShapeDtypeStruct((triple, frames), BF16),
            jax.ShapeDtypeStruct((8, frames), F32),
            jax.ShapeDtypeStruct((peers, size + size // 2, width), BF16),
            jax.ShapeDtypeStruct((size, frames), BF16),
        ),
        in_specs=[smem()] + vmem(1),
        out_specs=tuple(vmem(4)),
        scratch_shapes=[pltpu.VMEM((size, frames), F32)],
        compiler_params=pltpu.CompilerParams(vmem_limit_bytes=VMEM_LIMIT),
        cost_estimate=cost(),
        name="attention_forward",
    )(length, got)


def middle_kernel(
    groups,
    len_ref,
    att_ref,
    x_ref,
    before_ref,
    after_ref,
    cot_ref,
    weight_ref,
    gain_ref,
    taps_ref,
    layer_ref,
    resid_grad_ref,
    send_ref,
    att_out_ref,
    keep_ref,
    other_ref,
    resid_ref,
    unit_ref,
    conv_ref,
    grads_ref,
    into_ref,
    sum_ref,
    dot_ref,
    turned_ref,
    taps_out_ref,
):
    heads, packed_rows, width = att_ref.shape
    size = packed_rows * 2 // 3
    half = size // 2
    model = x_ref.shape[1]
    tap_count = taps_ref.shape[0]
    reach = (tap_count - 1) // 2
    near = HALO // 2
    main, edges = [], []
    for head in range(heads):
        main.append(att_ref[head, 0:size, :].astype(F32))
        packed = att_ref[head, size:, :].astype(F32)
        edges.append(packed[:, 0 : 2 * HALO])
        edges.append(packed[:, 2 * HALO :])
    att = jnp.concatenate(
        [jnp.concatenate(main, axis=0).T, jnp.concatenate(edges, axis=0).T], axis=0
    ).astype(BF16)
    product = dot_nt(att, weight_ref[...])
    resid_ref[0:HALO, :] = before_ref[0:HALO, :].astype(F32) + product[width : width + HALO]
    resid_ref[HALO : HALO + width, :] = x_ref[...].astype(F32) + product[:width]
    resid_ref[HALO + width :, :] = after_ref[0:HALO, :].astype(F32) + product[width + HALO :]
    unit, inv_std = unit_norm(resid_ref[...])
    unit_ref[...] = unit[HALO : HALO + width]
    rows = width + 2 * HALO
    place = lax.broadcasted_iota(jnp.int32, (rows, 1), 0) - HALO + lax.axis_index("seq") * width
    live = jnp.where((place >= 0) & (place < len_ref[0]), 1.0, 0.0).astype(F32)
    conv_ref[...] = (live * (unit * gain_ref[...][None])).astype(BF16).astype(F32)
    span = width + 2 * near
    live_span = live[near : near + span]
    live_main = live[HALO : HALO + width]
    sum_ref[...] = jnp.zeros_like(sum_ref)
    dot_ref[...] = jnp.zeros_like(dot_ref)

    taps_out_ref[...] = jnp.zeros_like(taps_out_ref)

    @pl.loop(0, model // CHUNK)
    def _(step):
        cols = pl.ds(pl.multiple_of(step * CHUNK, CHUNK), CHUNK)
        taps = taps_ref[:, cols]

        def put(tap, row):
            place = pl.ds(tap // heads * TAP_ROWS + step, 1)
            taps_out_ref[tap % heads, place, :] = row

        longest = tap_count // 8 * 8
        total = jnp.zeros((span, CHUNK), F32)
        for shift in range(8):
            part = conv_ref[pl.ds(HALO - near - reach + shift, span + longest), cols]
            for tap in range(shift, tap_count, 8):
                total = total + part[tap - shift : tap - shift + span] * taps[tap : tap + 1]
        gate = 1.0 / (1.0 + jnp.exp(-total))
        resid = resid_ref[pl.ds(HALO, width), cols]
        layer_ref[:, cols] = (
            live_main * (resid + total[near : near + width] * gate[near : near + width])
        ).astype(BF16)
        outer = live_span * jnp.concatenate(
            [before_ref[HALO:, cols], cot_ref[:, cols], after_ref[HALO:, cols]], axis=0
        ).astype(F32)
        grads = (outer * gate * (1.0 + total * (1.0 - gate))).astype(BF16).astype(F32)
        grads_ref[...] = grads
        inner = grads[near : near + width]
        for shift in range(8):
            part = conv_ref[pl.ds(HALO - reach + shift, width + longest), cols]
            for tap in range(shift, tap_count, 8):
                terms = part[tap - shift : tap - shift + width] * inner
                put(tap, jnp.sum(terms, axis=0, keepdims=True))
        into = jnp.zeros((width, CHUNK), F32)
        for shift in range(8):
            part = grads_ref[pl.ds(shift, width + longest), :]
            for offset in range(0, longest + 8, 8):
                tap = near + reach - shift - offset
                if tap < tap_count:
                    into = into + part[offset : offset + width] * taps[tap : tap + 1]
        into = into * live_main
        unit_part = unit_ref[:, cols]
        put(tap_count, jnp.sum(into * unit_part, axis=0, keepdims=True))
        scaled = into * gain_ref[cols][None]
        into_ref[:, cols] = scaled
        sum_ref[...] += scaled
        dot_ref[...] += scaled * unit_part

    mean = jnp.sum(sum_ref[...], axis=1, keepdims=True) / model
    mean_dot = jnp.sum(dot_ref[...], axis=1, keepdims=True) / model
    resid_grad = live_main * cot_ref[...].astype(F32) + inv_std[HALO : HALO + width] * (
        into_ref[...] - mean - unit_ref[...] * mean_dot
    )
    resid_grad_ref[...] = resid_grad
    send = dot_nn(resid_grad.astype(BF16), weight_ref[...]).T.astype(BF16)
    send_ref[:, 0:size, :] = send.reshape(heads, size, width)
    send_ref[:, size:, :] = taps_out_ref[...].astype(BF16)
    att_out_ref[...] = att[:width]
    chips = heads // 2
    share = model // (groups * heads)
    turned = resid_grad.T.astype(BF16)
    for group in range(groups):
        for chip in range(chips):
            for core in range(2):
                first = ((group * chips + chip) * 2 + core) * share
                place = (group * chips + chip) * share
                turned_ref[core, place : place + share, :] = turned[first : first + share]
    keep_ref[...] = turned_ref[(lax.axis_index("seq") % 2)]
    other_ref[...] = turned_ref[1 - (lax.axis_index("seq") % 2)]


def middle(groups, lengths, attended, frames, before, after, cotangent, out_weight, gain, taps):
    heads, packed_rows, width = attended.shape
    size = packed_rows * 2 // 3
    model = frames.shape[1]
    rows = width + 2 * HALO
    return pl.pallas_call(
        lambda *refs: middle_kernel(groups, *refs),
        out_shape=(
            jax.ShapeDtypeStruct((width, model), BF16),
            jax.ShapeDtypeStruct((width, model), F32),
            jax.ShapeDtypeStruct((heads, size + groups * TAP_ROWS, width), BF16),
            jax.ShapeDtypeStruct((width, heads * size), BF16),
            jax.ShapeDtypeStruct((model // 2, width), BF16),
            jax.ShapeDtypeStruct((model // 2, width), BF16),
        ),
        in_specs=[smem()] + vmem(8),
        out_specs=tuple(vmem(6)),
        scratch_shapes=[
            pltpu.VMEM((rows, model), F32),
            pltpu.VMEM((width, model), F32),
            pltpu.VMEM((rows, model), F32),
            pltpu.VMEM((width + HALO, CHUNK), F32),
            pltpu.VMEM((width, model), F32),
            pltpu.VMEM((width, CHUNK), F32),
            pltpu.VMEM((width, CHUNK), F32),
            pltpu.VMEM((2, model // 2, width), BF16),
            pltpu.VMEM((heads, groups * TAP_ROWS, width), F32),
        ],
        compiler_params=pltpu.CompilerParams(vmem_limit_bytes=VMEM_LIMIT),
        cost_estimate=cost(),
        name="middle",
    )(lengths, attended, frames, before, after, cotangent, out_weight, gain, taps)


def backward_kernel(len_ref, qkv_ref, stats_ref, grad_ref, send_ref, out_ref, *refs):
    tap_refs, total_ref = refs[:-1], refs[-1]
    size = qkv_ref.shape[0] // 3
    frames = qkv_ref.shape[1]
    peers, _, width = grad_ref.shape
    length = len_ref[0]
    total_ref[...] = jnp.sum(grad_ref[:, size:, :].astype(F32), axis=0)
    for place, tap_ref in enumerate(tap_refs):
        first = pl.multiple_of((lax.axis_index("dp") ^ place) * TAP_ROWS, TAP_ROWS)
        tap_ref[...] = total_ref[pl.ds(first, TAP_ROWS), :]
    scale = size**-0.5
    keys_turned = qkv_ref[size : 2 * size, :]
    keys = keys_turned.astype(F32).T.astype(BF16)
    values = qkv_ref[2 * size :, :].astype(F32).T.astype(BF16)
    grads = jnp.concatenate([grad_ref[peer, 0:size, :] for peer in range(peers)], axis=1)
    key_sum = jnp.zeros((size, frames), F32)
    value_sum = jnp.zeros((size, frames), F32)
    for start in range(0, frames, QUERY_BLOCK):
        cols = slice(start, start + QUERY_BLOCK)
        queries = qkv_ref[0:size, cols]
        block = grads[:, cols]
        scores = key_weights(dot_nn(keys, queries), length, scale)
        probs = jnp.exp(scores - stats_ref[0:1, cols]) * stats_ref[1:2, cols]
        prob_grads = dot_nn(values, block)
        delta = jnp.sum(probs * prob_grads, axis=0, keepdims=True)
        score_grads = (probs * (prob_grads - delta) * scale).astype(BF16)
        out_ref[0:size, cols] = dot_nn(keys_turned, score_grads).astype(BF16)
        key_sum = key_sum + dot_nt(queries, score_grads)
        value_sum = value_sum + dot_nt(block, probs.astype(BF16))
    out_ref[size : 2 * size, :] = key_sum.astype(BF16)
    out_ref[2 * size :, :] = value_sum.astype(BF16)
    for peer in range(peers):
        send_ref[peer] = out_ref[:, peer * width : (peer + 1) * width]


def attention_backward(lengths, qkv, stats, grads):
    peers, rows, width = grads.shape
    size = qkv.shape[0] // 3
    groups = (rows - size) // TAP_ROWS
    frames = peers * width
    return pl.pallas_call(
        backward_kernel,
        out_shape=(
            jax.ShapeDtypeStruct((peers, 3 * size, width), BF16),
            jax.ShapeDtypeStruct((3 * size, frames), BF16),
        )
        + (jax.ShapeDtypeStruct((TAP_ROWS, width), F32),) * groups,
        in_specs=[smem()] + vmem(3),
        out_specs=tuple(vmem(2 + groups)),
        scratch_shapes=[pltpu.VMEM((groups * TAP_ROWS, width), F32)],
        compiler_params=pltpu.CompilerParams(vmem_limit_bytes=VMEM_LIMIT),
        cost_estimate=cost(nbytes=22 * 10**6),
        name="attention_backward",
    )(lengths, qkv, stats, grads)


def chip_order(chip):
    far = chip // 2
    return (chip, chip ^ 1, 2 - far, 3 - 3 * far)


def qkv_kernel(left_ref, pair_ref, near_ref, far_ref, relayed_ref, *refs):
    out_refs, order_ref, blocks_ref = refs[:-2], refs[-2], refs[-1]
    blocks, double, half = near_ref.shape
    rows = left_ref.shape[0]
    width = double // 2
    for chip, origin in enumerate(chip_order((lax.axis_index("seq") // 2))):
        for place in range(2):
            frame = pl.multiple_of((origin * 2 + ((lax.axis_index("seq") % 2) ^ place)) * width, CHUNK)
            cols = slice((2 * chip + place) * width, (2 * chip + place + 1) * width)
            order_ref[:rows, cols] = left_ref[:, pl.ds(frame, width)]
            order_ref[rows:, cols] = pair_ref[:, pl.ds(frame, width)]
    span = 2 * CHUNK
    far = blocks * double
    for part in range(half // span):
        cols = slice(part * span, (part + 1) * span)
        product = dot_nn(order_ref[:, :far], near_ref[:, :, cols].reshape(far, span))
        rest = (far_ref[:, :, cols] + relayed_ref[:, :, cols]).reshape(far, span)
        product = product + dot_nn(order_ref[:, far:], rest)
        blocks_ref[cols, :] = product.T.astype(BF16)
    share = half // len(out_refs)
    for place, out_ref in enumerate(out_refs):
        first = pl.multiple_of((lax.axis_index("dp") ^ place) * share, 64)
        out_ref[...] = blocks_ref[pl.ds(first, share), :]


def qkv_parts(left, pair, near, far, relayed, groups):
    half = near.shape[2]
    rows, frames = left.shape
    return pl.pallas_call(
        qkv_kernel,
        out_shape=tuple(
            jax.ShapeDtypeStruct((half // groups, 2 * rows), BF16) for _ in range(groups)
        ),
        in_specs=vmem(5),
        out_specs=tuple(vmem(groups)),
        scratch_shapes=[
            pltpu.VMEM((2 * rows, frames), BF16),
            pltpu.VMEM((half, 2 * rows), BF16),
        ],
        compiler_params=pltpu.CompilerParams(vmem_limit_bytes=VMEM_LIMIT),
        cost_estimate=cost(),
        name="qkv_parts",
    )(left, pair, near, far, relayed)


def out_kernel(low_ref, att_ref, pair_low_ref, pair_att_ref, *out_refs):
    *out_refs, blocks_ref = out_refs
    product = dot_nn(low_ref[...], att_ref[...]) + dot_nn(pair_low_ref[...], pair_att_ref[...])
    blocks_ref[...] = product.astype(BF16).reshape(blocks_ref.shape)
    for place, out_ref in enumerate(out_refs):
        out_ref[...] = blocks_ref[lax.axis_index("dp") ^ place]


def out_parts(low, att, pair_low, pair_att, groups):
    rows = low.shape[0] // groups
    columns = att.shape[1]
    return pl.pallas_call(
        out_kernel,
        out_shape=tuple(jax.ShapeDtypeStruct((rows, columns), BF16) for _ in range(groups)),
        in_specs=vmem(4),
        out_specs=tuple(vmem(groups)),
        scratch_shapes=[pltpu.VMEM((groups, rows, columns), BF16)],
        compiler_params=pltpu.CompilerParams(vmem_limit_bytes=VMEM_LIMIT),
        cost_estimate=cost(),
        name="out_parts",
    )(low, att, pair_low, pair_att)


def summed(refs):
    total = refs[0][...].astype(F32)
    for ref in refs[1:]:
        total = total + ref[...].astype(F32)
    return total


def out_sum_kernel(*refs):
    refs[-1][...] = summed(refs[:-1]).astype(BF16)


def out_sums(parts):
    return pl.pallas_call(
        out_sum_kernel,
        out_shape=jax.ShapeDtypeStruct(parts[0].shape, BF16),
        in_specs=vmem(len(parts)),
        out_specs=vmem(1)[0],
        compiler_params=pltpu.CompilerParams(vmem_limit_bytes=VMEM_LIMIT),
        cost_estimate=cost(),
        name="out_sums",
    )(*parts)


def group_kernel(*refs):
    out_part_ref, out_ref = refs[-2], refs[-1]
    columns = out_part_ref.shape[1]
    chips, share, _ = out_ref.shape
    out_ref[:, :, :columns] = out_part_ref[...].reshape(chips, share, columns)
    out_ref[:, :, columns:] = summed(refs[:-2]).astype(BF16).reshape(chips, share, -1)


def group_sums(qkv_got, out_part, chips):
    rows = qkv_got[0].shape[0]
    columns = qkv_got[0].shape[1] + out_part.shape[1]
    return pl.pallas_call(
        group_kernel,
        out_shape=jax.ShapeDtypeStruct((chips, rows // chips, columns), BF16),
        in_specs=vmem(1 + len(qkv_got)),
        out_specs=vmem(1)[0],
        compiler_params=pltpu.CompilerParams(vmem_limit_bytes=VMEM_LIMIT),
        cost_estimate=cost(),
        name="group_sums",
    )(*qkv_got, out_part)


def input_kernel(grad_ref, weight_ref, x_ref, resid_grad_ref, gain_ref, *refs):
    tap_refs, (out_ref, row_ref, rows_ref, normed_ref) = refs[:-4], refs[-4:]
    step = pl.program_id(0)
    heads, triple, width = grad_ref.shape
    size = triple // 3
    block = weight_ref.shape[0]

    @pl.when(step == 0)
    def _():
        turned = jnp.concatenate(
            [
                grad_ref[head, part * size : (part + 1) * size, :].astype(F32)
                for part in range(3)
                for head in range(heads)
            ],
            axis=0,
        )
        rows_ref[...] = turned.T.astype(BF16)

    cols = pl.ds(pl.multiple_of(step * block, block), block)
    normed_ref[:, cols] = dot_nt(rows_ref[...], weight_ref[...])

    @pl.when(step == pl.num_programs(0) - 1)
    def _():
        taps = summed(tap_refs)
        for place in range(x_ref.shape[1] // width):
            row_ref[:, place * width : (place + 1) * width] = taps[place : place + 1]
        unit, inv_std = unit_norm(x_ref[...].astype(F32))
        scaled = normed_ref[...] * gain_ref[...][None]
        out_ref[...] = (
            resid_grad_ref[...]
            + inv_std
            * (
                scaled
                - jnp.mean(scaled, axis=-1, keepdims=True)
                - unit * jnp.mean(scaled * unit, axis=-1, keepdims=True)
            )
        ).astype(BF16)


def input_grads(grads, weight, frames, resid_grad, gain, taps):
    heads, triple, width = grads.shape
    model, columns = weight.shape
    block = 4 * CHUNK
    return pl.pallas_call(
        input_kernel,
        grid=(model // block,),
        out_shape=(
            jax.ShapeDtypeStruct((width, model), BF16),
            jax.ShapeDtypeStruct((1, model), F32),
        ),
        in_specs=[
            pl.BlockSpec((heads, triple, width), lambda i: (0, 0, 0)),
            pl.BlockSpec((block, columns), lambda i: (i, 0)),
            pl.BlockSpec((width, model), lambda i: (0, 0)),
            pl.BlockSpec((width, model), lambda i: (0, 0)),
            pl.BlockSpec((model,), lambda i: (0,)),
        ]
        + [pl.BlockSpec((TAP_ROWS, width), lambda i: (0, 0))] * len(taps),
        out_specs=(
            pl.BlockSpec((width, model), lambda i: (0, 0)),
            pl.BlockSpec((1, model), lambda i: (0, 0)),
        ),
        scratch_shapes=[pltpu.VMEM((width, columns), BF16), pltpu.VMEM((width, model), F32)],
        compiler_params=pltpu.CompilerParams(vmem_limit_bytes=VMEM_LIMIT),
        cost_estimate=cost(),
        name="input_grads",
    )(grads, weight, frames, resid_grad, gain, *taps)


def final_kernel(size, got_ref, weight_ref, gain_ref, taps_ref, out_ref, row_ref):
    chips = got_ref.shape[0]
    first = got_ref.shape[2] - 6 * size
    even = (lax.axis_index("seq") % 2) == 0
    rows = []
    for chip in range(chips):
        mine = got_ref[chip, :, first : first + 3 * size].astype(F32)
        pair = got_ref[chip, :, first + 3 * size :].astype(F32)
        rows += [jnp.where(even, mine, pair), jnp.where(even, pair, mine)]
    grads = jnp.concatenate(
        [row[:, part * size : (part + 1) * size] for part in range(3) for row in rows], axis=1
    )
    columns = grads.shape[1]
    out_ref[:, 0:columns] = grads
    total = got_ref[0, :, :first].astype(F32)
    for chip in range(1, chips):
        total = total + got_ref[chip, :, :first].astype(F32)
    out_ref[:, columns:] = total
    products = grads * weight_ref[...].astype(F32)
    gains = jnp.sum(products, axis=1, keepdims=True) / gain_ref[...]
    spare = jnp.zeros((CHUNK - gains.shape[0], 1), F32)
    turned = jnp.broadcast_to(jnp.concatenate([gains, spare], axis=0), (CHUNK, CHUNK)).T
    row = jnp.concatenate([taps_ref[...], turned[0:1]], axis=1)
    row_ref[...] = jnp.broadcast_to(row[None], row_ref.shape)


def final_sums(got, weight_rows, gain_rows, taps_row, everyone):
    rows, columns = weight_rows.shape
    size = columns // (6 * got.shape[0])
    width = columns + got.shape[2] - 6 * size
    return pl.pallas_call(
        lambda *refs: final_kernel(size, *refs),
        out_shape=(
            jax.ShapeDtypeStruct((rows, width), F32),
            jax.ShapeDtypeStruct((everyone, 1, taps_row.shape[1] + CHUNK), F32),
        ),
        in_specs=vmem(4),
        out_specs=tuple(vmem(2)),
        compiler_params=pltpu.CompilerParams(vmem_limit_bytes=VMEM_LIMIT),
        cost_estimate=cost(),
        name="final_sums",
    )(got, weight_rows, gain_rows, taps_row)


def exchange(blocks, axes):
    return lax.all_to_all(blocks, axes, split_axis=0, concat_axis=0, tiled=True)


def swap(block, axis, bit):
    return lax.ppermute(block, axis, [(i, i ^ bit) for i in range(lax.axis_size(axis))])


def across(block):
    return lax.ppermute(block, "seq", [(2, 4), (3, 5), (4, 2), (5, 3)])


def outward(block):
    return lax.ppermute(block, "seq", [(2, 0), (3, 1), (4, 6), (5, 7)])


def group_swap(parts):
    return [parts[0]] + [swap(parts[bit], "dp", bit) for bit in range(1, len(parts))]


def head_shards(
    frames_in,
    lengths,
    first_gain,
    second_gain,
    qkv_weight,
    out_weight,
    conv_kernel,
    layer_cotangent,
):
    both = ("dp", "seq")
    peers = lax.axis_size("seq")
    everyone = peers * lax.axis_size("dp")
    width, model = frames_in.shape[1:]
    size = out_weight.shape[1] // HEADS
    mine = lax.axis_index("seq")
    number = lax.axis_index("dp") * peers + mine
    share = model // everyone
    frames, cotangent = frames_in[0], layer_cotangent[0]
    groups = lax.axis_size("dp")
    chips = peers // 2
    qkv_send, normed = project(frames, first_gain, qkv_weight, peers)
    qkv_got = exchange(qkv_send, "seq")
    near = HALO // 2
    tails = jnp.concatenate([frames[width - HALO :], cotangent[width - near :]], axis=0)
    fronts = jnp.concatenate([frames[:HALO], cotangent[:near]], axis=0)
    before = lax.ppermute(tails, "seq", [(i, i + 1) for i in range(peers - 1)])
    after = lax.ppermute(fronts, "seq", [(i + 1, i) for i in range(peers - 1)])
    halves = normed.reshape(width, -1, 2, share).transpose(2, 0, 1, 3).reshape(2, width, -1)
    keep = lax.dynamic_index_in_dim(halves, mine % 2, 0, keepdims=False)
    other = lax.dynamic_index_in_dim(halves, 1 - mine % 2, 0, keepdims=False)
    paired = jnp.concatenate([keep, swap(other, "seq", 1)], axis=0)
    normed_near = jnp.stack([paired, swap(paired, "seq", 2)])
    weight_rows = lax.dynamic_slice_in_dim(qkv_weight, number * share, share, axis=0)
    gain_rows = lax.dynamic_slice_in_dim(first_gain, number * share, share, axis=0)[:, None]
    qkv_got, before, after, weight_rows, gain_rows = lax.optimization_barrier(
        (qkv_got, before, after, weight_rows, gain_rows)
    )
    qkv, stats, att_send, att_head = attention_forward(lengths, qkv_got)
    attended = exchange(att_send, "seq")
    attended, normed_near = lax.optimization_barrier((attended, normed_near))
    normed_far = across(normed_near)
    layer_out, resid_grad, grad_send, att_rows, low_keep, low_other = middle(
        groups, lengths, attended, frames, before, after, cotangent, out_weight, second_gain, conv_kernel
    )
    grad_send, normed_far = lax.optimization_barrier((grad_send, normed_far))
    grads = exchange(grad_send, "seq")
    blocks = out_parts( low_keep, att_rows, swap(low_other, "seq", 1), swap(att_rows, "seq", 1), groups
    )
    grads, blocks = lax.optimization_barrier((grads, blocks))
    normed_out = outward(normed_far)
    out_got = group_swap(blocks)
    back_send, back_head, *taps = attention_backward(lengths, qkv, stats, grads)
    pair_head = swap(back_head, "seq", 1)
    back_send, back_head, normed_out, out_got = lax.optimization_barrier(
        (back_send, back_head, normed_out, out_got)
    )
    back = exchange(back_send, "seq")
    qkv_got = group_swap(
        qkv_parts(back_head, pair_head, normed_near, normed_far, normed_out, groups)
    )
    out_part = out_sums(out_got)
    back, qkv_got, out_part = lax.optimization_barrier((back, qkv_got, out_part))
    taps_got = group_swap(taps)
    sums = group_sums(qkv_got, out_part, chips)
    cores = [list(range(core, peers, 2)) for core in range(2)]
    got = lax.all_to_all(
        sums, "seq", split_axis=0, concat_axis=0, tiled=True, axis_index_groups=cores
    )
    input_grad, taps_row = input_grads(back, qkv_weight, frames, resid_grad, first_gain, taps_got)
    got, input_grad = lax.optimization_barrier((got, input_grad))
    weight_grads, row = final_sums(got, weight_rows, gain_rows, taps_row, everyone)
    rows = exchange(row, both)[:, 0]
    tap_count = conv_kernel.shape[0]
    conv_grad = rows[:tap_count, :model]
    gain_grads = jnp.stack([rows[:, model : model + share].reshape(-1), rows[tap_count, :model]])
    return (layer_out[None], input_grad[None], weight_grads, gain_grads, conv_grad)


def solution(mesh):
    in_specs = (P("dp", "seq", None), P("dp"), P(), P(), P(), P(), P(), P("dp", "seq", None))
    out_specs = (P("dp", "seq", None), P("dp", "seq", None), P(("dp", "seq"), None), P(), P())
    seq_count = mesh.shape["seq"]
    device_count = seq_count * mesh.shape["dp"]

    def program(*args):
        frames_dev = args[0].shape[1] // seq_count
        fits = seq_count == HEADS and frames_dev == 128 and device_count == args[6].shape[0] + 1 == 32
        plan = head_shards if fits else general_shards
        return jax.shard_map(
            plan, mesh=mesh, in_specs=in_specs, out_specs=out_specs, check_vma=False
        )(*args)

    return program
```

```python
import jax
import jax.numpy as jnp
from jax import lax
from jax.experimental import pallas as pl
from jax.experimental.pallas import tpu as pltpu
from jax.sharding import PartitionSpec as P

HEADS = 8


epsilon = 1e-05


def padded_2(cells, sides, width):
    for axis, dim in sides:
        count = lax.axis_size(axis)
        ends = count - 1
        head = lax.slice_in_dim(cells, 0, width, axis=dim)
        tail = lax.slice_in_dim(cells, cells.shape[dim] - width, cells.shape[dim], axis=dim)
        cells = jnp.concatenate(
            [
                lax.ppermute(tail, axis, [(i, (i + 1) % count) for i in range(ends)]),
                cells,
                lax.ppermute(head, axis, [((i + 1) % count, i) for i in range(ends)]),
            ],
            axis=dim,
        )
    return cells


def layer_norm(rows, gain_vec):
    row_mean = jnp.mean(rows, axis=-1, keepdims=True)
    centered = rows - row_mean
    inv_std = lax.rsqrt(jnp.mean(centered * centered, axis=-1, keepdims=True) + epsilon)
    unit_rows = centered * inv_std
    return (unit_rows * gain_vec, unit_rows, inv_std)


def norm_backward(incoming, unit_rows, inv_std, gain_vec):
    scaled = incoming * gain_vec
    return inv_std * (
        scaled
        - jnp.mean(scaled, axis=-1, keepdims=True)
        - unit_rows * jnp.mean(scaled * unit_rows, axis=-1, keepdims=True)
    )


def contract_rows(left, right):
    return lax.dot_general(
        left, right, (((1,), (1,)), ((), ())), preferred_element_type=jnp.float32
    )


def contract_cols(left, right):
    return lax.dot_general(
        left, right, (((0,), (0,)), ((), ())), preferred_element_type=jnp.float32
    )


def soft_weights(queries, key_rows, key_valid):
    score_scale = queries.shape[1] ** (-0.5)
    scores = contract_rows(queries, key_rows) * score_scale
    scores = jnp.where(key_valid[None, :], scores, -jnp.inf)
    row_max = jnp.max(scores, axis=1, keepdims=True)
    exp_scores = jnp.exp(scores - row_max)
    return exp_scores / jnp.sum(exp_scores, axis=1, keepdims=True)


def attend_forward(queries, key_rows, value_rows, key_valid):
    block_rows = min(512, queries.shape[0])
    blocks = queries.reshape(queries.shape[0] // block_rows, block_rows, queries.shape[1])

    def one_block(query_block):
        attn_probs = soft_weights(query_block, key_rows, key_valid).astype(jnp.bfloat16)
        return jnp.dot(attn_probs, value_rows, preferred_element_type=jnp.float32).astype(
            jnp.bfloat16
        )

    return lax.map(one_block, blocks).reshape(queries.shape)


def attend_backward(queries, key_rows, value_rows, key_valid, out_grads):
    block_rows = min(512, queries.shape[0])
    block_count = queries.shape[0] // block_rows
    blocks = (
        queries.reshape(block_count, block_rows, queries.shape[1]),
        out_grads.reshape(block_count, block_rows, out_grads.shape[1]),
    )
    score_scale = queries.shape[1] ** (-0.5)

    def one_block(running, pieces):
        query_block, grad_block = pieces
        attn_probs = soft_weights(query_block, key_rows, key_valid)
        probs_low = attn_probs.astype(jnp.bfloat16)
        prob_grads = contract_rows(grad_block, value_rows)
        row_delta = jnp.sum(attn_probs * prob_grads, axis=1, keepdims=True)
        score_grads = (attn_probs * (prob_grads - row_delta) * score_scale).astype(jnp.bfloat16)
        query_grads = jnp.dot(score_grads, key_rows, preferred_element_type=jnp.float32).astype(
            jnp.bfloat16
        )
        key_sum = running[0] + contract_cols(score_grads, query_block)
        value_sum = running[1] + contract_cols(probs_low, grad_block)
        return ((key_sum, value_sum), query_grads)

    zero_rows = jnp.zeros(key_rows.shape, jnp.float32)
    totals, query_grads = lax.scan(one_block, (zero_rows, zero_rows), blocks)
    return (query_grads.reshape(queries.shape), totals[0], totals[1])


def depthwise(padded, kernel, frame_count):
    total = jnp.zeros((frame_count, padded.shape[1]), jnp.float32)
    for tap_index in range(kernel.shape[0]):
        total = (
            total
            + padded[tap_index : tap_index + frame_count].astype(jnp.float32) * kernel[tap_index]
        )
    return total


def kernel_grad(padded, grads, tap_count):
    frame_count = grads.shape[0]
    grads_wide = grads.astype(jnp.float32)
    sums = [
        jnp.sum(
            padded[tap_index : tap_index + frame_count].astype(jnp.float32) * grads_wide, axis=0
        )
        for tap_index in range(tap_count)
    ]
    return jnp.stack(sums)


def pack_queries(matrix, repeats, groups, channel):
    frames_dev = matrix.shape[0]
    shaped = matrix.reshape(repeats, frames_dev // repeats, groups, channel)
    return shaped.transpose(2, 0, 1, 3).reshape(groups * repeats, frames_dev // repeats, channel)


def pack_keys(matrix, repeats, groups, channel):
    frames_dev = matrix.shape[0]
    shaped = matrix.reshape(frames_dev, groups, channel).transpose(1, 0, 2)[:, None]
    widened = jnp.broadcast_to(shaped, (groups, repeats, frames_dev, channel))
    return widened.reshape(groups * repeats, frames_dev, channel)


def unpack_rows(stacked, repeats, groups):
    rows_each = stacked.shape[1]
    channel = stacked.shape[2]
    shaped = stacked.reshape(groups, repeats, rows_each, channel).transpose(1, 2, 0, 3)
    return shaped.reshape(repeats * rows_each, groups * channel)


def local_forward(query_rows, key_rows, value_rows, key_valid):
    outputs = attend_forward(query_rows, key_rows, value_rows, key_valid)
    return outputs


def local_backward(query_rows, key_rows, value_rows, key_valid, out_grads):
    query_list, key_list, value_list = ([], [], [])
    query_grads, key_sum, value_sum = attend_backward(
        query_rows, key_rows, value_rows, key_valid, out_grads
    )
    query_list.append(query_grads)
    key_list.append(key_sum)
    value_list.append(value_sum)
    return (query_list[0], key_list[0], value_list[0])


def general_shards(
    frames_in,
    lengths,
    first_gain,
    second_gain,
    qkv_weight,
    out_weight,
    conv_kernel,
    layer_cotangent,
):
    seq_count = lax.axis_size("seq")
    frames_dev = frames_in.shape[1]
    head_width = out_weight.shape[1]
    head_size = head_width // HEADS
    repeats = max(seq_count // HEADS, 1)
    per_device = max(HEADS // seq_count, 1)
    groups = seq_count // repeats
    channel = per_device * head_size
    tap_count = conv_kernel.shape[0]
    half_taps = (tap_count - 1) // 2
    my_index = lax.axis_index("seq")
    positions = my_index * frames_dev + jnp.arange(frames_dev, dtype=jnp.int32)
    live_rows = (positions < lengths[0]).astype(jnp.float32)[:, None]
    key_valid = jnp.arange(seq_count * frames_dev, dtype=jnp.int32) < lengths[0]
    inputs = frames_in[0].astype(jnp.float32)
    normed, unit_one, inv_one = layer_norm(inputs, first_gain)
    normed_low = normed.astype(jnp.bfloat16)
    projected = jnp.dot(normed_low, qkv_weight, preferred_element_type=jnp.float32).astype(
        jnp.bfloat16
    )
    query_send = pack_queries(projected[:, :head_width], repeats, groups, channel)
    key_send = pack_keys(projected[:, head_width : 2 * head_width], repeats, groups, channel)
    value_send = pack_keys(projected[:, 2 * head_width :], repeats, groups, channel)
    got_queries, got_keys, got_values = (
        lax.all_to_all(query_send, "seq", split_axis=0, concat_axis=1, tiled=True),
        lax.all_to_all(key_send, "seq", split_axis=0, concat_axis=1, tiled=True),
        lax.all_to_all(value_send, "seq", split_axis=0, concat_axis=1, tiled=True),
    )
    query_rows = got_queries[0]
    key_rows = got_keys[0]
    value_rows = got_values[0]
    head_out = local_forward(query_rows, key_rows, value_rows, key_valid)
    returned = lax.all_to_all(head_out[None], "seq", split_axis=1, concat_axis=0, tiled=True)
    attended = unpack_rows(returned, repeats, groups)
    resid = inputs + contract_rows(attended, out_weight)
    normed_two, unit_two, inv_two = layer_norm(resid, second_gain)
    conv_in = (live_rows * normed_two).astype(jnp.bfloat16)
    padded = padded_2(conv_in, (("seq", 0),), half_taps)
    conv_sum = depthwise(padded, conv_kernel, frames_dev)
    sigmoid_c = jax.nn.sigmoid(conv_sum)
    layer_out = (live_rows * (resid + conv_sum * sigmoid_c)).astype(jnp.bfloat16)
    outer_grad = live_rows * layer_cotangent[0].astype(jnp.float32)
    conv_grads = (outer_grad * sigmoid_c * (1.0 + conv_sum * (1.0 - sigmoid_c))).astype(
        jnp.bfloat16
    )
    kernel_part = kernel_grad(padded, conv_grads, tap_count)
    grad_padded = padded_2(conv_grads, (("seq", 0),), half_taps)
    into_conv = depthwise(grad_padded, conv_kernel[::-1], frames_dev) * live_rows
    second_part = jnp.sum(into_conv * unit_two, axis=0)
    resid_grad = outer_grad + norm_backward(into_conv, unit_two, inv_two, second_gain)
    resid_low = resid_grad.astype(jnp.bfloat16)
    attended_grad = jnp.dot(resid_low, out_weight, preferred_element_type=jnp.float32).astype(
        jnp.bfloat16
    )
    sent_grads = lax.all_to_all(
        pack_queries(attended_grad, repeats, groups, channel),
        "seq",
        split_axis=0,
        concat_axis=1,
        tiled=True,
    )
    query_grads, key_sums, value_sums = local_backward(
        query_rows, key_rows, value_rows, key_valid, sent_grads[0]
    )
    query_back = lax.all_to_all(query_grads[None], "seq", split_axis=1, concat_axis=0, tiled=True)
    key_back, value_back = (
        lax.all_to_all(
            key_sums[None].astype(jnp.bfloat16), "seq", split_axis=1, concat_axis=0, tiled=True
        ).astype(jnp.float32),
        lax.all_to_all(
            value_sums[None].astype(jnp.bfloat16), "seq", split_axis=1, concat_axis=0, tiled=True
        ).astype(jnp.float32),
    )

    def fold_parts(stacked):
        shaped = stacked.reshape(groups, repeats, frames_dev, channel)
        summed = jnp.sum(shaped, axis=1).transpose(1, 0, 2)
        return summed.reshape(frames_dev, head_width).astype(jnp.bfloat16)

    query_grad_rows = unpack_rows(query_back, repeats, groups)
    key_grad_rows = fold_parts(key_back)
    value_grad_rows = fold_parts(value_back)
    qkv_grads = jnp.concatenate([query_grad_rows, key_grad_rows, value_grad_rows], axis=1)
    normed_grad = contract_rows(qkv_grads, qkv_weight)
    first_part = jnp.sum(normed_grad * unit_one, axis=0)
    input_grad = (resid_grad + norm_backward(normed_grad, unit_one, inv_one, first_gain)).astype(
        jnp.bfloat16
    )
    weight_grads = lax.psum_scatter(
        jnp.concatenate(
            [contract_cols(normed_low, qkv_grads), contract_cols(resid_low, attended)], axis=1
        ),
        ("dp", "seq"),
        scatter_dimension=0,
        tiled=True,
    )
    gain_sum, kernel_sum = lax.psum(
        (jnp.stack([first_part, second_part]), kernel_part), ("dp", "seq")
    )
    return (layer_out[None], input_grad[None], weight_grads, gain_sum, kernel_sum)


HALO = 32
BF16 = jnp.bfloat16
F32 = jnp.float32
VMEM_LIMIT = 56 * 2**20
CHUNK = 128
QUERY_BLOCK = 1024
TAP_ROWS = 16


def vmem(count):
    return [pl.BlockSpec(memory_space=pltpu.VMEM)] * count


def smem():
    return pl.BlockSpec(memory_space=pltpu.SMEM)


def cost(flops=1000, nbytes=1000):
    return pl.CostEstimate(flops=flops, bytes_accessed=nbytes, transcendentals=0)


def dot_nn(left, right):
    return lax.dot_general(left, right, (((1,), (0,)), ((), ())), preferred_element_type=F32)


def dot_nt(left, right):
    return lax.dot_general(left, right, (((1,), (1,)), ((), ())), preferred_element_type=F32)


def unit_norm(rows):
    centered = rows - jnp.mean(rows, axis=-1, keepdims=True)
    inv_std = lax.rsqrt(jnp.mean(centered * centered, axis=-1, keepdims=True) + epsilon)
    return centered * inv_std, inv_std


def project_kernel(x_ref, gain_ref, weight_ref, send_ref, normed_ref):
    @pl.when(pl.program_id(0) == 0)
    def _():
        unit, _ = unit_norm(x_ref[...].astype(F32))
        normed_ref[...] = (unit * gain_ref[...][None]).astype(BF16)

    product = dot_nn(normed_ref[...], weight_ref[...])
    send_ref[...] = product.T.astype(BF16).reshape(send_ref.shape)


def project(frames, gain, weight, peers):
    width, model = frames.shape
    columns = weight.shape[1]
    size = columns // (3 * peers)
    return pl.pallas_call(
        project_kernel,
        grid=(3,),
        out_shape=(
            jax.ShapeDtypeStruct((peers, 3 * size, width), BF16),
            jax.ShapeDtypeStruct((width, model), BF16),
        ),
        in_specs=[
            pl.BlockSpec((width, model), lambda i: (0, 0)),
            pl.BlockSpec((model,), lambda i: (0,)),
            pl.BlockSpec((model, peers * size), lambda i: (0, i)),
        ],
        out_specs=(
            pl.BlockSpec((peers, size, width), lambda i: (0, i, 0)),
            pl.BlockSpec((width, model), lambda i: (0, 0)),
        ),
        compiler_params=pltpu.CompilerParams(vmem_limit_bytes=VMEM_LIMIT),
        cost_estimate=cost(),
        name="project",
    )(frames, gain, weight)


def key_weights(scores, length, scale):
    live = lax.broadcasted_iota(jnp.int32, scores.shape, 0) < length
    return jnp.where(live, scores * scale, -jnp.inf)


def forward_kernel(len_ref, got_ref, qkv_ref, stats_ref, out_ref, att_ref, wide_ref):
    size = qkv_ref.shape[0] // 3
    frames = qkv_ref.shape[1]
    length = len_ref[0]
    scale = size**-0.5
    span = got_ref.shape[2]
    for peer in range(got_ref.shape[0]):
        qkv_ref[:, peer * span : (peer + 1) * span] = got_ref[peer]
    keys = qkv_ref[size : 2 * size, :].astype(F32).T.astype(BF16)
    values = qkv_ref[2 * size :, :]
    for start in range(0, frames, QUERY_BLOCK):
        cols = slice(start, start + QUERY_BLOCK)
        scores = key_weights(dot_nn(keys, qkv_ref[0:size, cols]), length, scale)
        top = jnp.max(scores, axis=0, keepdims=True)
        exps = jnp.exp(scores - top)
        inverse = 1.0 / jnp.sum(exps, axis=0, keepdims=True)
        attended = dot_nn(values, (exps * inverse).astype(BF16)).astype(BF16)
        att_ref[:, cols] = attended
        wide_ref[:, cols] = attended.astype(F32)
        stats_ref[0:1, cols] = top
        stats_ref[1:2, cols] = inverse
    peers, rows, width = out_ref.shape
    half = size // 2
    blank = jnp.zeros((size, HALO), F32)
    for peer in range(peers):
        first, last = peer * width, (peer + 1) * width
        out_ref[peer, 0:size, :] = att_ref[:, first:last]
        before = wide_ref[:, first - width : first][:, width - HALO :] if peer else blank
        after = wide_ref[:, last : last + width][:, :HALO] if peer < peers - 1 else blank
        edges = jnp.concatenate([before, after], axis=1)
        packed = jnp.concatenate([edges[:half], edges[half:]], axis=1)
        out_ref[peer, size:, :] = packed.astype(BF16)


def attention_forward(length, got):
    peers, triple, width = got.shape
    size = triple // 3
    frames = peers * width
    return pl.pallas_call(
        forward_kernel,
        out_shape=(
            jax.ShapeDtypeStruct((triple, frames), BF16),
            jax.ShapeDtypeStruct((8, frames), F32),
            jax.ShapeDtypeStruct((peers, size + size // 2, width), BF16),
            jax.ShapeDtypeStruct((size, frames), BF16),
        ),
        in_specs=[smem()] + vmem(1),
        out_specs=tuple(vmem(4)),
        scratch_shapes=[pltpu.VMEM((size, frames), F32)],
        compiler_params=pltpu.CompilerParams(vmem_limit_bytes=VMEM_LIMIT),
        cost_estimate=cost(),
        name="attention_forward",
    )(length, got)


def middle_kernel(
    groups,
    len_ref,
    att_ref,
    x_ref,
    before_ref,
    after_ref,
    cot_ref,
    weight_ref,
    gain_ref,
    taps_ref,
    layer_ref,
    resid_grad_ref,
    send_ref,
    att_out_ref,
    keep_ref,
    other_ref,
    resid_ref,
    unit_ref,
    conv_ref,
    grads_ref,
    into_ref,
    sum_ref,
    dot_ref,
    turned_ref,
    taps_out_ref,
):
    heads, packed_rows, width = att_ref.shape
    size = packed_rows * 2 // 3
    half = size // 2
    model = x_ref.shape[1]
    tap_count = taps_ref.shape[0]
    reach = (tap_count - 1) // 2
    near = HALO // 2
    main, edges = [], []
    for head in range(heads):
        main.append(att_ref[head, 0:size, :].astype(F32))
        packed = att_ref[head, size:, :].astype(F32)
        edges.append(packed[:, 0 : 2 * HALO])
        edges.append(packed[:, 2 * HALO :])
    att = jnp.concatenate(
        [jnp.concatenate(main, axis=0).T, jnp.concatenate(edges, axis=0).T], axis=0
    ).astype(BF16)
    product = dot_nt(att, weight_ref[...])
    resid_ref[0:HALO, :] = before_ref[0:HALO, :].astype(F32) + product[width : width + HALO]
    resid_ref[HALO : HALO + width, :] = x_ref[...].astype(F32) + product[:width]
    resid_ref[HALO + width :, :] = after_ref[0:HALO, :].astype(F32) + product[width + HALO :]
    unit, inv_std = unit_norm(resid_ref[...])
    unit_ref[...] = unit[HALO : HALO + width]
    rows = width + 2 * HALO
    place = lax.broadcasted_iota(jnp.int32, (rows, 1), 0) - HALO + lax.axis_index("seq") * width
    live = jnp.where((place >= 0) & (place < len_ref[0]), 1.0, 0.0).astype(F32)
    conv_ref[...] = (live * (unit * gain_ref[...][None])).astype(BF16).astype(F32)
    span = width + 2 * near
    live_span = live[near : near + span]
    live_main = live[HALO : HALO + width]
    sum_ref[...] = jnp.zeros_like(sum_ref)
    dot_ref[...] = jnp.zeros_like(dot_ref)

    taps_out_ref[...] = jnp.zeros_like(taps_out_ref)

    @pl.loop(0, model // CHUNK)
    def _(step):
        cols = pl.ds(pl.multiple_of(step * CHUNK, CHUNK), CHUNK)
        taps = taps_ref[:, cols]

        def put(tap, row):
            place = pl.ds(tap // heads * TAP_ROWS + step, 1)
            taps_out_ref[tap % heads, place, :] = row

        longest = tap_count // 8 * 8
        total = jnp.zeros((span, CHUNK), F32)
        for shift in range(8):
            part = conv_ref[pl.ds(HALO - near - reach + shift, span + longest), cols]
            for tap in range(shift, tap_count, 8):
                total = total + part[tap - shift : tap - shift + span] * taps[tap : tap + 1]
        gate = 1.0 / (1.0 + jnp.exp(-total))
        resid = resid_ref[pl.ds(HALO, width), cols]
        layer_ref[:, cols] = (
            live_main * (resid + total[near : near + width] * gate[near : near + width])
        ).astype(BF16)
        outer = live_span * jnp.concatenate(
            [before_ref[HALO:, cols], cot_ref[:, cols], after_ref[HALO:, cols]], axis=0
        ).astype(F32)
        grads = (outer * gate * (1.0 + total * (1.0 - gate))).astype(BF16).astype(F32)
        grads_ref[...] = grads
        inner = grads[near : near + width]
        for shift in range(8):
            part = conv_ref[pl.ds(HALO - reach + shift, width + longest), cols]
            for tap in range(shift, tap_count, 8):
                terms = part[tap - shift : tap - shift + width] * inner
                put(tap, jnp.sum(terms, axis=0, keepdims=True))
        into = jnp.zeros((width, CHUNK), F32)
        for shift in range(8):
            part = grads_ref[pl.ds(shift, width + longest), :]
            for offset in range(0, longest + 8, 8):
                tap = near + reach - shift - offset
                if tap < tap_count:
                    into = into + part[offset : offset + width] * taps[tap : tap + 1]
        into = into * live_main
        unit_part = unit_ref[:, cols]
        put(tap_count, jnp.sum(into * unit_part, axis=0, keepdims=True))
        scaled = into * gain_ref[cols][None]
        into_ref[:, cols] = scaled
        sum_ref[...] += scaled
        dot_ref[...] += scaled * unit_part

    mean = jnp.sum(sum_ref[...], axis=1, keepdims=True) / model
    mean_dot = jnp.sum(dot_ref[...], axis=1, keepdims=True) / model
    resid_grad = live_main * cot_ref[...].astype(F32) + inv_std[HALO : HALO + width] * (
        into_ref[...] - mean - unit_ref[...] * mean_dot
    )
    resid_grad_ref[...] = resid_grad
    send = dot_nn(resid_grad.astype(BF16), weight_ref[...]).T.astype(BF16)
    send_ref[:, 0:size, :] = send.reshape(heads, size, width)
    send_ref[:, size:, :] = taps_out_ref[...].astype(BF16)
    att_out_ref[...] = att[:width]
    chips = heads // 2
    share = model // (groups * heads)
    turned = resid_grad.T.astype(BF16)
    for group in range(groups):
        for chip in range(chips):
            for core in range(2):
                first = ((group * chips + chip) * 2 + core) * share
                place = (group * chips + chip) * share
                turned_ref[core, place : place + share, :] = turned[first : first + share]
    keep_ref[...] = turned_ref[(lax.axis_index("seq") % 2)]
    other_ref[...] = turned_ref[1 - (lax.axis_index("seq") % 2)]


def middle(groups, lengths, attended, frames, before, after, cotangent, out_weight, gain, taps):
    heads, packed_rows, width = attended.shape
    size = packed_rows * 2 // 3
    model = frames.shape[1]
    rows = width + 2 * HALO
    return pl.pallas_call(
        lambda *refs: middle_kernel(groups, *refs),
        out_shape=(
            jax.ShapeDtypeStruct((width, model), BF16),
            jax.ShapeDtypeStruct((width, model), F32),
            jax.ShapeDtypeStruct((heads, size + groups * TAP_ROWS, width), BF16),
            jax.ShapeDtypeStruct((width, heads * size), BF16),
            jax.ShapeDtypeStruct((model // 2, width), BF16),
            jax.ShapeDtypeStruct((model // 2, width), BF16),
        ),
        in_specs=[smem()] + vmem(8),
        out_specs=tuple(vmem(6)),
        scratch_shapes=[
            pltpu.VMEM((rows, model), F32),
            pltpu.VMEM((width, model), F32),
            pltpu.VMEM((rows, model), F32),
            pltpu.VMEM((width + HALO, CHUNK), F32),
            pltpu.VMEM((width, model), F32),
            pltpu.VMEM((width, CHUNK), F32),
            pltpu.VMEM((width, CHUNK), F32),
            pltpu.VMEM((2, model // 2, width), BF16),
            pltpu.VMEM((heads, groups * TAP_ROWS, width), F32),
        ],
        compiler_params=pltpu.CompilerParams(vmem_limit_bytes=VMEM_LIMIT),
        cost_estimate=cost(),
        name="middle",
    )(lengths, attended, frames, before, after, cotangent, out_weight, gain, taps)


def backward_kernel(len_ref, qkv_ref, stats_ref, grad_ref, send_ref, out_ref, *refs):
    tap_refs, total_ref = refs[:-1], refs[-1]
    size = qkv_ref.shape[0] // 3
    frames = qkv_ref.shape[1]
    peers, _, width = grad_ref.shape
    length = len_ref[0]
    total_ref[...] = jnp.sum(grad_ref[:, size:, :].astype(F32), axis=0)
    for place, tap_ref in enumerate(tap_refs):
        first = pl.multiple_of((lax.axis_index("dp") ^ place) * TAP_ROWS, TAP_ROWS)
        tap_ref[...] = total_ref[pl.ds(first, TAP_ROWS), :]
    scale = size**-0.5
    keys_turned = qkv_ref[size : 2 * size, :]
    keys = keys_turned.astype(F32).T.astype(BF16)
    values = qkv_ref[2 * size :, :].astype(F32).T.astype(BF16)
    grads = jnp.concatenate([grad_ref[peer, 0:size, :] for peer in range(peers)], axis=1)
    key_sum = jnp.zeros((size, frames), F32)
    value_sum = jnp.zeros((size, frames), F32)
    for start in range(0, frames, QUERY_BLOCK):
        cols = slice(start, start + QUERY_BLOCK)
        queries = qkv_ref[0:size, cols]
        block = grads[:, cols]
        scores = key_weights(dot_nn(keys, queries), length, scale)
        probs = jnp.exp(scores - stats_ref[0:1, cols]) * stats_ref[1:2, cols]
        prob_grads = dot_nn(values, block)
        delta = jnp.sum(probs * prob_grads, axis=0, keepdims=True)
        score_grads = (probs * (prob_grads - delta) * scale).astype(BF16)
        out_ref[0:size, cols] = dot_nn(keys_turned, score_grads).astype(BF16)
        key_sum = key_sum + dot_nt(queries, score_grads)
        value_sum = value_sum + dot_nt(block, probs.astype(BF16))
    out_ref[size : 2 * size, :] = key_sum.astype(BF16)
    out_ref[2 * size :, :] = value_sum.astype(BF16)
    for peer in range(peers):
        send_ref[peer] = out_ref[:, peer * width : (peer + 1) * width]


def attention_backward(lengths, qkv, stats, grads):
    peers, rows, width = grads.shape
    size = qkv.shape[0] // 3
    groups = (rows - size) // TAP_ROWS
    frames = peers * width
    return pl.pallas_call(
        backward_kernel,
        out_shape=(
            jax.ShapeDtypeStruct((peers, 3 * size, width), BF16),
            jax.ShapeDtypeStruct((3 * size, frames), BF16),
        )
        + (jax.ShapeDtypeStruct((TAP_ROWS, width), F32),) * groups,
        in_specs=[smem()] + vmem(3),
        out_specs=tuple(vmem(2 + groups)),
        scratch_shapes=[pltpu.VMEM((groups * TAP_ROWS, width), F32)],
        compiler_params=pltpu.CompilerParams(vmem_limit_bytes=VMEM_LIMIT),
        cost_estimate=cost(nbytes=22 * 10**6),
        name="attention_backward",
    )(lengths, qkv, stats, grads)


def chip_order(chip):
    far = chip // 2
    return (chip, chip ^ 1, 2 - far, 3 - 3 * far)


def qkv_kernel(left_ref, pair_ref, near_ref, far_ref, relayed_ref, *refs):
    out_refs, order_ref, blocks_ref = refs[:-2], refs[-2], refs[-1]
    blocks, double, half = near_ref.shape
    rows = left_ref.shape[0]
    width = double // 2
    for chip, origin in enumerate(chip_order((lax.axis_index("seq") // 2))):
        for place in range(2):
            frame = pl.multiple_of((origin * 2 + ((lax.axis_index("seq") % 2) ^ place)) * width, CHUNK)
            cols = slice((2 * chip + place) * width, (2 * chip + place + 1) * width)
            order_ref[:rows, cols] = left_ref[:, pl.ds(frame, width)]
            order_ref[rows:, cols] = pair_ref[:, pl.ds(frame, width)]
    span = 2 * CHUNK
    far = blocks * double
    for part in range(half // span):
        cols = slice(part * span, (part + 1) * span)
        product = dot_nn(order_ref[:, :far], near_ref[:, :, cols].reshape(far, span))
        rest = (far_ref[:, :, cols] + relayed_ref[:, :, cols]).reshape(far, span)
        product = product + dot_nn(order_ref[:, far:], rest)
        blocks_ref[cols, :] = product.T.astype(BF16)
    share = half // len(out_refs)
    for place, out_ref in enumerate(out_refs):
        first = pl.multiple_of((lax.axis_index("dp") ^ place) * share, 64)
        out_ref[...] = blocks_ref[pl.ds(first, share), :]


def qkv_parts(left, pair, near, far, relayed, groups):
    half = near.shape[2]
    rows, frames = left.shape
    return pl.pallas_call(
        qkv_kernel,
        out_shape=tuple(
            jax.ShapeDtypeStruct((half // groups, 2 * rows), BF16) for _ in range(groups)
        ),
        in_specs=vmem(5),
        out_specs=tuple(vmem(groups)),
        scratch_shapes=[
            pltpu.VMEM((2 * rows, frames), BF16),
            pltpu.VMEM((half, 2 * rows), BF16),
        ],
        compiler_params=pltpu.CompilerParams(vmem_limit_bytes=VMEM_LIMIT),
        cost_estimate=cost(),
        name="qkv_parts",
    )(left, pair, near, far, relayed)


def out_kernel(low_ref, att_ref, pair_low_ref, pair_att_ref, *out_refs):
    *out_refs, blocks_ref = out_refs
    product = dot_nn(low_ref[...], att_ref[...]) + dot_nn(pair_low_ref[...], pair_att_ref[...])
    blocks_ref[...] = product.astype(BF16).reshape(blocks_ref.shape)
    for place, out_ref in enumerate(out_refs):
        out_ref[...] = blocks_ref[lax.axis_index("dp") ^ place]


def out_parts(low, att, pair_low, pair_att, groups):
    rows = low.shape[0] // groups
    columns = att.shape[1]
    return pl.pallas_call(
        out_kernel,
        out_shape=tuple(jax.ShapeDtypeStruct((rows, columns), BF16) for _ in range(groups)),
        in_specs=vmem(4),
        out_specs=tuple(vmem(groups)),
        scratch_shapes=[pltpu.VMEM((groups, rows, columns), BF16)],
        compiler_params=pltpu.CompilerParams(vmem_limit_bytes=VMEM_LIMIT),
        cost_estimate=cost(),
        name="out_parts",
    )(low, att, pair_low, pair_att)


def summed(refs):
    total = refs[0][...].astype(F32)
    for ref in refs[1:]:
        total = total + ref[...].astype(F32)
    return total


def out_sum_kernel(*refs):
    refs[-1][...] = summed(refs[:-1]).astype(BF16)


def out_sums(parts):
    return pl.pallas_call(
        out_sum_kernel,
        out_shape=jax.ShapeDtypeStruct(parts[0].shape, BF16),
        in_specs=vmem(len(parts)),
        out_specs=vmem(1)[0],
        compiler_params=pltpu.CompilerParams(vmem_limit_bytes=VMEM_LIMIT),
        cost_estimate=cost(),
        name="out_sums",
    )(*parts)


def group_kernel(*refs):
    out_part_ref, out_ref = refs[-2], refs[-1]
    columns = out_part_ref.shape[1]
    chips, share, _ = out_ref.shape
    out_ref[:, :, :columns] = out_part_ref[...].reshape(chips, share, columns)
    out_ref[:, :, columns:] = summed(refs[:-2]).astype(BF16).reshape(chips, share, -1)


def group_sums(qkv_got, out_part, chips):
    rows = qkv_got[0].shape[0]
    columns = qkv_got[0].shape[1] + out_part.shape[1]
    return pl.pallas_call(
        group_kernel,
        out_shape=jax.ShapeDtypeStruct((chips, rows // chips, columns), BF16),
        in_specs=vmem(1 + len(qkv_got)),
        out_specs=vmem(1)[0],
        compiler_params=pltpu.CompilerParams(vmem_limit_bytes=VMEM_LIMIT),
        cost_estimate=cost(),
        name="group_sums",
    )(*qkv_got, out_part)


def input_kernel(grad_ref, weight_ref, x_ref, resid_grad_ref, gain_ref, *refs):
    out_ref, rows_ref, normed_ref = refs
    step = pl.program_id(0)
    heads, triple, width = grad_ref.shape
    size = triple // 3
    block = weight_ref.shape[0]

    @pl.when(step == 0)
    def _():
        turned = jnp.concatenate(
            [
                grad_ref[head, part * size : (part + 1) * size, :].astype(F32)
                for part in range(3)
                for head in range(heads)
            ],
            axis=0,
        )
        rows_ref[...] = turned.T.astype(BF16)

    cols = pl.ds(pl.multiple_of(step * block, block), block)
    normed_ref[:, cols] = dot_nt(rows_ref[...], weight_ref[...])

    @pl.when(step == pl.num_programs(0) - 1)
    def _():
        unit, inv_std = unit_norm(x_ref[...].astype(F32))
        scaled = normed_ref[...] * gain_ref[...][None]
        out_ref[...] = (
            resid_grad_ref[...]
            + inv_std
            * (
                scaled
                - jnp.mean(scaled, axis=-1, keepdims=True)
                - unit * jnp.mean(scaled * unit, axis=-1, keepdims=True)
            )
        ).astype(BF16)


def input_grads(grads, weight, frames, resid_grad, gain):
    heads, triple, width = grads.shape
    model, columns = weight.shape
    block = 4 * CHUNK
    return pl.pallas_call(
        input_kernel,
        grid=(model // block,),
        out_shape=jax.ShapeDtypeStruct((width, model), BF16),
        in_specs=[
            pl.BlockSpec((heads, triple, width), lambda i: (0, 0, 0)),
            pl.BlockSpec((block, columns), lambda i: (i, 0)),
            pl.BlockSpec((width, model), lambda i: (0, 0)),
            pl.BlockSpec((width, model), lambda i: (0, 0)),
            pl.BlockSpec((model,), lambda i: (0,)),
        ],
        out_specs=pl.BlockSpec((width, model), lambda i: (0, 0)),
        scratch_shapes=[pltpu.VMEM((width, columns), BF16), pltpu.VMEM((width, model), F32)],
        compiler_params=pltpu.CompilerParams(vmem_limit_bytes=VMEM_LIMIT),
        cost_estimate=cost(),
        name="input_grads",
    )(grads, weight, frames, resid_grad, gain)


def final_kernel(size, got_ref, weight_ref, gain_ref, *refs):
    tap_refs, (out_ref, row_ref) = refs[:-2], refs[-2:]
    model = row_ref.shape[2] - CHUNK
    chips = got_ref.shape[0]
    first = got_ref.shape[2] - 6 * size
    even = (lax.axis_index("seq") % 2) == 0
    rows = []
    for chip in range(chips):
        mine = got_ref[chip, :, first : first + 3 * size].astype(F32)
        pair = got_ref[chip, :, first + 3 * size :].astype(F32)
        rows += [jnp.where(even, mine, pair), jnp.where(even, pair, mine)]
    grads = jnp.concatenate(
        [row[:, part * size : (part + 1) * size] for part in range(3) for row in rows], axis=1
    )
    columns = grads.shape[1]
    out_ref[:, 0:columns] = grads
    total = got_ref[0, :, :first].astype(F32)
    for chip in range(1, chips):
        total = total + got_ref[chip, :, :first].astype(F32)
    out_ref[:, columns:] = total
    products = grads * weight_ref[...].astype(F32)
    gains = jnp.sum(products, axis=1, keepdims=True) / gain_ref[...]
    spare = jnp.zeros((CHUNK - gains.shape[0], 1), F32)
    turned = jnp.broadcast_to(jnp.concatenate([gains, spare], axis=0), (CHUNK, CHUNK)).T
    taps = summed(tap_refs)
    places = [taps[place : place + 1] for place in range(model // CHUNK)]
    row = jnp.concatenate(places + [turned[0:1]], axis=1)
    row_ref[...] = jnp.broadcast_to(row[None], row_ref.shape)


def final_sums(got, weight_rows, gain_rows, taps, model, everyone):
    rows, columns = weight_rows.shape
    size = columns // (6 * got.shape[0])
    width = columns + got.shape[2] - 6 * size
    return pl.pallas_call(
        lambda *refs: final_kernel(size, *refs),
        out_shape=(
            jax.ShapeDtypeStruct((rows, width), F32),
            jax.ShapeDtypeStruct((everyone, 1, model + CHUNK), F32),
        ),
        in_specs=vmem(3 + len(taps)),
        out_specs=tuple(vmem(2)),
        compiler_params=pltpu.CompilerParams(vmem_limit_bytes=VMEM_LIMIT),
        cost_estimate=cost(),
        name="final_sums",
    )(got, weight_rows, gain_rows, *taps)


def exchange(blocks, axes):
    return lax.all_to_all(blocks, axes, split_axis=0, concat_axis=0, tiled=True)


def swap(block, axis, bit):
    return lax.ppermute(block, axis, [(i, i ^ bit) for i in range(lax.axis_size(axis))])


def across(block):
    return lax.ppermute(block, "seq", [(2, 4), (3, 5), (4, 2), (5, 3)])


def outward(block):
    return lax.ppermute(block, "seq", [(2, 0), (3, 1), (4, 6), (5, 7)])


def group_swap(parts):
    return [parts[0]] + [swap(parts[bit], "dp", bit) for bit in range(1, len(parts))]


def head_shards(
    frames_in,
    lengths,
    first_gain,
    second_gain,
    qkv_weight,
    out_weight,
    conv_kernel,
    layer_cotangent,
):
    both = ("dp", "seq")
    peers = lax.axis_size("seq")
    everyone = peers * lax.axis_size("dp")
    width, model = frames_in.shape[1:]
    size = out_weight.shape[1] // HEADS
    mine = lax.axis_index("seq")
    number = lax.axis_index("dp") * peers + mine
    share = model // everyone
    frames, cotangent = frames_in[0], layer_cotangent[0]
    groups = lax.axis_size("dp")
    chips = peers // 2
    qkv_send, normed = project(frames, first_gain, qkv_weight, peers)
    qkv_got = exchange(qkv_send, "seq")
    near = HALO // 2
    tails = jnp.concatenate([frames[width - HALO :], cotangent[width - near :]], axis=0)
    fronts = jnp.concatenate([frames[:HALO], cotangent[:near]], axis=0)
    before = lax.ppermute(tails, "seq", [(i, i + 1) for i in range(peers - 1)])
    after = lax.ppermute(fronts, "seq", [(i + 1, i) for i in range(peers - 1)])
    halves = normed.reshape(width, -1, 2, share).transpose(2, 0, 1, 3).reshape(2, width, -1)
    keep = lax.dynamic_index_in_dim(halves, mine % 2, 0, keepdims=False)
    other = lax.dynamic_index_in_dim(halves, 1 - mine % 2, 0, keepdims=False)
    paired = jnp.concatenate([keep, swap(other, "seq", 1)], axis=0)
    normed_near = jnp.stack([paired, swap(paired, "seq", 2)])
    weight_rows = lax.dynamic_slice_in_dim(qkv_weight, number * share, share, axis=0)
    gain_rows = lax.dynamic_slice_in_dim(first_gain, number * share, share, axis=0)[:, None]
    qkv_got, before, after, weight_rows, gain_rows = lax.optimization_barrier(
        (qkv_got, before, after, weight_rows, gain_rows)
    )
    qkv, stats, att_send, att_head = attention_forward(lengths, qkv_got)
    attended = exchange(att_send, "seq")
    attended, normed_near = lax.optimization_barrier((attended, normed_near))
    normed_far = across(normed_near)
    layer_out, resid_grad, grad_send, att_rows, low_keep, low_other = middle(
        groups, lengths, attended, frames, before, after, cotangent, out_weight, second_gain, conv_kernel
    )
    grad_send, normed_far = lax.optimization_barrier((grad_send, normed_far))
    grads = exchange(grad_send, "seq")
    blocks = out_parts( low_keep, att_rows, swap(low_other, "seq", 1), swap(att_rows, "seq", 1), groups
    )
    grads, blocks = lax.optimization_barrier((grads, blocks))
    normed_out = outward(normed_far)
    out_got = group_swap(blocks)
    back_send, back_head, *taps = attention_backward(lengths, qkv, stats, grads)
    pair_head = swap(back_head, "seq", 1)
    back_send, back_head, normed_out, out_got = lax.optimization_barrier(
        (back_send, back_head, normed_out, out_got)
    )
    back = exchange(back_send, "seq")
    qkv_got = group_swap(
        qkv_parts(back_head, pair_head, normed_near, normed_far, normed_out, groups)
    )
    out_part = out_sums(out_got)
    back, qkv_got, out_part = lax.optimization_barrier((back, qkv_got, out_part))
    taps_got = group_swap(taps)
    sums = group_sums(qkv_got, out_part, chips)
    cores = [list(range(core, peers, 2)) for core in range(2)]
    got = lax.all_to_all(
        sums, "seq", split_axis=0, concat_axis=0, tiled=True, axis_index_groups=cores
    )
    input_grad = input_grads(back, qkv_weight, frames, resid_grad, first_gain)
    got, input_grad = lax.optimization_barrier((got, input_grad))
    weight_grads, row = final_sums(got, weight_rows, gain_rows, taps_got, model, everyone)
    rows = exchange(row, both)[:, 0]
    tap_count = conv_kernel.shape[0]
    conv_grad = rows[:tap_count, :model]
    gain_grads = jnp.stack([rows[:, model : model + share].reshape(-1), rows[tap_count, :model]])
    return (layer_out[None], input_grad[None], weight_grads, gain_grads, conv_grad)


def solution(mesh):
    in_specs = (P("dp", "seq", None), P("dp"), P(), P(), P(), P(), P(), P("dp", "seq", None))
    out_specs = (P("dp", "seq", None), P("dp", "seq", None), P(("dp", "seq"), None), P(), P())
    seq_count = mesh.shape["seq"]
    device_count = seq_count * mesh.shape["dp"]

    def program(*args):
        frames_dev = args[0].shape[1] // seq_count
        fits = seq_count == HEADS and frames_dev == 128 and device_count == args[6].shape[0] + 1 == 32
        plan = head_shards if fits else general_shards
        return jax.shard_map(
            plan, mesh=mesh, in_specs=in_specs, out_specs=out_specs, check_vma=False
        )(*args)

    return program
```
